128 devices in a mesh: obj: 16 (over x, z), tok: 8 (over y, core).
Axes of the slice: x: 4, y: 4, z: 4, core: 2. Of those that a mesh axis runs over, the one named last changes fastest.
Arguments:
- tokens: bfloat16 [16, 1024, 512], P('obj', 'tok'), may hold values from -6 to 6, as said below
- camera: bfloat16 [16, 1024], P('obj'), may hold values from -6 to 6, as said below
- image: bfloat16 [16, 1040, 384], P('obj', 'tok'), may hold values from -6 to 6, as said below
- image_mask: int32 [16, 1040], P('obj'), may hold values from 0 to 1, as said below
- point_rows: int32 [16, 8192], P('obj', 'tok'), may hold values from 0 to 1023
- point_count: int32 [16, 8], P('obj', 'tok'), may hold values from 64 to 1024, as said below
- point_grads: bfloat16 [16, 8192, 512], P('obj', 'tok'), may hold values from -6 to 6
- mod_weight: bfloat16 [1024, 3072], replicated, as said below
- norm_gains: bfloat16 [3, 512], replicated, may hold values from 0.5 to 1.5
- wq_cross: bfloat16 [512, 512], replicated, as said below
- wkv_cross: bfloat16 [384, 1024], replicated, as said below
- wo_cross: bfloat16 [512, 512], replicated, may hold values from -6 to 6
- wqkv_self: bfloat16 [512, 1536], replicated, as said below
- wo_self: bfloat16 [512, 512], replicated, may hold values from -4 to 4
- w_in: bfloat16 [512, 2048], replicated, may hold values from -0.25 to 0.25
- w_out: bfloat16 [2048, 512], replicated, may hold values from -0.125 to 0.125
Outputs:
- layer_out: bfloat16 [16, 1024, 512], P('obj', 'tok')
- grad_tokens: float32 [16, 1024, 512], P('obj', 'tok')
- grad_image: float32 [16, 1040, 384], P('obj', 'tok')
- grad_mod_weight: float32 [1024, 3072], replicated
- grad_norm_gains: float32 [3, 512], replicated
- grad_wq_cross: float32 [512, 512], replicated
- grad_wkv_cross: float32 [384, 1024], replicated
- grad_wo_cross: float32 [512, 512], replicated
- grad_wqkv_self: float32 [512, 1536], replicated
- grad_wo_self: float32 [512, 512], replicated
- grad_w_in: float32 [512, 2048], replicated
- grad_w_out: float32 [2048, 512], replicated
The draws below stay inside these ranges and needn't reach their ends.
Inputs may be any that keep to these rules, and one draw needn't show every extreme that they name: The live ray points of a device are its first point_count slots; in every draw some device has all 1024 slots live. `image_mask`: image token 0 of every object is a key. `tokens`: independent entries of mean 0 and deviation 1. `camera`: independent entries of mean 0 and deviation 1. `image`: independent entries of mean 0 and deviation 1. `mod_weight`: independent entries of mean 0 and deviation 1024 ** -0.5, within four deviations. `wq_cross`: independent entries of mean 0 and deviation 512 ** -0.5, within four deviations. `wkv_cross`: independent entries of mean 0 and deviation 384 ** -0.5, within four deviations. `wqkv_self`: independent entries of mean 0 and deviation 512 ** -0.5, within four deviations.
All inputs are finite; a program needn't handle non-finite values.
Results may differ from the reference program's by a relative error of at most 0.028.
Values may be sent and summed in bfloat16 or wider, within the bound.
No kernel may reach another device: no remote copies, remote signals or barrier semaphores. Data moves between devices by JAX's collectives and lax.ppermute only.
A program may use at most 192 MiB of HBM per device.

```python
import math
import jax
import jax.numpy as jnp
from jax import lax

D = 512
HEADS = 8
HDIM = 64
FF = 2048
CIMG = 384
CAM = 1024
IMG = 1040
ROWS_DEV = 128
PTS_DEV = 1024
OBJECTS = 16
GROUPS = 8
ROWS = 1024
N_TOK = 8


def clipped_normal(key, shape, deviation, limit):
    values = jax.random.truncated_normal(key, -limit, limit, shape, jnp.float32)
    return (values * deviation).astype(jnp.bfloat16)


def draw_tokens(key, part):
    key = jax.random.fold_in(key, 31)
    return clipped_normal(key, (OBJECTS, ROWS, D), 1.0, 6.0)


def draw_camera(key, part):
    key = jax.random.fold_in(key, 37)
    return clipped_normal(key, (OBJECTS, CAM), 1.0, 6.0)


def draw_image(key, part):
    key = jax.random.fold_in(key, 41)
    return clipped_normal(key, (OBJECTS, IMG, CIMG), 1.0, 6.0)


def draw_mod_weight(key, part):
    key = jax.random.fold_in(key, 43)
    return clipped_normal(key, (CAM, 6 * D), CAM ** (-0.5), 4.0)


def draw_wq_cross(key, part):
    key = jax.random.fold_in(key, 47)
    return clipped_normal(key, (D, D), D ** (-0.5), 4.0)


def draw_wkv_cross(key, part):
    key = jax.random.fold_in(key, 53)
    return clipped_normal(key, (CIMG, 2 * D), CIMG ** (-0.5), 4.0)


def draw_wqkv_self(key, part):
    key = jax.random.fold_in(key, 59)
    return clipped_normal(key, (D, 3 * D), D ** (-0.5), 4.0)


def draw_point_count(key, part):
    key = jax.random.fold_in(key, 11)
    first_key, second_key, third_key = jax.random.split(key, 3)
    power = jax.random.randint(first_key, (OBJECTS, GROUPS), 0, 4)
    base_count = jnp.right_shift(jnp.int32(PTS_DEV), power.astype(jnp.int32))
    noise = jax.random.randint(second_key, (OBJECTS, GROUPS), 0, 1 << 20) % (base_count // 2 + 1)
    counts = (base_count - noise).astype(jnp.int32).reshape(-1)
    place = jax.random.randint(third_key, (), 0, OBJECTS * GROUPS)
    counts = counts.at[place].set(PTS_DEV)
    return counts.reshape(OBJECTS, GROUPS).astype(jnp.int32)


def draw_image_mask(key, part):
    key = jax.random.fold_in(key, 23)
    picks = jax.random.randint(key, (OBJECTS, IMG), 0, 8)
    keeps = (picks != 0).astype(jnp.int32)
    return keeps.at[:, 0].set(1)


def set_ends(values, key, smallest, top_value):
    index_at = [jax.random.randint(jax.random.fold_in(key, axis), (), 0, length) for axis, length in enumerate(values.shape)]
    main_axis = values.shape.index(max(values.shape))
    next_to = index_at[:main_axis] + [(index_at[main_axis] + 1) % values.shape[main_axis]] + index_at[main_axis + 1:]
    return values.at[tuple(index_at)].set(smallest).at[tuple(next_to)].set(top_value)


def steps_of(own_key, extent, cuts, smallest, high):
    def one(dim, parts):
        heights = jax.random.uniform(jax.random.fold_in(jax.random.fold_in(own_key, 6), dim), (parts,), jnp.float32, smallest / len(cuts), high / len(cuts))
        return jnp.repeat(jnp.exp(heights), extent[dim] // parts).reshape((-1,) + (1,) * (len(extent) - dim - 1))

    loudness = one(*cuts[0])
    for cut in cuts[1:]:
        loudness = loudness * one(*cut)
    return loudness


def centred(stream_key, shape, width, most, cuts=(), held_as=jnp.bfloat16):
    factor_of = steps_of(stream_key, shape, cuts, -0.22, 0.18) if cuts else 1.0
    values = jax.random.normal(stream_key, shape, jnp.float32) * width * factor_of
    return jnp.minimum(jnp.maximum(values, -most), most).astype(held_as)


def setup_inputs(seed: int = 0) -> dict:
    arg_keys = jax.random.split(jax.random.key(seed), 17)
    return {
        "tokens": draw_tokens(jax.random.fold_in(arg_keys[16], 71), 0),
        "camera": draw_camera(jax.random.fold_in(arg_keys[16], 71), 0),
        "image": draw_image(jax.random.fold_in(arg_keys[16], 71), 0),
        "image_mask": draw_image_mask(jax.random.fold_in(arg_keys[16], 71), 0),
        "point_rows": set_ends(jax.random.randint(arg_keys[4], (OBJECTS, GROUPS * PTS_DEV), 0, ROWS_DEV * N_TOK), jax.random.fold_in(arg_keys[4], 1), 0, (ROWS_DEV * N_TOK) - 1).astype(jnp.int32),
        "point_count": draw_point_count(jax.random.fold_in(arg_keys[16], 71), 0),
        "point_grads": centred(arg_keys[6], (OBJECTS, GROUPS * PTS_DEV, D), 1.0, 6.0, ((0, 16), (1, 8))),
        "mod_weight": draw_mod_weight(jax.random.fold_in(arg_keys[16], 71), 0),
        "norm_gains": jnp.clip(1.0 + 0.1 * jax.random.normal(arg_keys[8], (3, D), jnp.float32), 0.5, 1.5).astype(jnp.bfloat16),
        "wq_cross": draw_wq_cross(jax.random.fold_in(arg_keys[16], 71), 0),
        "wkv_cross": draw_wkv_cross(jax.random.fold_in(arg_keys[16], 71), 0),
        "wo_cross": centred(arg_keys[11], (D, D), (max(1, 4 * D // IMG)) ** -0.5, 6.0),
        "wqkv_self": draw_wqkv_self(jax.random.fold_in(arg_keys[16], 71), 0),
        "wo_self": centred(arg_keys[13], (D, D), (max(1, 4 * D // (ROWS_DEV * N_TOK))) ** -0.5, 4.0),
        "w_in": centred(arg_keys[14], (D, FF), D ** -0.5, 0.25),
        "w_out": centred(arg_keys[15], (FF, D), FF ** -0.5, 0.125),
    }


@jax.custom_vjp
def low(v):
    return lax.optimization_barrier(v.astype(jnp.bfloat16)).astype(jnp.float32)

@jax.custom_vjp
def low_back(v):
    return v

def low_keep(v):
    return (low(v), None)

def low_pass(kept, grad):
    return (grad,)

def back_keep(v):
    return (v, None)

def back_low(kept, grad):
    return (low(grad),)
low.defvjp(low_keep, low_pass)
low_back.defvjp(back_keep, back_low)

def matmul(left, right):
    return jnp.dot(left, right, precision=lax.Precision.HIGHEST)

def modnorm(values, gain_row, shift_row, scale_row):
    center = values - lax.optimization_barrier(jnp.mean(values, axis=-1, keepdims=True))
    spread = lax.optimization_barrier(jnp.mean(center * center, axis=-1, keepdims=True))
    return center * lax.rsqrt(spread + 1e-05) * gain_row * (1.0 + scale_row) + shift_row

def attend(queries, key_rows, value_rows, key_keep):
    query_total = queries.shape[0]
    block_rows = min(512, query_total)
    factor = 1.0 / math.sqrt(HDIM)
    key_heads = key_rows.reshape(-1, HEADS, HDIM)
    value_heads = value_rows.reshape(-1, HEADS, HDIM)

    def one_block(query_block):
        scores = jnp.einsum('qhd,khd->hqk', query_block, key_heads, precision=lax.Precision.HIGHEST) * factor
        scores = low_back(scores)
        scores = jnp.where(key_keep[None, None, :], scores, -1e+30)
        soft_weights = low(jax.nn.softmax(scores, axis=-1))
        return jnp.einsum('hqk,khd->qhd', soft_weights, value_heads, precision=lax.Precision.HIGHEST)
    blocks = queries.reshape(query_total // block_rows, block_rows, HEADS, HDIM)
    attended = lax.map(jax.checkpoint(one_block), blocks)
    return attended.reshape(query_total, HEADS * HDIM)

def object_layer(weight_set, tok_rows, img_rows, cam_row, key_keep):
    mod_weight, norm_gains, wq_cross, wkv_cross, wo_cross, wqkv_self, wo_self, w_in, w_out = weight_set
    cam_act = low(jax.nn.silu(cam_row))
    modulation = matmul(cam_act[None, :], mod_weight).reshape(6, D)
    normed = low(modnorm(tok_rows, norm_gains[0], modulation[0], modulation[1]))
    query_one = low_back(low(matmul(normed, wq_cross)))
    cross_kv = low_back(low(matmul(img_rows, wkv_cross)))
    attended = low_back(low(attend(query_one, cross_kv[:, :D], cross_kv[:, D:], key_keep)))
    after_cross = tok_rows + low_back(matmul(attended, wo_cross))
    normed = low(modnorm(after_cross, norm_gains[1], modulation[2], modulation[3]))
    packed = low_back(low(matmul(normed, wqkv_self)))
    all_keys = jnp.ones((packed.shape[0],), dtype=jnp.bool_)
    attended = low_back(low(attend(packed[:, :D], packed[:, D:2 * D], packed[:, 2 * D:], all_keys)))
    after_self = after_cross + low_back(matmul(attended, wo_self))
    normed = low(modnorm(after_self, norm_gains[2], modulation[4], modulation[5]))
    inner_act = low_back(matmul(normed, w_in))
    hidden = low(jax.nn.gelu(inner_act))
    return after_self + low_back(matmul(hidden, w_out))

def reference(tokens, camera, image, image_mask, point_rows, point_count, point_grads, mod_weight, norm_gains, wq_cross, wkv_cross, wo_cross, wqkv_self, wo_self, w_in, w_out):
    weight_set = tuple((item.astype(jnp.float32) for item in (mod_weight, norm_gains, wq_cross, wkv_cross, wo_cross, wqkv_self, wo_self, w_in, w_out)))
    slot_index = jnp.arange(GROUPS * PTS_DEV, dtype=jnp.int32)

    def per_object(totals, pieces):
        tok_obj, cam_obj, img_obj, mask_obj, rows_obj, count_obj, grads_obj = pieces
        key_keep = mask_obj > 0
        cam_float = cam_obj.astype(jnp.float32)

        def forward(weights_in, tok_in, img_in):
            return object_layer(weights_in, tok_in, img_in, cam_float, key_keep)
        result, pullback = jax.vjp(forward, weight_set, tok_obj.astype(jnp.float32), img_obj.astype(jnp.float32))
        live_slots = (slot_index % PTS_DEV < jnp.repeat(count_obj, PTS_DEV)).astype(jnp.float32)

        def read_points(field):
            return field[rows_obj]
        _, read_back = jax.vjp(read_points, result)
        cotangent, = read_back(grads_obj.astype(jnp.float32) * live_slots[:, None])
        weight_grads, tok_grad, img_grad = pullback(cotangent)
        totals = jax.tree.map(jnp.add, totals, weight_grads)
        return (totals, (result.astype(jnp.bfloat16), tok_grad, img_grad))
    zero_grads = jax.tree.map(jnp.zeros_like, weight_set)
    totals, (output, tok_grads, img_grads) = lax.scan(per_object, zero_grads, (tokens, camera, image, image_mask, point_rows, point_count, point_grads))
    return (output, tok_grads, img_grads, totals[0], totals[1], totals[2], totals[3], totals[4], totals[5], totals[6], totals[7], totals[8])
```

```python
import functools

import jax
import jax.numpy as jnp
from jax import lax
from jax.experimental import pallas as pl
from jax.experimental.pallas import tpu as pltpu
from jax.sharding import Mesh
from jax.sharding import PartitionSpec as P

BF = jnp.bfloat16
F32 = jnp.float32
D = 512
ROWS = 128
IMG_ROWS = 130
IMG_PAD = 144
IMG_KEYS = 8 * IMG_PAD
KEYS = 8 * ROWS
SCALE = 0.125
CORE_SWAP = [(0, 1), (1, 0)]
VMEM = pl.BlockSpec(memory_space=pltpu.VMEM)
SMEM = pl.BlockSpec(memory_space=pltpu.SMEM)


def nn(left, right):
    return jnp.dot(left, right, preferred_element_type=F32)


def nt(left, right):
    return lax.dot_general(left, right, (((1,), (1,)), ((), ())), preferred_element_type=F32)


def tn(left, right):
    return lax.dot_general(left, right, (((0,), (0,)), ((), ())), preferred_element_type=F32)


def kernel_call(body, outs, scratch, flops, moved, limit, *args, smem=0):
    in_specs = [SMEM] * smem + [VMEM] * (len(args) - smem)
    return pl.pallas_call(
        body,
        out_shape=[jax.ShapeDtypeStruct(shape, dtype) for shape, dtype in outs],
        in_specs=in_specs,
        out_specs=[VMEM] * len(outs),
        scratch_shapes=[pltpu.VMEM(shape, dtype) for shape, dtype in scratch],
        compiler_params=pltpu.CompilerParams(vmem_limit_bytes=limit << 20),
        cost_estimate=pl.CostEstimate(flops=flops, bytes_accessed=moved, transcendentals=0),
    )(*args)


def norm_parts(values, gain, scale):
    center = values - jnp.mean(values, axis=-1, keepdims=True)
    rstd = lax.rsqrt(jnp.mean(center * center, axis=-1, keepdims=True) + 1e-05)
    return center * rstd, rstd, gain * (1.0 + scale)


def norm_back(grad, xhat, rstd, slope):
    scaled = grad * slope
    return rstd * (
        scaled
        - jnp.mean(scaled, axis=-1, keepdims=True)
        - xhat * jnp.mean(scaled * xhat, axis=-1, keepdims=True)
    )


def norm_sums(grad, xhat, gain, scale):
    total = jnp.sum(grad * xhat, axis=0, keepdims=True)
    return total * (1.0 + scale), jnp.sum(grad, axis=0, keepdims=True), total * gain


def spread_columns(block):
    head = lax.broadcasted_iota(jnp.int32, block.shape, 0) >> 6
    return jnp.concatenate([jnp.where(head == j, block, 0.0) for j in range(4)], axis=1)


def spread_rows(block):
    head = lax.broadcasted_iota(jnp.int32, block.shape, 1) >> 6
    return jnp.concatenate([jnp.where(head == j, block, 0.0) for j in range(4)], axis=0)


def gather_heads(wide):
    return jnp.concatenate(
        [wide[64 * j : 64 * j + 64, 128 * j : 128 * j + 128] for j in range(4)], axis=0
    )


def fold8(values, reduce):
    rows, width = values.shape
    return reduce(values.reshape(rows // 8, 8, width), axis=0)


def attend(q_t, keys_ref, values_t_ref, probs_ref, score_ref, bias_ref):
    key_total = keys_ref.shape[0]
    chunks = [(start, min(256, key_total - start)) for start in range(0, key_total, 256)]
    parts = []
    for quad in range(2):
        lanes = slice(256 * quad, 256 * quad + 256)
        spread = spread_columns(q_t[lanes, :]).astype(BF)
        top = None
        for start, size in chunks:
            scores = nn(keys_ref[start : start + size, lanes], spread)
            if bias_ref is not None:
                scores = scores + bias_ref[start : start + size, :]
            score_ref[start : start + size, :] = scores
            here = fold8(scores, jnp.max)
            top = here if top is None else jnp.maximum(top, here)
        top = jnp.max(top, axis=0, keepdims=True)
        total = None
        for start, size in chunks:
            weights = jnp.exp(score_ref[start : start + size, :] - top)
            score_ref[start : start + size, :] = weights
            here = fold8(weights, jnp.sum)
            total = here if total is None else total + here
        inverse = 1.0 / jnp.sum(total, axis=0, keepdims=True)
        for start, size in chunks:
            probs_ref[quad, start : start + size, :] = (
                score_ref[start : start + size, :] * inverse
            ).astype(BF)
        parts.append(gather_heads(nn(values_t_ref[lanes, :], probs_ref[quad])))
    return jnp.concatenate(parts, axis=0)


def attend_back(q_s, grad, grad_t, out_t, keys_t_ref, values_ref, probs_ref, slopes_ref, gk_ref, gv_ref):
    key_total = values_ref.shape[0]
    chunks = [(start, min(256, key_total - start)) for start in range(0, key_total, 256)]
    inner = grad_t * out_t
    parts = []
    for quad in range(2):
        lanes = slice(256 * quad, 256 * quad + 256)
        spread = spread_columns(grad_t[lanes, :]).astype(BF)
        delta = jnp.concatenate(
            [
                jnp.sum(inner[256 * quad + 64 * j : 256 * quad + 64 * j + 64, :], axis=0, keepdims=True)
                for j in range(4)
            ],
            axis=1,
        )
        grad_rows = spread_rows(grad[:, lanes]).astype(BF)
        query_rows = spread_rows(q_s[:, lanes]).astype(BF)
        for start, size in chunks:
            span = slice(start, start + size)
            grad_probs = nn(values_ref[span, lanes], spread)
            probs = probs_ref[quad, span, :]
            slopes = (probs.astype(F32) * (grad_probs - delta)).astype(BF)
            slopes_ref[span, :] = slopes
            gv_ref[span, lanes] = nn(probs, grad_rows).astype(BF)
            gk_ref[span, lanes] = nn(slopes, query_rows).astype(BF)
        parts.append(gather_heads(nn(keys_t_ref[lanes, :], slopes_ref[...])))
    return jnp.concatenate(parts, axis=0).T * SCALE


def points_kernel(owner_ref, count_ref, rows_ref, grads_ref, camera_ref, modw_ref, keep_ref, send_ref, mod_ref, act_ref):
    row_ids = rows_ref[...]
    slot = lax.broadcasted_iota(jnp.int32, row_ids.shape, 1)
    row_ids = jnp.where(slot < count_ref[0], row_ids, -1)
    for block in range(8):
        target = lax.broadcasted_iota(jnp.int32, (ROWS, row_ids.shape[1]), 0) + owner_ref[block] * ROWS
        onehot = jnp.where(target == row_ids, 1.0, 0.0).astype(BF)
        part = nn(onehot, grads_ref[...]).astype(BF)
        out = keep_ref if block < 4 else send_ref
        out[ROWS * (block % 4) : ROWS * (block % 4) + ROWS, :] = part
    camera = camera_ref[...].astype(F32)
    act = (camera / (1.0 + jnp.exp(-camera))).astype(BF)
    act_ref[...] = act
    modulation = nn(jnp.broadcast_to(act, (16, act.shape[1])), modw_ref[...])
    for row in range(6):
        mod_ref[row : row + 1, :] = modulation[0:1, D * row : D * row + D]
    mod_ref[6:8, :] = jnp.zeros((2, D), F32)


def cross_kernel(
    tokens_ref, mod_ref, gains_ref, wq_ref, wkv_ref, wo_ref, bias_ref,
    i0, i1, i2, i3, i4, i5, i6, i7,
    after_ref, normed_ref, attended_ref, query_ref, probs_ref, values_ref, keys_t_ref, image_ref,
    keys_ref, values_t_ref, score_ref,
):
    for j, block in enumerate((i0, i1, i2, i3, i4, i5, i6, i7)):
        base = IMG_PAD * j
        image_ref[base + 128 : base + IMG_PAD, :] = jnp.zeros((16, image_ref.shape[1]), BF)
        image_ref[base : base + IMG_ROWS, :] = block[...]
    mod = mod_ref[...]
    gains = gains_ref[...].astype(F32)
    tokens = tokens_ref[...].astype(F32)
    xhat, _, slope = norm_parts(tokens, gains[0:1], mod[1:2])
    normed = (xhat * slope + mod[0:1]).astype(BF)
    query = nn(normed, wq_ref[...]).astype(BF)
    query_ref[...] = query
    wk, wv = wkv_ref[:, :D], wkv_ref[:, D:]
    keys_ref[...] = nn(image_ref[...], wk).astype(BF)
    values_t_ref[...] = nt(wv.T, image_ref[...]).astype(BF)
    values_ref[...] = nn(image_ref[...], wv).astype(BF)
    keys_t_ref[...] = nt(wk.T, image_ref[...]).astype(BF)
    q_t = query.astype(F32).T * SCALE
    out_t = attend(q_t, keys_ref, values_t_ref, probs_ref, score_ref, bias_ref)
    attended = out_t.T.astype(BF)
    attended_ref[...] = attended
    after = tokens + nn(attended, wo_ref[...])
    after_ref[...] = after
    xhat, _, slope = norm_parts(after, gains[1:2], mod[3:4])
    normed_ref[...] = (xhat * slope + mod[2:3]).astype(BF)


def gelu_parts(value):
    c = 0.7978845608028654
    square = value * value
    bent = jnp.tanh(c * value * (1.0 + 0.044715 * square))
    half = 0.5 * (1.0 + bent)
    slope = half + 0.5 * value * (1.0 - bent * bent) * (c * (1.0 + 3.0 * 0.044715 * square))
    return value * half, slope


def middle_kernel(
    core_ref, after_ref, mod_ref, gains_ref, wqkv_ref, wo_ref, w_in_ref, w_out_ref,
    n0, n1, n2, n3, n4, n5, n6, n7, c0, c1, c2, c3,
    out_ref, query_ref, probs_ref, values_ref, keys_t_ref, all_ref, attended_ref, grad_ref, branch_ref, sums_ref,
    keep_ref, send_ref,
    keys_ref, values_t_ref, score_ref, hidden_ref, normed_ref,
):
    core = core_ref[0]
    for j, block in enumerate((n0, n1, n2, n3, n4, n5, n6, n7)):
        all_ref[ROWS * j : ROWS * j + ROWS, :] = block[...]
    mod = mod_ref[...]
    gains = gains_ref[...].astype(F32)
    query = nn(n0[...], wqkv_ref[:, :D]).astype(BF)
    query_ref[...] = query
    wk, wv = wqkv_ref[:, D : 2 * D], wqkv_ref[:, 2 * D :]
    keys_ref[...] = nn(all_ref[...], wk).astype(BF)
    values_t_ref[...] = nt(wv.T, all_ref[...]).astype(BF)
    values_ref[...] = nn(all_ref[...], wv).astype(BF)
    keys_t_ref[...] = nt(wk.T, all_ref[...]).astype(BF)
    q_t = query.astype(F32).T * SCALE
    out_t = attend(q_t, keys_ref, values_t_ref, probs_ref, score_ref, None)
    attended = out_t.T.astype(BF)
    attended_ref[...] = attended
    after = after_ref[...] + nn(attended, wo_ref[...])
    xhat, rstd, slope = norm_parts(after, gains[2:3], mod[5:6])
    normed = (xhat * slope + mod[4:5]).astype(BF)
    normed_ref[...] = normed
    inner = nn(normed, w_in_ref[...])
    value, bend = gelu_parts(inner)
    hidden_ref[...] = value.astype(BF)
    result = after + nn(hidden_ref[...], w_out_ref[...])
    out_ref[...] = result.astype(BF)
    cot = c0[...].astype(F32) + c1[...].astype(F32) + c2[...].astype(F32) + c3[...].astype(F32)
    branch = cot.astype(BF)
    grad_inner = (nt(branch, w_out_ref[...]) * bend).astype(BF)
    for ref, half in ((keep_ref, core), (send_ref, 1 - core)):
        wide = pl.ds(pl.multiple_of(half * 1024, 1024), 1024)
        narrow = pl.ds(pl.multiple_of(half * 256, 256), 256)
        ref[:1024, :] = tn(hidden_ref[:, wide], branch).astype(BF)
        part = tn(normed_ref[:, narrow], grad_inner).astype(BF)
        for j in range(4):
            ref[1024 + 256 * j : 1280 + 256 * j, :] = part[:, D * j : D * j + D]
    grad = nt(grad_inner, w_in_ref[...])
    sums_ref[...] = jnp.zeros(sums_ref.shape, F32)
    for row, line in enumerate(norm_sums(grad, xhat, gains[2:3], mod[5:6])):
        sums_ref[row : row + 1, :] = line
    grad_after = cot + norm_back(grad, xhat, rstd, slope)
    grad_ref[...] = grad_after
    branch_ref[...] = grad_after.astype(BF)


def self_back_kernel(
    core_ref, branch_ref, wo_ref, wqkv_ref, query_ref, attended_ref, probs_ref, values_ref, keys_t_ref, all_ref,
    keep_ref, send_ref, wkeep_ref, wsend_ref,
    slopes_ref, gk_ref, gv_ref,
):
    core = core_ref[0]
    branch = branch_ref[...]
    grad = nt(branch, wo_ref[...]).astype(BF).astype(F32)
    grad_t = nt(wo_ref[...], branch).astype(BF).astype(F32)
    out_t = attended_ref[...].astype(F32).T
    query = query_ref[...].astype(F32) * SCALE
    gq = attend_back(
        query, grad, grad_t, out_t, keys_t_ref, values_ref, probs_ref, slopes_ref, gk_ref, gv_ref
    ).astype(BF)
    wq, wk, wv = wqkv_ref[:, :D], wqkv_ref[:, D : 2 * D], wqkv_ref[:, 2 * D :]
    for ref, base in ((keep_ref, 0), (send_ref, 512)):
        part = nt(gk_ref[base : base + 512, :], wk) + nt(gv_ref[base : base + 512, :], wv)
        if base == 0:
            ref[:ROWS, :] = (part[:ROWS] + nt(gq, wq)).astype(BF)
            ref[ROWS:, :] = part[ROWS:].astype(BF)
        else:
            ref[...] = part.astype(BF)
    for ref, half in ((wkeep_ref, core), (wsend_ref, 1 - core)):
        narrow = pl.ds(pl.multiple_of(half * 256, 256), 256)
        ref[0:256, :] = tn(attended_ref[:, narrow], branch).astype(BF)
        ref[256:512, :] = tn(all_ref[:ROWS, narrow], gq).astype(BF)
        ref[512:768, :] = tn(all_ref[:, narrow], gk_ref[...]).astype(BF)
        ref[768:1024, :] = tn(all_ref[:, narrow], gv_ref[...]).astype(BF)


def cross_back_kernel(
    core_ref, grad_ref, g0, g1, g2, g3, after_ref, tokens_ref, mod_ref, gains_ref, wo_ref, wq_ref, wkv_ref,
    query_ref, attended_ref, probs_ref, values_ref, keys_t_ref, image_ref, sums_in_ref,
    tokens_out_ref, keep_ref, send_ref, wkeep_ref, wsend_ref, sums_ref,
    slopes_ref, kv_ref, normed_ref,
):
    core = core_ref[0]
    mod = mod_ref[...]
    gains = gains_ref[...].astype(F32)
    incoming = g0[...].astype(F32) + g1[...].astype(F32) + g2[...].astype(F32) + g3[...].astype(F32)
    xhat, rstd, slope = norm_parts(after_ref[...], gains[1:2], mod[3:4])
    sums_ref[...] = sums_in_ref[...]
    for row, line in enumerate(norm_sums(incoming, xhat, gains[1:2], mod[3:4])):
        sums_ref[3 + row : 4 + row, :] = line
    grad_after = grad_ref[...] + norm_back(incoming, xhat, rstd, slope)
    branch = grad_after.astype(BF)
    grad = nt(branch, wo_ref[...]).astype(BF).astype(F32)
    grad_t = nt(wo_ref[...], branch).astype(BF).astype(F32)
    out_t = attended_ref[...].astype(F32).T
    query = query_ref[...].astype(F32) * SCALE
    gk_ref, gv_ref = kv_ref.at[0], kv_ref.at[1]
    gq = attend_back(
        query, grad, grad_t, out_t, keys_t_ref, values_ref, probs_ref, slopes_ref, gk_ref, gv_ref
    ).astype(BF)
    tokens = tokens_ref[...].astype(F32)
    xhat, rstd, slope = norm_parts(tokens, gains[0:1], mod[1:2])
    normed_ref[...] = (xhat * slope + mod[0:1]).astype(BF)
    incoming = nt(gq, wq_ref[...])
    for row, line in enumerate(norm_sums(incoming, xhat, gains[0:1], mod[1:2])):
        sums_ref[6 + row : 7 + row, :] = line
    tokens_out_ref[...] = grad_after + norm_back(incoming, xhat, rstd, slope)
    wk, wv = wkv_ref[:, :D], wkv_ref[:, D:]
    half_keys = IMG_KEYS // 2
    for ref, base in ((keep_ref, 0), (send_ref, half_keys)):
        span = slice(base, base + half_keys)
        ref[...] = (nt(kv_ref[0, span, :], wk) + nt(kv_ref[1, span, :], wv)).astype(BF)
    for ref, half in ((wkeep_ref, core), (wsend_ref, 1 - core)):
        narrow = pl.ds(pl.multiple_of(half * 256, 256), 256)
        ref[0:256, :] = tn(attended_ref[:, narrow], branch).astype(BF)
        ref[256:512, :] = tn(normed_ref[:, narrow], gq).astype(BF)
        ref[512:896, :] = tn(image_ref[...], kv_ref[half]).astype(BF)
        ref[896:1024, :] = jnp.zeros((128, D), BF)


def wide_out_kernel(core_ref, own_ref, other_ref, w_in_ref, w_out_ref):
    core = core_ref[0]
    for ref, half in ((own_ref, core), (other_ref, 1 - core)):
        w_out_ref[pl.ds(pl.multiple_of(half * 1024, 1024), 1024), :] = ref[:1024, :].astype(F32)
        narrow = pl.ds(pl.multiple_of(half * 256, 256), 256)
        for j in range(4):
            w_in_ref[narrow, D * j : D * j + D] = ref[1024 + 256 * j : 1280 + 256 * j, :].astype(F32)


def middle_out_kernel(core_ref, own_ref, other_ref, wo_ref, wqkv_ref):
    core = core_ref[0]
    for ref, half in ((own_ref, core), (other_ref, 1 - core)):
        narrow = pl.ds(pl.multiple_of(half * 256, 256), 256)
        wo_ref[narrow, :] = ref[0:256, :].astype(F32)
        for j in range(3):
            wqkv_ref[narrow, D * j : D * j + D] = ref[256 + 256 * j : 512 + 256 * j, :].astype(F32)


def last_out_kernel(
    core_ref, own_ref, other_ref, extra_own_ref, extra_other_ref,
    wo_ref, wq_ref, wkv_ref, modw_ref, gains_ref,
):
    core = core_ref[0]
    for ref, half in ((own_ref, core), (other_ref, 1 - core)):
        narrow = pl.ds(pl.multiple_of(half * 256, 256), 256)
        wo_ref[narrow, :] = ref[0:256, :].astype(F32)
        wq_ref[narrow, :] = ref[256:512, :].astype(F32)
        wkv_ref[:, pl.ds(pl.multiple_of(half * D, D), D)] = ref[512:896, :].astype(F32)
    sums = extra_own_ref[...].astype(F32) + extra_other_ref[...].astype(F32)
    acts = jnp.concatenate([extra_own_ref[:, 9, :], extra_own_ref[:, 10, :]], axis=1)
    for norm in range(3):
        first = 3 * (2 - norm)
        gains_ref[norm : norm + 1, :] = jnp.sum(sums[:, first, :], axis=0, keepdims=True)
        for kind in range(2):
            lines = sums[:, first + 1 + kind, :]
            column = D * (2 * norm + kind)
            modw_ref[:, column : column + D] = lax.dot_general(
                acts.astype(F32), lines, (((0,), (0,)), ((), ())),
                preferred_element_type=F32, precision=lax.Precision.HIGHEST,
            )


def swap_core(value):
    return lax.ppermute(value, "core", CORE_SWAP)


def swap_y(value, step):
    return lax.ppermute(value, "y", [(i, i ^ step) for i in range(4)])


def gather_eight(value):
    across = [value] + [swap_y(value, step) for step in (1, 2, 3)]
    return across + [swap_core(item) for item in across]


def scatter_eight(keep, send):
    got = swap_core(send)
    mixed = (keep.astype(F32) + got.astype(F32)).astype(BF).reshape(4, keep.shape[0] // 4, keep.shape[1])
    return [mixed[0]] + [swap_y(mixed[step], step) for step in (1, 2, 3)]


def add_all(items):
    total = items[0].astype(F32)
    for item in items[1:]:
        total = total + item.astype(F32)
    return total


def sum_everywhere(keep, send, extra=None):
    got = swap_core(send)
    mixed = (keep.astype(F32) + got.astype(F32)).astype(BF)
    rows, width = mixed.shape
    parts = lax.all_to_all(mixed, ("x", "z"), 0, 0, tiled=True).reshape(16, rows // 16, width)
    total = jnp.sum(parts.astype(F32), axis=0).astype(BF)
    if extra is not None:
        total = jnp.concatenate([total, extra[0]], axis=0)
    total = add_all([total] + [swap_y(total, step) for step in (1, 2, 3)]).astype(BF)
    if extra is not None:
        total = jnp.concatenate([total, extra[1]], axis=0)
    copies = jnp.broadcast_to(total[None], (16,) + total.shape)
    own = lax.all_to_all(copies, ("x", "z"), 0, 0, tiled=True)
    other = swap_core(own)
    if extra is None:
        return own.reshape(rows, width), other.reshape(rows, width)
    cut = rows // 16
    return (
        own[:, :cut].reshape(rows, width),
        other[:, :cut].reshape(rows, width),
        own[:, cut:],
        other[:, cut:],
    )


def local(
    tokens, camera, image, image_mask, point_rows, point_count, point_grads, mod_weight, norm_gains,
    wq_cross, wkv_cross, wo_cross, wqkv_self, wo_self, w_in, w_out,
):
    y, core = lax.axis_index("y"), lax.axis_index("core")
    core_id = core.astype(jnp.int32).reshape(1)
    owners = jnp.stack([2 * (y ^ (j % 4)) + (core ^ (j // 4)) for j in range(8)]).astype(jnp.int32)
    toks = tokens[0]

    image_blocks = gather_eight(image[0])

    bias = jnp.where(image_mask[0] > 0, 0.0, -1e30).astype(F32).reshape(4, 2, IMG_ROWS)
    flip = (y & 1) == 1
    bias = jnp.where(flip, bias[jnp.array([1, 0, 3, 2])], bias)
    bias = jnp.where((y & 2) == 2, bias[jnp.array([2, 3, 0, 1])], bias)
    bias = jnp.where(core == 1, bias[:, ::-1], bias)
    bias = jnp.pad(bias.transpose(1, 0, 2), ((0, 0), (0, 0), (0, IMG_PAD - IMG_ROWS)), constant_values=-1e30)
    bias = bias.reshape(IMG_KEYS, 1)

    cot_keep, cot_send, mod, act = kernel_call(
        points_kernel,
        [((512, D), BF), ((512, D), BF), ((8, D), F32), ((1, 1024), BF)],
        [], 2 * 1024 * 1024 * 512, 9 << 20, 40,
        owners, point_count[0], point_rows, point_grads[0], camera, mod_weight, smem=2,
    )
    cot_parts = scatter_eight(cot_keep, cot_send)

    after_cross, normed_two, attended_one, query_one, probs_one, values_one, keys_t_one, image_all = kernel_call(
        cross_kernel,
        [
            ((ROWS, D), F32), ((ROWS, D), BF), ((ROWS, D), BF), ((ROWS, D), BF),
            ((2, IMG_KEYS, 512), BF), ((IMG_KEYS, D), BF), ((D, IMG_KEYS), BF), ((IMG_KEYS, 384), BF),
        ],
        [((IMG_KEYS, D), BF), ((D, IMG_KEYS), BF), ((IMG_KEYS, 512), F32)],
        3 * 10**9, 8 << 20, 48,
        toks, mod, norm_gains, wq_cross, wkv_cross, wo_cross, bias, *image_blocks,
    )

    normed_blocks = gather_eight(normed_two)
    (
        layer_out, query_two, probs_two, values_two, keys_t_two, normed_all, attended_two, grad_after_self,
        branch_two, sums, wide_keep, wide_send,
    ) = kernel_call(
        middle_kernel,
        [
            ((ROWS, D), BF), ((ROWS, D), BF), ((2, KEYS, 512), BF), ((KEYS, D), BF), ((D, KEYS), BF),
            ((KEYS, D), BF), ((ROWS, D), BF), ((ROWS, D), F32), ((ROWS, D), BF), ((16, D), F32),
            ((2048, D), BF), ((2048, D), BF),
        ],
        [((KEYS, D), BF), ((D, KEYS), BF), ((KEYS, 512), F32), ((ROWS, 2048), BF), ((ROWS, D), BF)],
        6 * 10**9, 20 << 20, 56,
        core_id, after_cross, mod, norm_gains, wqkv_self, wo_self, w_in, w_out, *normed_blocks, *cot_parts, smem=1,
    )
    wide = sum_everywhere(wide_keep, wide_send)

    back_keep, back_send, mid_keep, mid_send = kernel_call(
        self_back_kernel,
        [((512, D), BF), ((512, D), BF), ((1024, D), BF), ((1024, D), BF)],
        [((KEYS, 512), BF), ((KEYS, D), BF), ((KEYS, D), BF)],
        6 * 10**9, 12 << 20, 48,
        core_id, branch_two, wo_self, wqkv_self, query_two, attended_two, probs_two, values_two, keys_t_two,
        normed_all, smem=1,
    )
    back_parts = scatter_eight(back_keep, back_send)
    middle = sum_everywhere(mid_keep, mid_send)

    grad_tokens, img_keep, img_send, last_keep, last_send, sums = kernel_call(
        cross_back_kernel,
        [
            ((ROWS, D), F32), ((IMG_KEYS // 2, 384), BF), ((IMG_KEYS // 2, 384), BF),
            ((1024, D), BF), ((1024, D), BF), ((16, D), F32),
        ],
        [((IMG_KEYS, 512), BF), ((2, IMG_KEYS, D), BF), ((ROWS, D), BF)],
        6 * 10**9, 12 << 20, 48,
        core_id, grad_after_self, *back_parts, after_cross, toks, mod, norm_gains, wo_cross, wq_cross, wkv_cross,
        query_one, attended_one, probs_one, values_one, keys_t_one, image_all, sums, smem=1,
    )
    grad_image = add_all(scatter_eight(img_keep, img_send))[:IMG_ROWS]

    extra = (sums.astype(BF), jnp.pad(act.reshape(2, D), ((9, 5), (0, 0))))
    own, other, extra_own, extra_other = sum_everywhere(last_keep, last_send, extra)
    extra_own = jnp.concatenate([extra_own[:, :9], extra_own[:, 25:32]], axis=1)
    extra_other = extra_other[:, :16]

    g_in, g_out = kernel_call(
        wide_out_kernel, [((D, 2048), F32), ((2048, D), F32)], [], 10**7, 12 << 20, 40, core_id, *wide, smem=1
    )
    g_wo_self, g_wqkv = kernel_call(
        middle_out_kernel, [((D, D), F32), ((D, 3 * D), F32)], [], 10**7, 6 << 20, 40, core_id, *middle, smem=1
    )
    g_wo_cross, g_wq, g_wkv, g_mod, g_gains = kernel_call(
        last_out_kernel,
        [((D, D), F32), ((D, D), F32), ((384, 2 * D), F32), ((1024, 6 * D), F32), ((3, D), F32)],
        [], 10**8, 18 << 20, 48,
        core_id, own, other, extra_own, extra_other, smem=1,
    )
    return (
        layer_out[None], grad_tokens[None], grad_image[None], g_mod, g_gains, g_wq, g_wkv, g_wo_cross, g_wqkv,
        g_wo_self, g_in, g_out,
    )


def solution(mesh):
    split = Mesh(mesh.devices.reshape(4, 4, 4, 2), ("x", "z", "y", "core"))
    obj, tok = ("x", "z"), ("y", "core")
    return jax.shard_map(
        local,
        mesh=split,
        in_specs=(
            P(obj, tok, None), P(obj, None), P(obj, tok, None), P(obj, None), P(obj, tok), P(obj, tok),
            P(obj, tok, None),
        )
        + (P(),) * 9,
        out_specs=(P(obj, tok, None),) * 3 + (P(),) * 9,
        check_vma=False,
    )
```

```python
import functools

import jax
import jax.numpy as jnp
from jax import lax
from jax.experimental import pallas as pl
from jax.experimental.pallas import tpu as pltpu
from jax.sharding import Mesh
from jax.sharding import PartitionSpec as P

BF = jnp.bfloat16
F32 = jnp.float32
D = 512
ROWS = 128
IMG_ROWS = 130
IMG_PAD = 144
IMG_KEYS = 8 * IMG_PAD
KEYS = 8 * ROWS
SCALE = 0.125
CORE_SWAP = [(0, 1), (1, 0)]
VMEM = pl.BlockSpec(memory_space=pltpu.VMEM)
SMEM = pl.BlockSpec(memory_space=pltpu.SMEM)
ANY = pl.BlockSpec(memory_space=pl.ANY)


def nn(left, right):
    return jnp.dot(left, right, preferred_element_type=F32)


def nt(left, right):
    return lax.dot_general(left, right, (((1,), (1,)), ((), ())), preferred_element_type=F32)


def tn(left, right):
    return lax.dot_general(left, right, (((0,), (0,)), ((), ())), preferred_element_type=F32)


def kernel_call(body, outs, scratch, flops, *args, smem=0, hbm=0, hbm_outs=0, copies=0):
    in_specs = [SMEM] * smem + [VMEM] * (len(args) - smem - hbm) + [ANY] * hbm
    moved = sum(item.size * item.dtype.itemsize for item in args)
    return pl.pallas_call(
        body,
        out_shape=[jax.ShapeDtypeStruct(shape, dtype) for shape, dtype in outs],
        in_specs=in_specs,
        out_specs=[VMEM] * (len(outs) - hbm_outs) + [ANY] * hbm_outs,
        scratch_shapes=[pltpu.VMEM(shape, dtype) for shape, dtype in scratch]
        + ([pltpu.SemaphoreType.DMA((copies,))] if copies else []),
        compiler_params=pltpu.CompilerParams(vmem_limit_bytes=60 << 20),
        cost_estimate=pl.CostEstimate(flops=flops, bytes_accessed=moved, transcendentals=0),
    )(*args)


def fetch(pairs, semaphores, first=0):
    copies = [
        pltpu.make_async_copy(source, target, semaphores.at[first + i]) for i, (source, target) in enumerate(pairs)
    ]
    for copy in copies:
        copy.start()
    return copies


def norm_parts(values, gain, scale):
    center = values - jnp.mean(values, axis=-1, keepdims=True)
    rstd = lax.rsqrt(jnp.mean(center * center, axis=-1, keepdims=True) + 1e-05)
    return center * rstd, rstd, gain * (1.0 + scale)


def norm_back(grad, xhat, rstd, slope):
    scaled = grad * slope
    return rstd * (
        scaled
        - jnp.mean(scaled, axis=-1, keepdims=True)
        - xhat * jnp.mean(scaled * xhat, axis=-1, keepdims=True)
    )


def norm_sums(grad, xhat, gain, scale):
    total = jnp.sum(grad * xhat, axis=0, keepdims=True)
    return total * (1.0 + scale), jnp.sum(grad, axis=0, keepdims=True), total * gain


def spread_columns(block):
    head = lax.broadcasted_iota(jnp.int32, block.shape, 0) >> 6
    return jnp.concatenate([jnp.where(head == j, block, 0.0) for j in range(4)], axis=1)


def spread_rows(block):
    head = lax.broadcasted_iota(jnp.int32, block.shape, 1) >> 6
    return jnp.concatenate([jnp.where(head == j, block, 0.0) for j in range(4)], axis=0)


def gather_heads(wide):
    return jnp.concatenate(
        [wide[64 * j : 64 * j + 64, 128 * j : 128 * j + 128] for j in range(4)], axis=0
    )


def fold8(values, reduce):
    rows, width = values.shape
    return reduce(values.reshape(rows // 8, 8, width), axis=0)


def chunked(total):
    return [(start, min(256, total - start)) for start in range(0, total, 256)]


def soften_quad(quad, q_t, keys_ref, probs_ref, score_ref, bias_ref):
    chunks = chunked(keys_ref.shape[0])
    lanes = slice(256 * quad, 256 * quad + 256)
    spread = spread_columns(q_t[lanes, :]).astype(BF)
    top = None
    for start, size in chunks:
        scores = nn(keys_ref[start : start + size, lanes], spread)
        if bias_ref is not None:
            scores = scores + bias_ref[start : start + size, :]
        score_ref[start : start + size, :] = scores
        here = fold8(scores, jnp.max)
        top = here if top is None else jnp.maximum(top, here)
    top = jnp.max(top, axis=0, keepdims=True)
    total = None
    for start, size in chunks:
        weights = jnp.exp(score_ref[start : start + size, :] - top)
        score_ref[start : start + size, :] = weights
        here = fold8(weights, jnp.sum)
        total = here if total is None else total + here
    inverse = 1.0 / jnp.sum(total, axis=0, keepdims=True)
    for start, size in chunks:
        probs_ref[quad, start : start + size, :] = (score_ref[start : start + size, :] * inverse).astype(BF)


def soften(q_t, keys_ref, probs_ref, score_ref, bias_ref):
    for quad in range(2):
        soften_quad(quad, q_t, keys_ref, probs_ref, score_ref, bias_ref)


def attend(q_t, keys_ref, values_t_ref, probs_ref, score_ref, bias_ref):
    parts = []
    for quad in range(2):
        soften_quad(quad, q_t, keys_ref, probs_ref, score_ref, bias_ref)
        parts.append(gather_heads(nn(values_t_ref[256 * quad : 256 * quad + 256, :], probs_ref[quad])))
    return jnp.concatenate(parts, axis=0)


def attend_back(q_s, grad, grad_t, out_t, keys_t_ref, values_ref, probs_ref, slopes_ref, gk_ref, gv_ref):
    key_total = values_ref.shape[0]
    chunks = [(start, min(256, key_total - start)) for start in range(0, key_total, 256)]
    inner = grad_t * out_t
    parts = []
    for quad in range(2):
        lanes = slice(256 * quad, 256 * quad + 256)
        spread = spread_columns(grad_t[lanes, :]).astype(BF)
        delta = jnp.concatenate(
            [
                jnp.sum(inner[256 * quad + 64 * j : 256 * quad + 64 * j + 64, :], axis=0, keepdims=True)
                for j in range(4)
            ],
            axis=1,
        )
        grad_rows = spread_rows(grad[:, lanes]).astype(BF)
        query_rows = spread_rows(q_s[:, lanes]).astype(BF)
        for start, size in chunks:
            span = slice(start, start + size)
            grad_probs = nn(values_ref[span, lanes], spread)
            probs = probs_ref[quad, span, :]
            slopes = (probs.astype(F32) * (grad_probs - delta)).astype(BF)
            slopes_ref[span, :] = slopes
            gv_ref[span, lanes] = nn(probs, grad_rows).astype(BF)
            gk_ref[span, lanes] = nn(slopes, query_rows).astype(BF)
        parts.append(gather_heads(nn(keys_t_ref[lanes, :], slopes_ref[...])))
    return jnp.concatenate(parts, axis=0).T * SCALE


def points_kernel(owner_ref, count_ref, rows_ref, grads_ref, camera_ref, modw_ref, keep_ref, send_ref, mod_ref, act_ref):
    row_ids = rows_ref[...]
    slot = lax.broadcasted_iota(jnp.int32, row_ids.shape, 1)
    row_ids = jnp.where(slot < count_ref[0], row_ids, -1)
    for block in range(8):
        target = lax.broadcasted_iota(jnp.int32, (ROWS, row_ids.shape[1]), 0) + owner_ref[block] * ROWS
        onehot = jnp.where(target == row_ids, 1.0, 0.0).astype(BF)
        part = nn(onehot, grads_ref[...]).astype(BF)
        out = keep_ref if block < 4 else send_ref
        out[ROWS * (block % 4) : ROWS * (block % 4) + ROWS, :] = part
    camera = camera_ref[...].astype(F32)
    act = (camera / (1.0 + jnp.exp(-camera))).astype(BF)
    act_ref[...] = act
    modulation = nn(jnp.broadcast_to(act, (16, act.shape[1])), modw_ref[...])
    for row in range(6):
        mod_ref[row : row + 1, :] = modulation[0:1, D * row : D * row + D]
    mod_ref[6:8, :] = jnp.zeros((2, D), F32)


def stack_image(image_ref, blocks):
    for j, block in enumerate(blocks):
        base = IMG_PAD * j
        image_ref[base + 128 : base + IMG_PAD, :] = jnp.zeros((16, image_ref.shape[1]), BF)
        image_ref[base : base + IMG_ROWS, :] = block[...]


def cross_kernel(
    tokens_ref, mod_ref, gains_ref, wq_ref, bias_ref, i0, i1, i2, i3, i4, i5, i6, i7, wkv_hbm, wo_hbm,
    after_ref, normed_ref, attended_ref, query_ref,
    image_ref, keys_ref, values_t_ref, score_ref, probs_ref, wkv_ref, wo_ref, sems,
):
    copies = fetch([(wkv_hbm, wkv_ref), (wo_hbm, wo_ref)], sems)
    stack_image(image_ref, (i0, i1, i2, i3, i4, i5, i6, i7))
    mod = mod_ref[...]
    gains = gains_ref[...].astype(F32)
    tokens = tokens_ref[...].astype(F32)
    xhat, _, slope = norm_parts(tokens, gains[0:1], mod[1:2])
    normed = (xhat * slope + mod[0:1]).astype(BF)
    query = nn(normed, wq_ref[...]).astype(BF)
    query_ref[...] = query
    copies[0].wait()
    keys_ref[...] = nn(image_ref[...], wkv_ref[:, :D]).astype(BF)
    values_t_ref[...] = nt(wkv_ref[:, D:].T, image_ref[...]).astype(BF)
    q_t = query.astype(F32).T * SCALE
    out_t = attend(q_t, keys_ref, values_t_ref, probs_ref, score_ref, bias_ref)
    attended = out_t.T.astype(BF)
    attended_ref[...] = attended
    copies[1].wait()
    after = tokens + nn(attended, wo_ref[...])
    after_ref[...] = after
    xhat, _, slope = norm_parts(after, gains[1:2], mod[3:4])
    normed_ref[...] = (xhat * slope + mod[2:3]).astype(BF)


def cross_rest_kernel(
    query_ref, bias_ref, wkv_ref, i0, i1, i2, i3, i4, i5, i6, i7,
    values_ref, keys_t_ref, image_ref, probs_ref,
    keys_ref, score_ref,
):
    stack_image(image_ref, (i0, i1, i2, i3, i4, i5, i6, i7))
    keys_ref[...] = nn(image_ref[...], wkv_ref[:, :D]).astype(BF)
    values_ref[...] = nn(image_ref[...], wkv_ref[:, D:]).astype(BF)
    keys_t_ref[...] = nt(wkv_ref[:, :D].T, image_ref[...]).astype(BF)
    soften(query_ref[...].astype(F32).T * SCALE, keys_ref, probs_ref, score_ref, bias_ref)


def gelu_parts(value):
    c = 0.7978845608028654
    square = value * value
    bent = jnp.tanh(c * value * (1.0 + 0.044715 * square))
    half = 0.5 * (1.0 + bent)
    slope = half + 0.5 * value * (1.0 - bent * bent) * (c * (1.0 + 3.0 * 0.044715 * square))
    return value * half, slope


def middle_kernel(
    place_ref, after_ref, mod_ref, gains_ref, wqkv_ref, n0, n1, n2, n3, n4, n5, n6, n7, c0, c1, c2, c3,
    wo_hbm, w_in_hbm, w_out_hbm,
    out_ref, grad_ref, sums_ref, keep_ref, send_ref, mid_keep_ref, mid_send_ref, pack_keep_hbm, pack_send_hbm,
    all_ref, keys_ref, keys_t_ref, values_ref, values_t_ref, probs_ref, score_ref, slopes_ref, gk_ref, gv_ref,
    hidden_ref, inner_ref, attended_ref, pack_keep_ref, pack_send_ref, wo_ref, w_in_ref, w_out_ref, sems,
):
    copies = fetch([(wo_hbm, wo_ref), (w_in_hbm, w_in_ref), (w_out_hbm, w_out_ref)], sems)
    y, core = place_ref[2], place_ref[3]
    for j, block in enumerate((n0, n1, n2, n3, n4, n5, n6, n7)):
        all_ref[ROWS * j : ROWS * j + ROWS, :] = block[...]
    mod = mod_ref[...]
    gains = gains_ref[...].astype(F32)
    wq, wk, wv = wqkv_ref[:, :D], wqkv_ref[:, D : 2 * D], wqkv_ref[:, 2 * D :]
    query = nn(n0[...], wq).astype(BF).astype(F32) * SCALE
    keys_ref[...] = nn(all_ref[...], wk).astype(BF)
    values_t_ref[...] = nt(wv.T, all_ref[...]).astype(BF)
    values_ref[...] = nn(all_ref[...], wv).astype(BF)
    keys_t_ref[...] = nt(wk.T, all_ref[...]).astype(BF)
    out_t = attend(query.T, keys_ref, values_t_ref, probs_ref, score_ref, None)
    attended = out_t.T.astype(BF)
    attended_ref[...] = attended
    copies[0].wait()
    after = after_ref[...] + nn(attended, wo_ref[...])
    xhat, rstd, slope = norm_parts(after, gains[2:3], mod[5:6])
    normed = (xhat * slope + mod[4:5]).astype(BF)
    copies[1].wait()
    inner = nn(normed, w_in_ref[...])
    value, bend = gelu_parts(inner)
    hidden_ref[...] = value.astype(BF)
    copies[2].wait()
    result = after + nn(hidden_ref[...], w_out_ref[...])
    out_ref[...] = result.astype(BF)
    cot = add_all([c0[...], c1[...], c2[...], c3[...]])
    branch = cot.astype(BF)
    grad_inner = (nt(branch, w_out_ref[...]) * bend).astype(BF)
    inner_ref[...] = grad_inner
    for ref, half in ((pack_send_ref, 1 - core), (pack_keep_ref, core)):
        wide = pl.ds(pl.multiple_of(half * 1024, 1024), 1024)
        ref[:, :D] = normed
        ref[:, D : 2 * D] = branch
        ref[:, 1024:2048] = hidden_ref[:, wide]
        ref[:, 2048:] = inner_ref[:, wide]
    saved = fetch([(pack_send_ref, pack_send_hbm), (pack_keep_ref, pack_keep_hbm)], sems, 3)
    grad = nt(grad_inner, w_in_ref[...])
    sums_ref[...] = jnp.zeros(sums_ref.shape, F32)
    for row, line in enumerate(norm_sums(grad, xhat, gains[2:3], mod[5:6])):
        sums_ref[row : row + 1, :] = line
    grad_after = cot + norm_back(grad, xhat, rstd, slope)
    grad_ref[...] = grad_after
    branch = grad_after.astype(BF)
    grad = nt(branch, wo_ref[...]).astype(BF).astype(F32)
    grad_t = nt(wo_ref[...], branch).astype(BF).astype(F32)
    gq = attend_back(
        query, grad, grad_t, out_t, keys_t_ref, values_ref, probs_ref, slopes_ref, gk_ref, gv_ref
    ).astype(BF)
    for ref, base in ((send_ref, 512), (keep_ref, 0)):
        part = nt(gk_ref[base : base + 512, :], wk) + nt(gv_ref[base : base + 512, :], wv)
        if base == 0:
            ref[:ROWS, :] = (part[:ROWS] + nt(gq, wq)).astype(BF)
            ref[ROWS:, :] = part[ROWS:].astype(BF)
        else:
            ref[...] = part.astype(BF)
    for ref, half in ((mid_send_ref, 1 - core), (mid_keep_ref, core)):
        narrow = pl.ds(pl.multiple_of(half * 256, 256), 256)
        ref[y] = tn(attended_ref[:, narrow], branch).astype(BF)
        ref[1 ^ y] = tn(all_ref[:ROWS, narrow], gq).astype(BF)
        ref[2 ^ y] = tn(all_ref[:, narrow], gk_ref[...]).astype(BF)
        ref[3 ^ y] = tn(all_ref[:, narrow], gv_ref[...]).astype(BF)
    for copy in saved:
        copy.wait()


def wide_kernel(own_ref, got_ref, out_ref, rows_ref):
    rows_ref[:ROWS, :] = own_ref[...]
    rows_ref[ROWS:, :] = got_ref[...]
    out_ref[:1024, :] = tn(rows_ref[:, 1024:2048], rows_ref[:, D : 2 * D]).astype(BF)
    for j in range(2):
        part = tn(rows_ref[:, :D], rows_ref[:, 2048 + D * j : 2560 + D * j])
        out_ref[1024 + D * j : 1536 + D * j, :] = part.astype(BF)


def cross_back_kernel(
    place_ref, grad_ref, g0, g1, g2, g3, after_ref, tokens_ref, mod_ref, gains_ref, query_ref, attended_ref,
    sums_in_ref, act_ref, wo_hbm, values_hbm, probs_hbm, keys_t_hbm, wq_hbm, wkv_hbm, image_hbm,
    tokens_out_ref, keep_ref, send_ref, last_keep_ref, last_send_ref,
    sums_ref, slopes_ref, kv_ref, normed_ref, wo_ref, values_ref, probs_ref, keys_t_ref, wq_ref, wkv_ref, image_ref, sems,
):
    copies = fetch(
        [
            (wo_hbm, wo_ref), (values_hbm, values_ref), (probs_hbm, probs_ref), (keys_t_hbm, keys_t_ref),
            (wq_hbm, wq_ref), (wkv_hbm, wkv_ref), (image_hbm, image_ref),
        ],
        sems,
    )
    y, core = place_ref[2], place_ref[3]
    mod = mod_ref[...]
    gains = gains_ref[...].astype(F32)
    incoming = add_all([g0[...], g1[...], g2[...], g3[...]])
    xhat, rstd, slope = norm_parts(after_ref[...], gains[1:2], mod[3:4])
    sums_ref[...] = sums_in_ref[...]
    for row, line in enumerate(norm_sums(incoming, xhat, gains[1:2], mod[3:4])):
        sums_ref[3 + row : 4 + row, :] = line
    grad_after = grad_ref[...] + norm_back(incoming, xhat, rstd, slope)
    branch = grad_after.astype(BF)
    copies[0].wait()
    grad = nt(branch, wo_ref[...]).astype(BF).astype(F32)
    grad_t = nt(wo_ref[...], branch).astype(BF).astype(F32)
    out_t = attended_ref[...].astype(F32).T
    query = query_ref[...].astype(F32) * SCALE
    gk_ref, gv_ref = kv_ref.at[0], kv_ref.at[1]
    for copy in copies[1:4]:
        copy.wait()
    gq = attend_back(
        query, grad, grad_t, out_t, keys_t_ref, values_ref, probs_ref, slopes_ref, gk_ref, gv_ref
    ).astype(BF)
    tokens = tokens_ref[...].astype(F32)
    xhat, rstd, slope = norm_parts(tokens, gains[0:1], mod[1:2])
    normed_ref[...] = (xhat * slope + mod[0:1]).astype(BF)
    for copy in copies[4:]:
        copy.wait()
    incoming = nt(gq, wq_ref[...])
    for row, line in enumerate(norm_sums(incoming, xhat, gains[0:1], mod[1:2])):
        sums_ref[6 + row : 7 + row, :] = line
    tokens_out_ref[...] = grad_after + norm_back(incoming, xhat, rstd, slope)
    wk, wv = wkv_ref[:, :D], wkv_ref[:, D:]
    half_keys = IMG_KEYS // 2
    for ref, base in ((keep_ref, 0), (send_ref, half_keys)):
        span = slice(base, base + half_keys)
        ref[...] = (nt(kv_ref[0, span, :], wk) + nt(kv_ref[1, span, :], wv)).astype(BF)
    act = act_ref[...].astype(F32)
    sums_ref[9:10, :] = act[:, :D]
    sums_ref[10:11, :] = act[:, D:]
    sums = sums_ref[...].astype(BF)
    for ref, half in ((last_send_ref, 1 - core), (last_keep_ref, core)):
        narrow = pl.ds(pl.multiple_of(half * 256, 256), 256)
        ref[y, :256, :] = tn(attended_ref[:, narrow], branch).astype(BF)
        ref[1 ^ y, :256, :] = tn(normed_ref[:, narrow], gq).astype(BF)
        part = tn(image_ref[...], kv_ref[half]).astype(BF)
        for side in range(2):
            ref[(2 + side) ^ y, :192, :] = part[192 * side : 192 * side + 192, :]
            ref[(2 + side) ^ y, 192:256, :] = jnp.zeros((64, D), BF)
        for j in range(4):
            ref[j, 256:, :] = sums


def fold_kernel(place_ref, m0, m1, m2, m3, l0, l1, l2, l3, t0, t1, t2, t3, total_ref):
    total_ref[:, :64, :] = add_all([m0[...], m1[...], m2[...], m3[...]]).astype(BF).reshape(4, 64, D)
    late = add_all([l0[...], l1[...], l2[...], l3[...]]).astype(BF)
    total_ref[:, 64:, :] = late[:256].reshape(4, 64, D)
    for j, ref in enumerate((t0, t1, t2, t3)):
        ref[:ROWS, :] = total_ref[place_ref[0] ^ j]
        ref[ROWS:, :] = late[256:]


def join_kernel(a_ref, b_ref, c_ref, d_ref, out_ref):
    refs = (a_ref, b_ref, c_ref, d_ref)
    out_ref[:ROWS, :] = add_all([ref[:ROWS, :] for ref in refs]).astype(BF)
    for j, ref in enumerate(refs):
        out_ref[ROWS + 16 * j : ROWS + 16 * j + 16, :] = ref[ROWS:, :]


def meet_kernel(a_ref, b_ref, c_ref, d_ref, out_ref, sums_ref):
    refs = (a_ref, b_ref, c_ref, d_ref)
    out_ref[...] = add_all([ref[:ROWS, :] for ref in refs]).astype(BF)
    for j, ref in enumerate(refs):
        sums_ref[64 * j : 64 * j + 64, :] = ref[ROWS:, :]


def wide_sum_kernel(parts_ref, total_ref):
    total_ref[...] = jnp.sum(parts_ref[...].astype(F32), axis=0).astype(BF)


def wide_copies_kernel(a_ref, b_ref, c_ref, d_ref, copies_ref):
    total = add_all([a_ref[...], b_ref[...], c_ref[...], d_ref[...]]).astype(BF)
    for j in range(16):
        copies_ref[j] = total


def wide_out_kernel(place_ref, own_ref, other_ref, w_in_hbm, w_out_hbm, w_in_ref, w_out_ref, sems):
    core = place_ref[3]
    copies = []
    for ref, half in ((own_ref, core), (other_ref, 1 - core)):
        for j in range(2):
            rows = pl.ds(pl.multiple_of(half * 1024 + D * j, D), D)
            w_out_ref[rows, :] = ref[4 * j : 4 * j + 4].reshape(D, D).astype(F32)
            copies += fetch([(w_out_ref.at[rows], w_out_hbm.at[rows])], sems, len(copies))
        for j in range(2):
            columns = pl.ds(pl.multiple_of(half * 1024 + D * j, D), D)
            w_in_ref[:, columns] = ref[8 + 4 * j : 12 + 4 * j].reshape(D, D).astype(F32)
            copies += fetch([(w_in_ref.at[:, columns], w_in_hbm.at[:, columns])], sems, len(copies))
    for copy in copies:
        copy.wait()


def modulation_kernel(sums_in_ref, gains_ref, modw_hbm, modw_ref, sems):
    sums = sums_in_ref[...].astype(F32)
    acts = (jnp.concatenate([sums[:, 9, :], sums[:, 10, :]], axis=1) * 0.125).astype(BF)
    copies = []
    for norm in range(3):
        first = 3 * (2 - norm)
        gains_ref[norm : norm + 1, :] = jnp.sum(sums[:, first, :], axis=0, keepdims=True)
        for kind in range(2):
            part = 2 * norm + kind
            modw_ref[part] = tn(acts, sums[:, first + 1 + kind, :].astype(BF))
            target = modw_hbm.at[:, D * part : D * part + D]
            copies += fetch([(modw_ref.at[part], target)], sems, len(copies))
    for copy in copies:
        copy.wait()


def late_out_kernel(place_ref, a0, a1, a2, a3, b0, b1, b2, b3, wo_self_ref, wqkv_ref, wo_ref, wq_ref, wkv_ref):
    x, y, core = place_ref[0], place_ref[2], place_ref[3]
    for side, refs in enumerate(((a0, a1, a2, a3), (b0, b1, b2, b3))):
        half = core ^ side
        column = pl.ds(pl.multiple_of(half * D, D), D)
        for j, ref in enumerate(refs):
            block = y ^ j
            for across in range(4):
                strip = x ^ across
                rows = pl.ds(pl.multiple_of(half * 256 + strip * 64, 64), 64)
                early, late = ref[across, :64, :].astype(F32), ref[across, 64:, :].astype(F32)

                @pl.when(block == 0)
                def _():
                    wo_self_ref[rows, :] = early
                    wo_ref[rows, :] = late

                @pl.when(block > 0)
                def _():
                    wqkv_ref[rows, pl.ds(pl.multiple_of((block - 1) * D, D), D)] = early

                @pl.when(block == 1)
                def _():
                    wq_ref[rows, :] = late

                @pl.when((block > 1) & (strip < 3))
                def _():
                    start = pl.multiple_of((block - 2) * 192 + strip * 64, 64)
                    wkv_ref[pl.ds(start, 64), column] = late


def tie(*values):
    return lax.optimization_barrier(values)


def swap_core(value):
    return lax.ppermute(value, "core", CORE_SWAP)


def swap(value, axis, step):
    return lax.ppermute(value, axis, [(i, i ^ step) for i in range(4)])


def swap_y(value, step):
    return swap(value, "y", step)


def gather_eight(value):
    across = [value] + [swap_y(value, step) for step in (1, 2, 3)]
    return across + [swap_core(item) for item in across]


def scatter_eight(keep, send):
    got = swap_core(send)
    mixed = (keep.astype(F32) + got.astype(F32)).astype(BF).reshape(4, keep.shape[0] // 4, keep.shape[1])
    return [mixed[0]] + [swap_y(mixed[step], step) for step in (1, 2, 3)]


def add_all(items):
    total = items[0].astype(F32)
    for item in items[1:]:
        total = total + item.astype(F32)
    return total


def halve(keep, send):
    return (keep.astype(F32) + swap_core(send).astype(F32)).astype(BF)


def spread(mixed):
    rows, width = mixed.shape
    return lax.all_to_all(mixed, ("x", "z"), 0, 0, tiled=True).reshape(16, rows // 16, width)


def collect(copies):
    return lax.all_to_all(copies, ("x", "z"), 0, 0, tiled=True)


def others(pieces, axis):
    return [pieces[0]] + [swap(pieces[step], axis, step) for step in (1, 2, 3)]


def gather_axis(value, axis):
    return jnp.stack(others([value] * 4, axis))


def local(
    tokens, camera, image, image_mask, point_rows, point_count, point_grads, mod_weight, norm_gains,
    wq_cross, wkv_cross, wo_cross, wqkv_self, wo_self, w_in, w_out,
):
    place = [lax.axis_index(axis).astype(jnp.int32) for axis in ("x", "z", "y", "core")]
    y, core = place[2:]
    place = jnp.stack(place)
    owners = jnp.stack([2 * (y ^ (j % 4)) + (core ^ (j // 4)) for j in range(8)]).astype(jnp.int32)
    toks = tokens[0]

    image_blocks = gather_eight(image[0])

    bias = jnp.where(image_mask[0] > 0, 0.0, -1e30).astype(F32).reshape(2, 2, 2, IMG_ROWS)
    for axis, bit in ((0, y & 2), (1, y & 1), (2, core)):
        bias = jnp.where(bit != 0, jnp.flip(bias, axis), bias)
    bias = jnp.pad(bias.transpose(2, 0, 1, 3), ((0, 0),) * 3 + ((0, IMG_PAD - IMG_ROWS),), constant_values=-1e30)
    bias = bias.reshape(IMG_KEYS, 1)

    cot_keep, cot_send, mod, act = kernel_call(
        points_kernel,
        [((512, D), BF), ((512, D), BF), ((8, D), F32), ((1, 1024), BF)],
        [], 6 * 10**9,
        owners, point_count[0], point_rows, point_grads[0], camera, mod_weight, smem=2,
    )
    cot_parts = scatter_eight(cot_keep, cot_send)

    after_cross, normed_two, attended_one, query_one = kernel_call(
        cross_kernel,
        [((ROWS, D), F32), ((ROWS, D), BF), ((ROWS, D), BF), ((ROWS, D), BF)],
        [
            ((IMG_KEYS, 384), BF), ((IMG_KEYS, D), BF), ((D, IMG_KEYS), BF), ((IMG_KEYS, 512), F32),
            ((2, IMG_KEYS, 512), BF), ((384, 2 * D), BF), ((D, D), BF),
        ],
        10 * 10**9,
        toks, mod, norm_gains, wq_cross, bias, *image_blocks, wkv_cross, wo_cross, hbm=2, copies=2,
    )

    normed_two, *cot_parts = tie(normed_two, *cot_parts)
    across = others([normed_two] * 4, "y")
    values_one, keys_t_one, image_all, probs_one = kernel_call(
        cross_rest_kernel,
        [((IMG_KEYS, D), BF), ((D, IMG_KEYS), BF), ((IMG_KEYS, 384), BF), ((2, IMG_KEYS, 512), BF)],
        [((IMG_KEYS, D), BF), ((IMG_KEYS, 512), F32)],
        7 * 10**9, tie(query_one, normed_two)[0], bias, wkv_cross, *image_blocks,
    )
    values_one, keys_t_one, image_all, probs_one, *across = tie(values_one, keys_t_one, image_all, probs_one, *across)
    normed_blocks = across + [swap_core(item) for item in across]
    (
        layer_out, grad_after_self, sums, back_keep, back_send, mid_keep, mid_send, pack_keep, pack_send,
    ) = kernel_call(
        middle_kernel,
        [
            ((ROWS, D), BF), ((ROWS, D), F32), ((16, D), F32), ((512, D), BF), ((512, D), BF),
            ((4, 256, D), BF), ((4, 256, D), BF), ((ROWS, 3072), BF), ((ROWS, 3072), BF),
        ],
        [
            ((KEYS, D), BF), ((KEYS, D), BF), ((D, KEYS), BF), ((KEYS, D), BF), ((D, KEYS), BF),
            ((2, KEYS, 512), BF), ((KEYS, 512), F32), ((KEYS, 512), BF), ((KEYS, D), BF), ((KEYS, D), BF),
            ((ROWS, 2048), BF), ((ROWS, 2048), BF), ((ROWS, D), BF), ((ROWS, 3072), BF), ((ROWS, 3072), BF),
            ((D, D), BF), ((D, 2048), BF), ((2048, D), BF),
        ],
        20 * 10**9,
        place, after_cross, mod, norm_gains, wqkv_self, *normed_blocks, *cot_parts, wo_self, w_in, w_out,
        smem=1, hbm=3, hbm_outs=2, copies=5,
    )

    back_got = swap_core(back_send)
    pack_got = swap_core(pack_send)
    mid_got = swap_core(mid_send)
    back_mixed = (back_keep.astype(F32) + back_got.astype(F32)).astype(BF)
    back_parts = others(back_mixed.reshape(4, ROWS, D), "y")
    (wide_mixed,) = kernel_call(
        wide_kernel, [((2048, D), BF)], [((256, 3072), BF)], 3 * 10**9, tie(pack_keep, back_mixed)[0], pack_got
    )
    mid_keep, mid_got, _ = tie(mid_keep, mid_got, back_mixed)
    mid_pieces = [(mid_keep[j].astype(F32) + mid_got[j].astype(F32)).astype(BF) for j in range(4)]
    wide_mixed, *pieces = tie(wide_mixed, *back_parts, *mid_pieces)
    back_parts, mid_pieces = pieces[:4], pieces[4:]
    wide_parts = spread(wide_mixed)
    mid_pieces = others(mid_pieces, "y")

    grad_tokens, img_keep, img_send, last_keep, last_send = kernel_call(
        cross_back_kernel,
        [
            ((ROWS, D), F32), ((IMG_KEYS // 2, 384), BF), ((IMG_KEYS // 2, 384), BF),
            ((4, 272, D), BF), ((4, 272, D), BF),
        ],
        [
            ((16, D), F32), ((IMG_KEYS, 512), BF), ((2, IMG_KEYS, D), BF), ((ROWS, D), BF), ((D, D), BF), ((IMG_KEYS, D), BF),
            ((2, IMG_KEYS, 512), BF), ((D, IMG_KEYS), BF), ((D, D), BF), ((384, 2 * D), BF), ((IMG_KEYS, 384), BF),
        ],
        11 * 10**9,
        place, grad_after_self, *back_parts, after_cross, toks, mod, norm_gains, query_one, attended_one, sums, act,
        wo_cross, values_one, probs_one, keys_t_one, wq_cross, wkv_cross, image_all, smem=1, hbm=7, copies=7,
    )
    last_send, img_send, *mid_pieces = tie(last_send, img_send, *mid_pieces)
    last_got = swap_core(last_send)
    last_pieces = others([(last_keep[j].astype(F32) + last_got[j].astype(F32)).astype(BF) for j in range(4)], "y")
    *last_pieces, wide_parts, img_send = tie(*last_pieces, wide_parts, img_send)
    late_pieces = kernel_call(
        fold_kernel, [((144, D), BF)] * 4, [((4, ROWS, D), BF)], 2 * 10**9, place, *mid_pieces, *last_pieces, smem=1
    )
    late_pieces = others(late_pieces, "x")
    (wide,) = kernel_call(wide_sum_kernel, [((ROWS, D), BF)], [], 2 * 10**9, wide_parts)
    wide_pieces = others([wide] * 4, "y")
    late_pieces[3], wide = tie(late_pieces[3], wide)
    (late,) = kernel_call(join_kernel, [((192, D), BF)], [], 10**9, *late_pieces)
    late_pieces = others([late] * 4, "z")
    late_pieces[3], *wide_pieces = tie(late_pieces[3], *wide_pieces)
    late, all_sums = kernel_call(meet_kernel, [((ROWS, D), BF), ((256, D), BF)], [], 10**9, *late_pieces)
    (wide,) = kernel_call(wide_copies_kernel, [((16, ROWS, D), BF)], [], 2 * 10**9, *wide_pieces)
    late_pieces = others([late] * 4, "x")
    late_pieces, wide = tie(late_pieces, wide)
    late = jnp.stack(late_pieces)
    wide = collect(wide)
    late_own = others([late] * 4, "y")
    grad_image = add_all(scatter_eight(img_keep, tie(img_send, late)[0]))[:IMG_ROWS]
    g_gains, g_mod = kernel_call(
        modulation_kernel, [((3, D), F32), ((1024, 6 * D), F32)], [((6, 1024, D), F32)], 7 * 10**9,
        tie(all_sums, late)[0].reshape(16, 16, D), hbm_outs=1, copies=6,
    )
    late_other = [swap_core(late_own[0])]
    late_own, late_other, g_gains, g_mod, grad_image = tie(late_own, late_other, g_gains, g_mod, grad_image)
    late_other = late_other + [swap_core(item) for item in late_own[1:]]
    g_wo_self, g_wqkv, g_wo_cross, g_wq, g_wkv = kernel_call(
        late_out_kernel,
        [((D, D), F32), ((D, 3 * D), F32), ((D, D), F32), ((D, D), F32), ((384, 2 * D), F32)],
        [], 5 * 10**9, place, *late_own, *late_other, smem=1,
    )
    wide, late_other = tie(wide, late_other)
    g_in, g_out = kernel_call(
        wide_out_kernel, [((D, 2048), F32), ((2048, D), F32)],
        [((D, 2048), F32), ((2048, D), F32)],
        4 * 10**9, place, wide, swap_core(wide), smem=1, hbm_outs=2, copies=8,
    )
    return (
        layer_out[None], grad_tokens[None], grad_image[None], g_mod, g_gains, g_wq, g_wkv, g_wo_cross, g_wqkv,
        g_wo_self, g_in, g_out,
    )


def solution(mesh):
    split = Mesh(mesh.devices.reshape(4, 4, 4, 2), ("x", "z", "y", "core"))
    obj, tok = ("x", "z"), ("y", "core")
    return jax.shard_map(
        local,
        mesh=split,
        in_specs=(
            P(obj, tok, None), P(obj, None), P(obj, tok, None), P(obj, None), P(obj, tok), P(obj, tok),
            P(obj, tok, None),
        )
        + (P(),) * 9,
        out_specs=(P(obj, tok, None),) * 3 + (P(),) * 9,
        check_vma=False,
    )
```

```python
import functools

import jax
import jax.numpy as jnp
from jax import lax
from jax.experimental import pallas as pl
from jax.experimental.pallas import tpu as pltpu
from jax.sharding import Mesh
from jax.sharding import PartitionSpec as P

BF = jnp.bfloat16
F32 = jnp.float32
D = 512
ROWS = 128
IMG_ROWS = 130
IMG_PAD = 144
IMG_KEYS = 8 * IMG_PAD
KEYS = 8 * ROWS
SCALE = 0.125
MIDDLE_OUTS = [
    ((ROWS, D), BF), ((ROWS, D), F32), ((4, ROWS, D), BF), ((4, ROWS, D), BF),
    ((4, 256, D), BF), ((4, 256, D), BF), ((ROWS, 3072), BF), ((ROWS, 3072), BF),
]
CROSS_OUTS = [
    ((4, 272, D), BF), ((4, 272, D), BF), ((4, IMG_PAD, 384), BF), ((4, IMG_PAD, 384), BF), ((ROWS, D), F32),
]
GRAD_OUTS = [
    ((D, 2048), F32), ((2048, D), F32), ((D, D), F32), ((D, 3 * D), F32), ((D, D), F32), ((D, D), F32),
    ((384, 2 * D), F32),
]
CORE_SWAP = [(0, 1), (1, 0)]
VMEM = pl.BlockSpec(memory_space=pltpu.VMEM)
SMEM = pl.BlockSpec(memory_space=pltpu.SMEM)
HBM = pl.BlockSpec(memory_space=pl.ANY)


def nn(left, right):
    return jnp.dot(left, right, preferred_element_type=F32)


def nt(left, right):
    return lax.dot_general(left, right, (((1,), (1,)), ((), ())), preferred_element_type=F32)


def tn(left, right):
    return lax.dot_general(left, right, (((0,), (0,)), ((), ())), preferred_element_type=F32)


def kernel_call(body, outs, scratch, flops, *args, smem=0, hbm=0, hbm_outs=0, copies=0, limit=60, aliases=None):
    in_specs = [SMEM] * smem + [VMEM] * (len(args) - smem - hbm) + [HBM] * hbm
    moved = sum(item.size * item.dtype.itemsize for item in args)
    return pl.pallas_call(
        body,
        out_shape=[jax.ShapeDtypeStruct(shape, dtype) for shape, dtype in outs],
        in_specs=in_specs,
        out_specs=[VMEM] * (len(outs) - hbm_outs) + [HBM] * hbm_outs,
        scratch_shapes=[pltpu.VMEM(shape, dtype) for shape, dtype in scratch]
        + ([pltpu.SemaphoreType.DMA((copies,))] if copies else []),
        input_output_aliases=aliases or {},
        compiler_params=pltpu.CompilerParams(vmem_limit_bytes=limit << 20),
        cost_estimate=pl.CostEstimate(flops=flops, bytes_accessed=moved, transcendentals=0),
    )(*args)


def fetch(pairs, semaphores, first=0):
    copies = [
        pltpu.make_async_copy(source, target, semaphores.at[first + i]) for i, (source, target) in enumerate(pairs)
    ]
    for copy in copies:
        copy.start()
    return copies


def norm_parts(values, gain, scale):
    center = values - jnp.mean(values, axis=-1, keepdims=True)
    rstd = lax.rsqrt(jnp.mean(center * center, axis=-1, keepdims=True) + 1e-05)
    return center * rstd, rstd, gain * (1.0 + scale)


def norm_back(grad, xhat, rstd, slope):
    scaled = grad * slope
    return rstd * (
        scaled
        - jnp.mean(scaled, axis=-1, keepdims=True)
        - xhat * jnp.mean(scaled * xhat, axis=-1, keepdims=True)
    )


def norm_sums(grad, xhat, gain, scale):
    total = jnp.sum(grad * xhat, axis=0, keepdims=True)
    return total * (1.0 + scale), jnp.sum(grad, axis=0, keepdims=True), total * gain


def spread_columns(block):
    head = lax.broadcasted_iota(jnp.int32, block.shape, 0) >> 6
    return jnp.concatenate([jnp.where(head == j, block, 0.0) for j in range(4)], axis=1)


def spread_rows(block):
    head = lax.broadcasted_iota(jnp.int32, block.shape, 1) >> 6
    return jnp.concatenate([jnp.where(head == j, block, 0.0) for j in range(4)], axis=0)


def gather_heads(wide):
    return jnp.concatenate(
        [wide[64 * j : 64 * j + 64, 128 * j : 128 * j + 128] for j in range(4)], axis=0
    )


def fold8(values, reduce):
    rows, width = values.shape
    return reduce(values.reshape(rows // 8, 8, width), axis=0)


def chunked(total):
    return [(start, min(256, total - start)) for start in range(0, total, 256)]


def soften_quad(quad, q_t, keys_ref, probs_ref, score_ref, bias_ref):
    chunks = chunked(keys_ref.shape[0])
    lanes = slice(256 * quad, 256 * quad + 256)
    spread = spread_columns(q_t[lanes, :]).astype(BF)
    top = None
    for start, size in chunks:
        scores = nn(keys_ref[start : start + size, lanes], spread)
        if bias_ref is not None:
            scores = scores + bias_ref[start : start + size, :]
        score_ref[start : start + size, :] = scores
        here = fold8(scores, jnp.max)
        top = here if top is None else jnp.maximum(top, here)
    top = jnp.max(top, axis=0, keepdims=True)
    total = None
    for start, size in chunks:
        weights = jnp.exp(score_ref[start : start + size, :] - top)
        score_ref[start : start + size, :] = weights
        here = fold8(weights, jnp.sum)
        total = here if total is None else total + here
    inverse = 1.0 / jnp.sum(total, axis=0, keepdims=True)
    for start, size in chunks:
        probs_ref[quad, start : start + size, :] = (score_ref[start : start + size, :] * inverse).astype(BF)


def attend(q_t, keys_ref, values_t_ref, probs_ref, score_ref, bias_ref):
    parts = []
    for quad in range(2):
        soften_quad(quad, q_t, keys_ref, probs_ref, score_ref, bias_ref)
        parts.append(gather_heads(nn(values_t_ref[256 * quad : 256 * quad + 256, :], probs_ref[quad])))
    return jnp.concatenate(parts, axis=0)


def attend_back(q_s, grad, grad_t, out_t, keys_ref, values_t_ref, probs_ref, slopes_ref, gk_ref, gv_ref):
    inner = grad_t * out_t
    parts = []
    for quad in range(2):
        lanes = slice(256 * quad, 256 * quad + 256)
        spread = spread_columns(grad_t[lanes, :]).astype(BF)
        delta = jnp.concatenate(
            [
                jnp.sum(inner[256 * quad + 64 * j : 256 * quad + 64 * j + 64, :], axis=0, keepdims=True)
                for j in range(4)
            ],
            axis=1,
        )
        grad_rows = spread_rows(grad[:, lanes]).astype(BF)
        query_rows = spread_rows(q_s[:, lanes]).astype(BF)
        for start, size in chunked(keys_ref.shape[0]):
            span = slice(start, start + size)
            grad_probs = tn(values_t_ref[lanes, span], spread)
            probs = probs_ref[quad, span, :]
            slopes = (probs.astype(F32) * (grad_probs - delta)).astype(BF)
            slopes_ref[span, :] = slopes
            gv_ref[span, lanes] = nn(probs, grad_rows).astype(BF)
            gk_ref[span, lanes] = nn(slopes, query_rows).astype(BF)
        parts.append(gather_heads(tn(keys_ref[:, lanes], slopes_ref[...])))
    return jnp.concatenate(parts, axis=0).T * SCALE


def points_kernel(owner_ref, count_ref, rows_ref, grads_ref, camera_ref, modw_hbm, keep_ref, send_ref, mod_ref, act_ref, modw_ref, sems):
    copies = fetch([(modw_hbm, modw_ref)], sems)
    row_ids = rows_ref[...]
    slot = lax.broadcasted_iota(jnp.int32, row_ids.shape, 1)
    row_ids = jnp.where(slot < count_ref[0], row_ids, -1)
    for block in range(8):
        target = lax.broadcasted_iota(jnp.int32, (ROWS, row_ids.shape[1]), 0) + owner_ref[block] * ROWS
        onehot = jnp.where(target == row_ids, 1.0, 0.0).astype(BF)
        part = nn(onehot, grads_ref[...]).astype(BF)
        out = keep_ref if block < 4 else send_ref
        out[block % 4] = part
    camera = camera_ref[...].astype(F32)
    act = (camera / (1.0 + jnp.exp(-camera))).astype(BF)
    act_ref[...] = act
    copies[0].wait()
    modulation = nn(jnp.broadcast_to(act, (16, act.shape[1])), modw_ref[...])
    for row in range(6):
        mod_ref[row : row + 1, :] = modulation[0:1, D * row : D * row + D]
    mod_ref[6:8, :] = jnp.zeros((2, D), F32)


def stack_image(image_ref, blocks):
    for j, block in enumerate(blocks):
        base = IMG_PAD * j
        image_ref[base + 128 : base + IMG_PAD, :] = jnp.zeros((16, image_ref.shape[1]), BF)
        image_ref[base : base + IMG_ROWS, :] = block[...]


def cross_kernel(
    tokens_ref, mod_ref, gains_ref, bias_ref, i0, i1, i2, i3, i4, i5, i6, i7, wq_hbm, wkv_hbm, wo_hbm,
    after_ref, normed_ref, attended_ref, query_ref,
    image_ref, keys_ref, values_t_ref, score_ref, probs_ref, wq_ref, wkv_ref, wo_ref, sems,
):
    copies = fetch([(wkv_hbm, wkv_ref)], sems)
    stack_image(image_ref, (i0, i1, i2, i3, i4, i5, i6, i7))
    copies[0].wait()
    copies += fetch([(wq_hbm, wq_ref), (wo_hbm, wo_ref)], sems, 1)
    keys_ref[...] = nn(image_ref[...], wkv_ref[:, :D]).astype(BF)
    values_t_ref[...] = nt(wkv_ref[:, D:].T, image_ref[...]).astype(BF)
    mod = mod_ref[...]
    gains = gains_ref[...].astype(F32)
    tokens = tokens_ref[...].astype(F32)
    xhat, _, slope = norm_parts(tokens, gains[0:1], mod[1:2])
    normed = (xhat * slope + mod[0:1]).astype(BF)
    copies[1].wait()
    query = nn(normed, wq_ref[...]).astype(BF)
    query_ref[...] = query
    q_t = query.astype(F32).T * SCALE
    out_t = attend(q_t, keys_ref, values_t_ref, probs_ref, score_ref, bias_ref)
    attended = out_t.T.astype(BF)
    attended_ref[...] = attended
    copies[2].wait()
    after = tokens + nn(attended, wo_ref[...])
    after_ref[...] = after
    xhat, _, slope = norm_parts(after, gains[1:2], mod[3:4])
    normed_ref[...] = (xhat * slope + mod[2:3]).astype(BF)


def cross_rest_kernel(
    query_ref, bias_ref, i0, i1, i2, i3, i4, i5, i6, i7, wkv_hbm,
    keys_hbm, values_t_hbm, image_hbm, probs_hbm,
    wkv_ref, keys_ref, values_t_ref, image_ref, probs_ref, score_ref, sems,
):
    copies = fetch([(wkv_hbm, wkv_ref)], sems)
    stack_image(image_ref, (i0, i1, i2, i3, i4, i5, i6, i7))
    saved = fetch([(image_ref, image_hbm)], sems, 1)
    copies[0].wait()
    keys_ref[...] = nn(image_ref[...], wkv_ref[:, :D]).astype(BF)
    values_t_ref[...] = nt(wkv_ref[:, D:].T, image_ref[...]).astype(BF)
    saved += fetch([(keys_ref, keys_hbm), (values_t_ref, values_t_hbm)], sems, 2)
    q_t = query_ref[...].astype(F32).T * SCALE
    for quad in range(2):
        soften_quad(quad, q_t, keys_ref, probs_ref, score_ref, bias_ref)
        saved += fetch([(probs_ref.at[quad], probs_hbm.at[quad])], sems, 4 + quad)
    for copy in saved:
        copy.wait()


def gelu_parts(value):
    c = 0.7978845608028654
    square = value * value
    bent = jnp.tanh(c * value * (1.0 + 0.044715 * square))
    half = 0.5 * (1.0 + bent)
    slope = half + 0.5 * value * (1.0 - bent * bent) * (c * (1.0 + 3.0 * 0.044715 * square))
    return value * half, slope


def middle_kernel(
    place_ref, mod_ref, gains_ref, n0, n1, n2, n3, n4, n5, n6, n7, c0, c1, c2, c3,
    after_hbm, wqkv_hbm, wo_hbm, w_in_hbm, w_out_hbm,
    sums_ref, out_hbm, grad_hbm, keep_hbm, send_hbm, mid_keep_hbm, mid_send_hbm, pack_keep_hbm, pack_send_hbm,
    out_ref, grad_ref, keep_ref, send_ref, mid_keep_ref, mid_send_ref, pack_keep_ref, pack_send_ref,
    after_ref, wqkv_ref, wo_ref, w_in_ref, w_out_ref, cot_ref,
    all_ref, keys_ref, values_t_ref, probs_ref, score_ref, slopes_ref, gk_ref, gv_ref,
    hidden_ref, inner_ref, attended_ref, query_ref, out_t_ref, gq_ref, sems,
):
    blocks = (n0, n1, n2, n3, n4, n5, n6, n7)
    copies = fetch(
        [(wqkv_hbm, wqkv_ref)]
        + [(block, all_ref.at[ROWS * j : ROWS * j + ROWS]) for j, block in enumerate(blocks)],
        sems,
    )
    saved = []

    def save(*pairs):
        saved.extend(fetch(pairs, sems, 17 + len(saved)))

    y, core = place_ref[2], place_ref[3]
    step = pl.when(core >= 0)
    halves = ((mid_send_ref, 1 - core), (mid_keep_ref, core))
    wq, wk, wv = (pl.ds(D * j, D) for j in range(3))
    for copy in copies:
        copy.wait()
    copies = fetch(
        [(after_hbm, after_ref), (wo_hbm, wo_ref), (w_in_hbm, w_in_ref), (w_out_hbm, w_out_ref)]
        + [(piece, cot_ref.at[j]) for j, piece in enumerate((c0, c1, c2, c3))],
        sems, 9,
    )

    @step
    def _():
        query = nn(all_ref[:ROWS, :], wqkv_ref[:, wq]).astype(BF).astype(F32) * SCALE
        query_ref[...] = query
        keys_ref[...] = nn(all_ref[...], wqkv_ref[:, wk]).astype(BF)
        values_t_ref[...] = nt(wqkv_ref[:, wv].T, all_ref[...]).astype(BF)
        out_t = attend(query.T, keys_ref, values_t_ref, probs_ref, score_ref, None)
        out_t_ref[...] = out_t
        attended_ref[...] = out_t.T.astype(BF)

    for copy in copies:
        copy.wait()

    @step
    def _():
        mod = mod_ref[...]
        gains = gains_ref[...].astype(F32)
        after = after_ref[...] + nn(attended_ref[...], wo_ref[...])
        xhat, rstd, slope = norm_parts(after, gains[2:3], mod[5:6])
        normed = (xhat * slope + mod[4:5]).astype(BF)
        inner = nn(normed, w_in_ref[...])
        value, bend = gelu_parts(inner)
        hidden_ref[...] = value.astype(BF)
        result = after + nn(hidden_ref[...], w_out_ref[...])
        out_ref[...] = result.astype(BF)
        cot = add_all([cot_ref[j] for j in range(4)])
        branch = cot.astype(BF)
        grad_inner = (nt(branch, w_out_ref[...]) * bend).astype(BF)
        inner_ref[...] = grad_inner
        for ref, half in ((pack_send_ref, 1 - core), (pack_keep_ref, core)):
            wide = pl.ds(pl.multiple_of(half * 1024, 1024), 1024)
            ref[:, :D] = normed
            ref[:, D : 2 * D] = branch
            ref[:, 1024:2048] = hidden_ref[:, wide]
            ref[:, 2048:] = inner_ref[:, wide]
        grad = nt(grad_inner, w_in_ref[...])
        sums_ref[...] = jnp.zeros(sums_ref.shape, F32)
        for row, line in enumerate(norm_sums(grad, xhat, gains[2:3], mod[5:6])):
            sums_ref[row : row + 1, :] = line
        grad_ref[...] = cot + norm_back(grad, xhat, rstd, slope)

    save((pack_send_ref, pack_send_hbm), (pack_keep_ref, pack_keep_hbm), (out_ref, out_hbm), (grad_ref, grad_hbm))

    @step
    def _():
        branch = grad_ref[...].astype(BF)
        grad = nt(branch, wo_ref[...]).astype(BF).astype(F32)
        grad_t = nt(wo_ref[...], branch).astype(BF).astype(F32)
        gq_ref[...] = attend_back(
            query_ref[...], grad, grad_t, out_t_ref[...], keys_ref, values_t_ref, probs_ref, slopes_ref, gk_ref,
            gv_ref,
        ).astype(BF)
        for ref, half in halves:
            narrow = pl.ds(pl.multiple_of(half * 256, 256), 256)
            ref[y] = tn(attended_ref[:, narrow], branch).astype(BF)
            ref[1 ^ y] = tn(all_ref[:ROWS, narrow], gq_ref[...]).astype(BF)
            ref[2 ^ y] = tn(all_ref[:, narrow], gk_ref[...]).astype(BF)
            ref[3 ^ y] = tn(all_ref[:, narrow], gv_ref[...]).astype(BF)

    save((mid_send_ref, mid_send_hbm), (mid_keep_ref, mid_keep_hbm))

    @step
    def _():
        part = nt(gk_ref[512:, :], wqkv_ref[:, wk]) + nt(gv_ref[512:, :], wqkv_ref[:, wv])
        send_ref[...] = part.astype(BF).reshape(4, ROWS, D)

    save((send_ref, send_hbm))

    @step
    def _():
        part = nt(gk_ref[:512, :], wqkv_ref[:, wk]) + nt(gv_ref[:512, :], wqkv_ref[:, wv])
        keep_ref[0] = (part[:ROWS] + nt(gq_ref[...], wqkv_ref[:, wq])).astype(BF)
        keep_ref[1:] = part[ROWS:].astype(BF).reshape(3, ROWS, D)

    save((keep_ref, keep_hbm))
    for copy in saved:
        copy.wait()


def wide_kernel(own_hbm, got_hbm, out_hbm, rows_ref, out_ref, sems):
    for copy in fetch([(own_hbm, rows_ref.at[:ROWS]), (got_hbm, rows_ref.at[ROWS:])], sems):
        copy.wait()
    out_ref[:1024, :] = tn(rows_ref[:, 1024:2048], rows_ref[:, D : 2 * D]).astype(BF)
    saved = fetch([(out_ref.at[:1024], out_hbm.at[:1024])], sems, 2)
    for j in range(2):
        part = tn(rows_ref[:, :D], rows_ref[:, 2048 + D * j : 2560 + D * j])
        rows = slice(1024 + D * j, 1536 + D * j)
        out_ref[rows, :] = part.astype(BF)
        saved += fetch([(out_ref.at[rows], out_hbm.at[rows])], sems, 3 + j)
    for copy in saved:
        copy.wait()


def cross_back_kernel(
    place_ref, mod_ref, gains_ref, sums_in_ref, act_ref, g0, g1, g2, g3,
    after_hbm, wo_hbm, grad_hbm, attended_hbm, values_t_hbm, probs_hbm, keys_hbm, query_hbm, tokens_hbm, wq_hbm,
    image_hbm, wkv_hbm,
    last_keep_hbm, last_send_hbm, keep_hbm, send_hbm, tokens_out_hbm,
    last_keep_ref, last_send_ref, keep_ref, send_ref, tokens_out_ref,
    g_ref, after_ref, wo_ref, grad_ref, attended_ref, values_t_ref, probs_ref, keys_ref, query_ref, tokens_ref,
    wq_ref, image_ref, wkv_ref, sums_ref, slopes_ref, kv_ref, normed_ref, sems,
):
    early = fetch(
        [(piece, g_ref.at[j]) for j, piece in enumerate((g0, g1, g2, g3))]
        + [
            (after_hbm, after_ref), (wo_hbm, wo_ref), (grad_hbm, grad_ref), (attended_hbm, attended_ref),
            (query_hbm, query_ref),
        ],
        sems,
    )
    copies = fetch(
        [
            (values_t_hbm, values_t_ref), (probs_hbm, probs_ref), (keys_hbm, keys_ref), (tokens_hbm, tokens_ref),
            (wq_hbm, wq_ref), (image_hbm, image_ref), (wkv_hbm, wkv_ref),
        ],
        sems, 9,
    )
    saved = []

    def save(*pairs):
        saved.extend(fetch(pairs, sems, 16 + len(saved)))

    y, core = place_ref[2], place_ref[3]
    halves = ((last_send_ref, 1 - core), (last_keep_ref, core))
    for copy in early:
        copy.wait()

    mod = mod_ref[...]
    gains = gains_ref[...].astype(F32)
    incoming = add_all([g_ref[j] for j in range(4)])
    xhat, rstd, slope = norm_parts(after_ref[...], gains[1:2], mod[3:4])
    sums_ref[...] = sums_in_ref[...]
    for row, line in enumerate(norm_sums(incoming, xhat, gains[1:2], mod[3:4])):
        sums_ref[3 + row : 4 + row, :] = line
    grad_ref[...] += norm_back(incoming, xhat, rstd, slope)
    branch = grad_ref[...].astype(BF)
    for ref, half in halves:
        narrow = pl.ds(pl.multiple_of(half * 256, 256), 256)
        ref[y, :256, :] = tn(attended_ref[:, narrow], branch).astype(BF)

    for copy in copies[:3]:
        copy.wait()
    grad = nt(branch, wo_ref[...]).astype(BF).astype(F32)
    grad_t = nt(wo_ref[...], branch).astype(BF).astype(F32)
    out_t = attended_ref[...].astype(F32).T
    query = query_ref[...].astype(F32) * SCALE
    gq = attend_back(
        query, grad, grad_t, out_t, keys_ref, values_t_ref, probs_ref, slopes_ref, kv_ref.at[0], kv_ref.at[1],
    ).astype(BF)
    for copy in copies[3:]:
        copy.wait()
    tokens = tokens_ref[...].astype(F32)
    xhat, rstd, slope = norm_parts(tokens, gains[0:1], mod[1:2])
    normed_ref[...] = (xhat * slope + mod[0:1]).astype(BF)
    incoming = nt(gq, wq_ref[...])
    for row, line in enumerate(norm_sums(incoming, xhat, gains[0:1], mod[1:2])):
        sums_ref[6 + row : 7 + row, :] = line
    tokens_out_ref[...] = grad_ref[...] + norm_back(incoming, xhat, rstd, slope)
    act = act_ref[...].astype(F32)
    sums_ref[9:10, :] = act[:, :D]
    sums_ref[10:11, :] = act[:, D:]
    sums = sums_ref[...].astype(BF)
    for ref, half in halves:
        narrow = pl.ds(pl.multiple_of(half * 256, 256), 256)
        ref[1 ^ y, :256, :] = tn(normed_ref[:, narrow], gq).astype(BF)
        part = tn(image_ref[...], kv_ref[half]).astype(BF)
        for side in range(2):
            ref[(2 + side) ^ y, :192, :] = part[192 * side : 192 * side + 192, :]
            ref[(2 + side) ^ y, 192:256, :] = jnp.zeros((64, D), BF)
        for j in range(4):
            ref[j, 256:, :] = sums

    save((last_send_ref, last_send_hbm), (last_keep_ref, last_keep_hbm), (tokens_out_ref, tokens_out_hbm))

    wk, wv = wkv_ref[:, :D], wkv_ref[:, D:]
    half_keys = IMG_KEYS // 2
    for ref, base in ((keep_ref, 0), (send_ref, half_keys)):
        span = slice(base, base + half_keys)
        part = nt(kv_ref[0, span, :], wk) + nt(kv_ref[1, span, :], wv)
        ref[...] = part.astype(BF).reshape(4, IMG_PAD, 384)

    save((keep_ref, keep_hbm), (send_ref, send_hbm))
    for copy in saved:
        copy.wait()


def fold_kernel(place_ref, m0, m1, m2, m3, l0, l1, l2, l3, t0, t1, t2, t3, total_ref):
    total_ref[:, :64, :] = add_all([m0[...], m1[...], m2[...], m3[...]]).astype(BF).reshape(4, 64, D)
    late = add_all([l0[...], l1[...], l2[...], l3[...]]).astype(BF)
    total_ref[:, 64:, :] = late[:256].reshape(4, 64, D)
    for j, ref in enumerate((t0, t1, t2, t3)):
        ref[:ROWS, :] = total_ref[place_ref[0] ^ j]
        ref[ROWS:, :] = late[256:]


def join_kernel(a_ref, b_ref, c_ref, d_ref, out_ref):
    refs = (a_ref, b_ref, c_ref, d_ref)
    out_ref[:ROWS, :] = add_all([ref[:ROWS, :] for ref in refs]).astype(BF)
    for j, ref in enumerate(refs):
        out_ref[ROWS + 16 * j : ROWS + 16 * j + 16, :] = ref[ROWS:, :]


def meet_kernel(a_ref, b_ref, c_ref, d_ref, out_ref, sums_ref):
    refs = (a_ref, b_ref, c_ref, d_ref)
    out_ref[...] = add_all([ref[:ROWS, :] for ref in refs]).astype(BF)
    for j, ref in enumerate(refs):
        sums_ref[64 * j : 64 * j + 64, :] = ref[ROWS:, :]


def wide_sum_kernel(parts_ref, copies_ref):
    total = jnp.sum(parts_ref[...].astype(F32), axis=0).astype(BF)
    for j in range(4):
        copies_ref[j] = total


def wide_copies_kernel(parts_ref, copies_ref):
    total = jnp.sum(parts_ref[...].astype(F32), axis=0).astype(BF)
    for j in range(16):
        copies_ref[j] = total


def modulation_kernel(sums_in_ref, a_ref, b_ref, c_ref, d_ref, gains_ref, image_ref, modw_hbm, modw_ref, sems):
    sums = sums_in_ref[...].astype(F32)
    acts = (jnp.concatenate([sums[:, 9, :], sums[:, 10, :]], axis=1) * 0.125).astype(BF)
    copies = []
    for norm in range(3):
        first = 3 * (2 - norm)
        gains_ref[norm : norm + 1, :] = jnp.sum(sums[:, first, :], axis=0, keepdims=True)
        for kind in range(2):
            part = 2 * norm + kind
            modw_ref[part] = tn(acts, sums[:, first + 1 + kind, :].astype(BF))
            target = modw_hbm.at[:, D * part : D * part + D]
            copies += fetch([(modw_ref.at[part], target)], sems, len(copies))
    image_ref[...] = add_all([a_ref[...], b_ref[...], c_ref[...], d_ref[...]])[:IMG_ROWS]
    for copy in copies:
        copy.wait()


def out_kernel(side, place_ref, wide_hbm, p0, p1, p2, p3, *refs):
    targets, refs = (refs[:7], refs[7:]) if side == 0 else (refs[7:14], refs[14:])
    w_in_ref, w_out_ref, wo_self_ref, wqkv_ref, wo_ref, wq_ref, wkv_ref, wide_ref, late_ref, sems = refs
    w_in_hbm, w_out_hbm, wo_self_hbm, wqkv_hbm, wo_hbm, wq_hbm, wkv_hbm = targets
    x, y, core = place_ref[0], place_ref[2], place_ref[3]
    step = pl.when(core >= 0)
    half = core ^ side
    wide_in = fetch([(wide_hbm.at[8 * j : 8 * j + 8], wide_ref.at[8 * j : 8 * j + 8]) for j in range(2)], sems)
    late_in = fetch([(piece, late_ref.at[j]) for j, piece in enumerate((p0, p1, p2, p3))], sems, 2)
    saved = []

    def save(*pairs):
        saved.extend(fetch(pairs, sems, 6 + len(saved)))

    wide_rows = pl.ds(pl.multiple_of(half * 1024, 1024), 1024)
    rows = pl.ds(pl.multiple_of(half * 256, 256), 256)
    columns = pl.ds(pl.multiple_of(half * D, D), D)
    wide_in[0].wait()

    @step
    def _():
        w_out_ref[...] = wide_ref[:8].reshape(1024, D).astype(F32)

    save((w_out_ref, w_out_hbm.at[wide_rows]))
    wide_in[1].wait()

    @step
    def _():
        for j in range(2):
            w_in_ref[:, D * j : D * j + D] = wide_ref[8 + 4 * j : 12 + 4 * j].reshape(D, D).astype(F32)

    save((w_in_ref, w_in_hbm.at[:, wide_rows]))
    for copy in late_in:
        copy.wait()

    @step
    def _():
        for piece in range(4):
            block = y ^ piece
            for across in range(4):
                strip = x ^ across
                strip_rows = pl.ds(pl.multiple_of(strip * 64, 64), 64)
                early = late_ref[piece, across, :64, :].astype(F32)
                late = late_ref[piece, across, 64:, :].astype(F32)

                @pl.when(block == 0)
                def _():
                    wo_self_ref[strip_rows, :] = early
                    wo_ref[strip_rows, :] = late

                @pl.when(block > 0)
                def _():
                    wqkv_ref[strip_rows, pl.ds(pl.multiple_of((block - 1) * D, D), D)] = early

                @pl.when(block == 1)
                def _():
                    wq_ref[strip_rows, :] = late

                @pl.when((block > 1) & (strip < 3))
                def _():
                    start = pl.multiple_of((block - 2) * 192 + strip * 64, 64)
                    wkv_ref[pl.ds(start, 64), :] = late

    save(
        (wo_self_ref, wo_self_hbm.at[rows]), (wqkv_ref, wqkv_hbm.at[rows]), (wo_ref, wo_hbm.at[rows]),
        (wq_ref, wq_hbm.at[rows]), (wkv_ref, wkv_hbm.at[:, columns]),
    )
    for copy in saved:
        copy.wait()


def tie(*values):
    return lax.optimization_barrier(values)


def swap_core(value):
    return lax.ppermute(value, "core", CORE_SWAP)


def swap(value, axis, step):
    return lax.ppermute(value, axis, [(i, i ^ step) for i in range(4)])


def swap_y(value, step):
    return swap(value, "y", step)


def gather_eight(value):
    across = [value] + [swap_y(value, step) for step in (1, 2, 3)]
    return across + [swap_core(item) for item in across]


def scatter_eight(keep, send):
    return others(halve(keep, send), "y")


def add_all(items):
    total = items[0].astype(F32)
    for item in items[1:]:
        total = total + item.astype(F32)
    return total


def halve(keep, send):
    got = swap_core(send)
    return [(keep[j].astype(F32) + got[j].astype(F32)).astype(BF) for j in range(4)]


def spread(mixed):
    rows, width = mixed.shape
    return lax.all_to_all(mixed, ("x", "z"), 0, 0, tiled=True).reshape(16, rows // 16, width)


def collect(copies):
    return lax.all_to_all(copies, ("x", "z"), 0, 0, tiled=True)


def others(pieces, axis):
    return [pieces[0]] + [swap(pieces[step], axis, step) for step in (1, 2, 3)]


def gather_axis(value, axis):
    return jnp.stack(others([value] * 4, axis))


def local(
    tokens, camera, image, image_mask, point_rows, point_count, point_grads, mod_weight, norm_gains,
    wq_cross, wkv_cross, wo_cross, wqkv_self, wo_self, w_in, w_out,
):
    place = [lax.axis_index(axis).astype(jnp.int32) for axis in ("x", "z", "y", "core")]
    y, core = place[2:]
    place = jnp.stack(place)
    owners = jnp.stack([2 * (y ^ (j % 4)) + (core ^ (j // 4)) for j in range(8)]).astype(jnp.int32)
    toks = tokens[0]

    image_blocks = gather_eight(image[0])

    bias = jnp.where(image_mask[0] > 0, 0.0, -1e30).astype(F32).reshape(2, 2, 2, IMG_ROWS)
    for axis, bit in ((0, y & 2), (1, y & 1), (2, core)):
        bias = jnp.where(bit != 0, jnp.flip(bias, axis), bias)
    bias = jnp.pad(bias.transpose(2, 0, 1, 3), ((0, 0),) * 3 + ((0, IMG_PAD - IMG_ROWS),), constant_values=-1e30)
    bias = bias.reshape(IMG_KEYS, 1)

    cot_keep, cot_send, mod, act = kernel_call(
        points_kernel,
        [((4, ROWS, D), BF), ((4, ROWS, D), BF), ((8, D), F32), ((1, 1024), BF)],
        [((1024, 6 * D), BF)], 6 * 10**9,
        owners, point_count[0], point_rows, point_grads[0], camera, mod_weight, smem=2, hbm=1, copies=1,
    )
    cot_parts = scatter_eight(cot_keep, cot_send)

    after_cross, normed_two, attended_one, query_one = kernel_call(
        cross_kernel,
        [((ROWS, D), F32), ((ROWS, D), BF), ((ROWS, D), BF), ((ROWS, D), BF)],
        [
            ((IMG_KEYS, 384), BF), ((IMG_KEYS, D), BF), ((D, IMG_KEYS), BF), ((IMG_KEYS, 512), F32),
            ((2, IMG_KEYS, 512), BF), ((D, D), BF), ((384, 2 * D), BF), ((D, D), BF),
        ],
        10 * 10**9,
        toks, mod, norm_gains, bias, *image_blocks, wq_cross, wkv_cross, wo_cross, hbm=3, copies=3,
    )

    normed_two, *cot_parts = tie(normed_two, *cot_parts)
    across = others([normed_two] * 4, "y")
    keys_one, values_t_one, image_all, probs_one = kernel_call(
        cross_rest_kernel,
        [((IMG_KEYS, D), BF), ((D, IMG_KEYS), BF), ((IMG_KEYS, 384), BF), ((2, IMG_KEYS, 512), BF)],
        [
            ((384, 2 * D), BF), ((IMG_KEYS, D), BF), ((D, IMG_KEYS), BF), ((IMG_KEYS, 384), BF),
            ((2, IMG_KEYS, 512), BF), ((IMG_KEYS, 512), F32),
        ],
        7 * 10**9, tie(query_one, normed_two)[0], bias, *image_blocks, wkv_cross, hbm=1, hbm_outs=4, copies=6,
    )
    keys_one, values_t_one, image_all, probs_one, *across = tie(keys_one, values_t_one, image_all, probs_one, *across)
    normed_blocks = across + [swap_core(item) for item in across]
    (
        sums, layer_out, grad_after_self, back_keep, back_send, mid_keep, mid_send, pack_keep, pack_send,
    ) = kernel_call(
        middle_kernel,
        [((16, D), F32)] + MIDDLE_OUTS,
        MIDDLE_OUTS
        + [
            ((ROWS, D), F32), ((D, 3 * D), BF), ((D, D), BF), ((D, 2048), BF), ((2048, D), BF), ((4, ROWS, D), BF),
            ((KEYS, D), BF), ((KEYS, D), BF), ((D, KEYS), BF),
            ((2, KEYS, 512), BF), ((KEYS, 512), F32), ((KEYS, 512), BF), ((KEYS, D), BF), ((KEYS, D), BF),
            ((ROWS, 2048), BF), ((ROWS, 2048), BF), ((ROWS, D), BF), ((ROWS, D), F32), ((D, ROWS), F32),
            ((ROWS, D), BF),
        ],
        20 * 10**9,
        place, mod, norm_gains, *normed_blocks, *cot_parts, after_cross, wqkv_self, wo_self, w_in, w_out,
        smem=1, hbm=17, hbm_outs=8, copies=25,
    )

    back_parts = halve(back_keep, back_send)
    pack_send, mid_send, *back_parts = tie(pack_send, mid_send, *back_parts)
    pack_got = swap_core(pack_send)
    mid_got = swap_core(mid_send)
    back_parts = others(back_parts, "y")
    (wide_mixed,) = kernel_call(
        wide_kernel, [((2048, D), BF)], [((256, 3072), BF), ((2048, D), BF)], 3 * 10**9, pack_keep, pack_got,
        hbm=2, hbm_outs=1, copies=5,
    )
    mid_pieces = [(mid_keep[j].astype(F32) + mid_got[j].astype(F32)).astype(BF) for j in range(4)]
    wide_mixed, *pieces = tie(wide_mixed, *back_parts, *mid_pieces)
    back_parts, mid_pieces = pieces[:4], pieces[4:]
    wide_parts = spread(wide_mixed)
    mid_pieces = others(mid_pieces, "y")

    last_keep, last_send, img_keep, img_send, grad_tokens = kernel_call(
        cross_back_kernel,
        CROSS_OUTS,
        CROSS_OUTS
        + [
            ((4, ROWS, D), BF), ((ROWS, D), F32), ((D, D), BF), ((ROWS, D), F32), ((ROWS, D), BF), ((D, IMG_KEYS), BF),
            ((2, IMG_KEYS, 512), BF), ((IMG_KEYS, D), BF), ((ROWS, D), BF), ((ROWS, D), BF), ((D, D), BF),
            ((IMG_KEYS, 384), BF), ((384, 2 * D), BF), ((16, D), F32), ((IMG_KEYS, 512), BF), ((2, IMG_KEYS, D), BF),
            ((ROWS, D), BF),
        ],
        11 * 10**9,
        place, mod, norm_gains, sums, act, *back_parts, after_cross, wo_cross, grad_after_self, attended_one,
        values_t_one, probs_one, keys_one, query_one, toks, wq_cross, image_all, wkv_cross,
        smem=1, hbm=16, hbm_outs=5, copies=22,
    )
    last_send, img_send, *mid_pieces = tie(last_send, img_send, *mid_pieces)
    last_pieces = others(halve(last_keep, last_send), "y")
    img_mixed = halve(img_keep, img_send)
    (wide,) = kernel_call(wide_sum_kernel, [((4, ROWS, D), BF)], [], 2 * 10**9, wide_parts)
    *last_pieces, wide, img_mixed = tie(*last_pieces, wide, img_mixed)
    late_pieces = kernel_call(
        fold_kernel, [((144, D), BF)] * 4, [((4, ROWS, D), BF)], 2 * 10**9, place, *mid_pieces, *last_pieces, smem=1
    )
    late_pieces = others(late_pieces, "x")
    late_pieces[1], wide = tie(late_pieces[1], wide)
    wide = lax.all_to_all(wide, "y", 0, 0, tiled=True)
    (late,) = kernel_call(join_kernel, [((192, D), BF)], [], 10**9, *late_pieces)
    late, *img_mixed = tie(late, *img_mixed)
    late_pieces = others([late] * 4, "z")
    img_pieces = others(img_mixed, "y")
    *late_pieces, wide = tie(*late_pieces, wide)
    late, all_sums = kernel_call(meet_kernel, [((ROWS, D), BF), ((256, D), BF)], [], 10**9, *late_pieces)
    late_pieces = others([late] * 4, "x")
    (wide,) = kernel_call(wide_copies_kernel, [((16, ROWS, D), BF)], [], 2 * 10**9, wide)
    pieces = tie(*late_pieces, wide, *img_pieces)
    late_pieces, wide, img_pieces = pieces[:4], pieces[4], pieces[5:]
    late = jnp.stack(late_pieces)
    wide = collect(wide)
    late_own = others([late] * 4, "y")
    g_gains, grad_image, g_mod = kernel_call(
        modulation_kernel, [((3, D), F32), ((IMG_ROWS, 384), F32), ((1024, 6 * D), F32)], [((6, 1024, D), F32)],
        7 * 10**9, tie(all_sums, late)[0].reshape(16, 16, D), *img_pieces, hbm_outs=1, copies=6,
    )
    late_other = [swap_core(late_own[0])]
    late_own, late_other, g_gains, g_mod, wide = tie(late_own, late_other, g_gains, g_mod, wide)
    late_other = late_other + [swap_core(item) for item in late_own[1:]]
    halves = [
        ((D, 1024), F32), ((1024, D), F32), ((256, D), F32), ((256, 3 * D), F32), ((256, D), F32), ((256, D), F32),
        ((384, D), F32), ((16, ROWS, D), BF), ((4, 4, ROWS, D), BF),
    ]
    wide_other = swap_core(wide)
    grads = kernel_call(
        functools.partial(out_kernel, 0), GRAD_OUTS, halves, 4 * 10**9, place, wide, *late_own,
        smem=1, hbm=5, hbm_outs=7, copies=13,
    )
    g_in, g_out, g_wo_self, g_wqkv, g_wo_cross, g_wq, g_wkv = kernel_call(
        functools.partial(out_kernel, 1), GRAD_OUTS, halves, 4 * 10**9, place, wide_other, *late_other, *grads,
        smem=1, hbm=12, hbm_outs=7, copies=13, aliases={6 + j: j for j in range(7)},
    )
    return (
        layer_out[None], grad_tokens[None], grad_image[None], g_mod, g_gains, g_wq, g_wkv, g_wo_cross, g_wqkv,
        g_wo_self, g_in, g_out,
    )


def solution(mesh):
    split = Mesh(mesh.devices.reshape(4, 4, 4, 2), ("x", "z", "y", "core"))
    obj, tok = ("x", "z"), ("y", "core")
    return jax.shard_map(
        local,
        mesh=split,
        in_specs=(
            P(obj, tok, None), P(obj, None), P(obj, tok, None), P(obj, None), P(obj, tok), P(obj, tok),
            P(obj, tok, None),
        )
        + (P(),) * 9,
        out_specs=(P(obj, tok, None),) * 3 + (P(),) * 9,
        check_vma=False,
    )
```

```python
import functools

import jax
import jax.numpy as jnp
from jax import lax
from jax.experimental import pallas as pl
from jax.experimental.pallas import tpu as pltpu
from jax.sharding import Mesh
from jax.sharding import PartitionSpec as P

BF = jnp.bfloat16
F32 = jnp.float32
D = 512
ROWS = 128
IMG_ROWS = 130
IMG_PAD = 144
IMG_KEYS = 8 * IMG_PAD
KEYS = 8 * ROWS
SCALE = 0.125
MIDDLE_OUTS = [
    ((ROWS, D), BF), ((ROWS, D), F32), ((4, ROWS, D), BF), ((4, ROWS, D), BF),
    ((4, 256, D), BF), ((4, 256, D), BF), ((ROWS, 3072), BF), ((ROWS, 3072), BF),
]
CROSS_OUTS = [
    ((4, 272, D), BF), ((4, 272, D), BF), ((4, IMG_PAD, 384), BF), ((4, IMG_PAD, 384), BF), ((ROWS, D), F32),
]
GRAD_OUTS = [
    ((D, 2048), F32), ((2048, D), F32), ((D, D), F32), ((D, 3 * D), F32), ((D, D), F32), ((D, D), F32),
    ((384, 2 * D), F32),
]
CORE_SWAP = [(0, 1), (1, 0)]
VMEM = pl.BlockSpec(memory_space=pltpu.VMEM)
SMEM = pl.BlockSpec(memory_space=pltpu.SMEM)
HBM = pl.BlockSpec(memory_space=pl.ANY)


def nn(left, right):
    return jnp.dot(left, right, preferred_element_type=F32)


def nt(left, right):
    return lax.dot_general(left, right, (((1,), (1,)), ((), ())), preferred_element_type=F32)


def tn(left, right):
    return lax.dot_general(left, right, (((0,), (0,)), ((), ())), preferred_element_type=F32)


def kernel_call(body, outs, scratch, flops, *args, smem=0, hbm=0, hbm_outs=0, copies=0, limit=60, aliases=None):
    in_specs = [SMEM] * smem + [VMEM] * (len(args) - smem - hbm) + [HBM] * hbm
    moved = sum(item.size * item.dtype.itemsize for item in args)
    return pl.pallas_call(
        body,
        out_shape=[jax.ShapeDtypeStruct(shape, dtype) for shape, dtype in outs],
        in_specs=in_specs,
        out_specs=[VMEM] * (len(outs) - hbm_outs) + [HBM] * hbm_outs,
        scratch_shapes=[pltpu.VMEM(shape, dtype) for shape, dtype in scratch]
        + ([pltpu.SemaphoreType.DMA((copies,))] if copies else []),
        input_output_aliases=aliases or {},
        compiler_params=pltpu.CompilerParams(vmem_limit_bytes=limit << 20),
        cost_estimate=pl.CostEstimate(flops=flops, bytes_accessed=moved, transcendentals=0),
    )(*args)


def fetch(pairs, semaphores, first=0):
    copies = [
        pltpu.make_async_copy(source, target, semaphores.at[first + i]) for i, (source, target) in enumerate(pairs)
    ]
    for copy in copies:
        copy.start()
    return copies


def norm_parts(values, gain, scale):
    center = values - jnp.mean(values, axis=-1, keepdims=True)
    rstd = lax.rsqrt(jnp.mean(center * center, axis=-1, keepdims=True) + 1e-05)
    return center * rstd, rstd, gain * (1.0 + scale)


def norm_back(grad, xhat, rstd, slope):
    scaled = grad * slope
    return rstd * (
        scaled
        - jnp.mean(scaled, axis=-1, keepdims=True)
        - xhat * jnp.mean(scaled * xhat, axis=-1, keepdims=True)
    )


def norm_sums(grad, xhat, gain, scale):
    total = jnp.sum(grad * xhat, axis=0, keepdims=True)
    return total * (1.0 + scale), jnp.sum(grad, axis=0, keepdims=True), total * gain


def spread_columns(block):
    head = lax.broadcasted_iota(jnp.int32, block.shape, 0) >> 6
    return jnp.concatenate([jnp.where(head == j, block, 0.0) for j in range(4)], axis=1)


def spread_rows(block):
    head = lax.broadcasted_iota(jnp.int32, block.shape, 1) >> 6
    return jnp.concatenate([jnp.where(head == j, block, 0.0) for j in range(4)], axis=0)


def gather_heads(wide):
    return jnp.concatenate(
        [wide[64 * j : 64 * j + 64, 128 * j : 128 * j + 128] for j in range(4)], axis=0
    )


def fold8(values, reduce):
    rows, width = values.shape
    return reduce(values.reshape(rows // 8, 8, width), axis=0)


def chunked(total):
    return [(start, min(256, total - start)) for start in range(0, total, 256)]


def soften_quad(quad, q_t, keys_ref, probs_ref, score_ref, bias_ref):
    chunks = chunked(keys_ref.shape[0])
    lanes = slice(256 * quad, 256 * quad + 256)
    spread = spread_columns(q_t[lanes, :]).astype(BF)
    top = None
    for start, size in chunks:
        scores = nn(keys_ref[start : start + size, lanes], spread)
        if bias_ref is not None:
            scores = scores + jnp.concatenate([bias_ref[start : start + size, :]] * 4, axis=1)
        score_ref[start : start + size, :] = scores
        here = fold8(scores, jnp.max)
        top = here if top is None else jnp.maximum(top, here)
    top = jnp.max(top, axis=0, keepdims=True)
    total = None
    for start, size in chunks:
        weights = jnp.exp(score_ref[start : start + size, :] - top)
        score_ref[start : start + size, :] = weights
        here = fold8(weights, jnp.sum)
        total = here if total is None else total + here
    inverse = 1.0 / jnp.sum(total, axis=0, keepdims=True)
    for start, size in chunks:
        probs_ref[quad, start : start + size, :] = (score_ref[start : start + size, :] * inverse).astype(BF)


def attend(q_t, keys_ref, values_t_ref, probs_ref, score_ref, bias_ref):
    parts = []
    for quad in range(2):
        soften_quad(quad, q_t, keys_ref, probs_ref, score_ref, bias_ref)
        parts.append(gather_heads(nn(values_t_ref[256 * quad : 256 * quad + 256, :], probs_ref[quad])))
    return jnp.concatenate(parts, axis=0)


def attend_back(q_s, grad, grad_t, out_t, keys_ref, values_t_ref, probs_ref, slopes_ref, gk_ref, gv_ref):
    inner = grad_t * out_t
    parts = []
    for quad in range(2):
        lanes = slice(256 * quad, 256 * quad + 256)
        spread = spread_columns(grad_t[lanes, :]).astype(BF)
        delta = jnp.concatenate(
            [
                jnp.sum(inner[256 * quad + 64 * j : 256 * quad + 64 * j + 64, :], axis=0, keepdims=True)
                for j in range(4)
            ],
            axis=1,
        )
        grad_rows = spread_rows(grad[:, lanes]).astype(BF)
        query_rows = spread_rows(q_s[:, lanes]).astype(BF)
        for start, size in chunked(keys_ref.shape[0]):
            span = slice(start, start + size)
            grad_probs = tn(values_t_ref[lanes, span], spread)
            probs = probs_ref[quad, span, :]
            slopes = (probs.astype(F32) * (grad_probs - delta)).astype(BF)
            slopes_ref[span, :] = slopes
            gv_ref[span, lanes] = nn(probs, grad_rows).astype(BF)
            gk_ref[span, lanes] = nn(slopes, query_rows).astype(BF)
        parts.append(gather_heads(tn(keys_ref[:, lanes], slopes_ref[...])))
    return jnp.concatenate(parts, axis=0).T * SCALE


def points_kernel(place_ref, count_ref, rows_ref, grads_ref, camera_ref, modw_hbm, keep_ref, send_ref, mod_ref, act_ref, modw_ref, sems):
    copies = fetch([(modw_hbm, modw_ref)], sems)
    row_ids = rows_ref[...]
    slot = lax.broadcasted_iota(jnp.int32, row_ids.shape, 1)
    row_ids = jnp.where(slot < count_ref[0], row_ids, -1)
    for block in range(8):
        target = lax.broadcasted_iota(jnp.int32, (ROWS, row_ids.shape[1]), 0) + place_ref[4 + block] * ROWS
        onehot = jnp.where(target == row_ids, 1.0, 0.0).astype(BF)
        part = nn(onehot, grads_ref[...]).astype(BF)
        out = keep_ref if block < 4 else send_ref
        out[block % 4] = part
    camera = camera_ref[...].astype(F32)
    act = (camera / (1.0 + jnp.exp(-camera))).astype(BF)
    act_ref[...] = act
    copies[0].wait()
    modulation = nn(jnp.broadcast_to(act, (16, act.shape[1])), modw_ref[...])
    for row in range(6):
        mod_ref[row : row + 1, :] = modulation[0:1, D * row : D * row + D]
    mod_ref[6:8, :] = jnp.zeros((2, D), F32)


def stack_image(image_ref, blocks):
    for j, block in enumerate(blocks):
        base = IMG_PAD * j
        image_ref[base + 128 : base + IMG_PAD, :] = jnp.zeros((16, image_ref.shape[1]), BF)
        image_ref[base : base + IMG_ROWS, :] = block[...]


def mask_columns(mask_ref, bias_ref):
    row = lax.broadcasted_iota(jnp.int32, (16, IMG_KEYS), 0)
    padded = jnp.where(row == 0, mask_ref[...].astype(F32), 0.0).astype(BF)
    kept = tn(padded, jnp.ones((16, 128), BF))
    bias_ref[...] = jnp.where(kept > 0.5, 0.0, -1e30)


def cross_kernel(
    tokens_ref, mod_ref, gains_ref, mask_ref, i0, i1, i2, i3, i4, i5, i6, i7, wq_hbm, wkv_hbm, wo_hbm,
    after_ref, normed_ref, attended_ref, query_ref,
    image_ref, keys_ref, values_t_ref, score_ref, probs_ref, wq_ref, wkv_ref, wo_ref, bias_ref, sems,
):
    copies = fetch([(wkv_hbm, wkv_ref)], sems)
    mask_columns(mask_ref, bias_ref)
    stack_image(image_ref, (i0, i1, i2, i3, i4, i5, i6, i7))
    copies[0].wait()
    copies += fetch([(wq_hbm, wq_ref), (wo_hbm, wo_ref)], sems, 1)
    keys_ref[...] = nn(image_ref[...], wkv_ref[:, :D]).astype(BF)
    values_t_ref[...] = nt(wkv_ref[:, D:].T, image_ref[...]).astype(BF)
    mod = mod_ref[...]
    gains = gains_ref[...].astype(F32)
    tokens = tokens_ref[...].astype(F32)
    xhat, _, slope = norm_parts(tokens, gains[0:1], mod[1:2])
    normed = (xhat * slope + mod[0:1]).astype(BF)
    copies[1].wait()
    query = nn(normed, wq_ref[...]).astype(BF)
    query_ref[...] = query
    q_t = query.astype(F32).T * SCALE
    out_t = attend(q_t, keys_ref, values_t_ref, probs_ref, score_ref, bias_ref)
    attended = out_t.T.astype(BF)
    attended_ref[...] = attended
    copies[2].wait()
    after = tokens + nn(attended, wo_ref[...])
    after_ref[...] = after
    xhat, _, slope = norm_parts(after, gains[1:2], mod[3:4])
    normed_ref[...] = (xhat * slope + mod[2:3]).astype(BF)


def cross_rest_kernel(
    query_ref, mask_ref, i0, i1, i2, i3, i4, i5, i6, i7, wkv_hbm,
    keys_hbm, values_t_hbm, image_hbm, probs_hbm,
    wkv_ref, keys_ref, values_t_ref, image_ref, probs_ref, score_ref, bias_ref, sems,
):
    copies = fetch([(wkv_hbm, wkv_ref)], sems)
    mask_columns(mask_ref, bias_ref)
    stack_image(image_ref, (i0, i1, i2, i3, i4, i5, i6, i7))
    saved = fetch([(image_ref, image_hbm)], sems, 1)
    copies[0].wait()
    keys_ref[...] = nn(image_ref[...], wkv_ref[:, :D]).astype(BF)
    values_t_ref[...] = nt(wkv_ref[:, D:].T, image_ref[...]).astype(BF)
    saved += fetch([(keys_ref, keys_hbm), (values_t_ref, values_t_hbm)], sems, 2)
    q_t = query_ref[...].astype(F32).T * SCALE
    for quad in range(2):
        soften_quad(quad, q_t, keys_ref, probs_ref, score_ref, bias_ref)
        saved += fetch([(probs_ref.at[quad], probs_hbm.at[quad])], sems, 4 + quad)
    for copy in saved:
        copy.wait()


def gelu_parts(value):
    c = 0.7978845608028654
    square = value * value
    bent = jnp.tanh(c * value * (1.0 + 0.044715 * square))
    half = 0.5 * (1.0 + bent)
    slope = half + 0.5 * value * (1.0 - bent * bent) * (c * (1.0 + 3.0 * 0.044715 * square))
    return value * half, slope


def middle_kernel(
    place_ref, mod_ref, gains_ref, n0, n1, n2, n3, n4, n5, n6, n7, c0, c1, c2, c3,
    after_hbm, wqkv_hbm, wo_hbm, w_in_hbm, w_out_hbm,
    sums_ref, out_hbm, grad_hbm, keep_hbm, send_hbm, mid_keep_hbm, mid_send_hbm, pack_keep_hbm, pack_send_hbm,
    out_ref, grad_ref, keep_ref, send_ref, mid_keep_ref, mid_send_ref, pack_keep_ref, pack_send_ref,
    after_ref, wqkv_ref, wo_ref, w_in_ref, w_out_ref, cot_ref,
    all_ref, keys_ref, values_t_ref, probs_ref, score_ref, slopes_ref, gk_ref, gv_ref,
    hidden_ref, inner_ref, attended_ref, query_ref, out_t_ref, gq_ref, sems,
):
    blocks = (n0, n1, n2, n3, n4, n5, n6, n7)
    copies = fetch(
        [(wqkv_hbm, wqkv_ref)]
        + [(block, all_ref.at[ROWS * j : ROWS * j + ROWS]) for j, block in enumerate(blocks)],
        sems,
    )
    saved = []

    def save(*pairs):
        saved.extend(fetch(pairs, sems, 17 + len(saved)))

    y, core = place_ref[2], place_ref[3]
    step = pl.when(core >= 0)
    halves = ((mid_send_ref, 1 - core), (mid_keep_ref, core))
    wq, wk, wv = (pl.ds(D * j, D) for j in range(3))
    for copy in copies:
        copy.wait()
    copies = fetch(
        [(after_hbm, after_ref), (wo_hbm, wo_ref), (w_in_hbm, w_in_ref), (w_out_hbm, w_out_ref)]
        + [(piece, cot_ref.at[j]) for j, piece in enumerate((c0, c1, c2, c3))],
        sems, 9,
    )

    @step
    def _():
        query = nn(all_ref[:ROWS, :], wqkv_ref[:, wq]).astype(BF).astype(F32) * SCALE
        query_ref[...] = query
        keys_ref[...] = nn(all_ref[...], wqkv_ref[:, wk]).astype(BF)
        values_t_ref[...] = nt(wqkv_ref[:, wv].T, all_ref[...]).astype(BF)
        out_t = attend(query.T, keys_ref, values_t_ref, probs_ref, score_ref, None)
        out_t_ref[...] = out_t
        attended_ref[...] = out_t.T.astype(BF)

    for copy in copies:
        copy.wait()

    @step
    def _():
        mod = mod_ref[...]
        gains = gains_ref[...].astype(F32)
        after = after_ref[...] + nn(attended_ref[...], wo_ref[...])
        xhat, rstd, slope = norm_parts(after, gains[2:3], mod[5:6])
        normed = (xhat * slope + mod[4:5]).astype(BF)
        inner = nn(normed, w_in_ref[...])
        value, bend = gelu_parts(inner)
        hidden_ref[...] = value.astype(BF)
        result = after + nn(hidden_ref[...], w_out_ref[...])
        out_ref[...] = result.astype(BF)
        cot = add_all([cot_ref[j] for j in range(4)])
        branch = cot.astype(BF)
        grad_inner = (nt(branch, w_out_ref[...]) * bend).astype(BF)
        inner_ref[...] = grad_inner
        for ref, half in ((pack_send_ref, 1 - core), (pack_keep_ref, core)):
            wide = pl.ds(pl.multiple_of(half * 1024, 1024), 1024)
            ref[:, :D] = normed
            ref[:, D : 2 * D] = branch
            ref[:, 1024:2048] = hidden_ref[:, wide]
            ref[:, 2048:] = inner_ref[:, wide]
        grad = nt(grad_inner, w_in_ref[...])
        sums_ref[...] = jnp.zeros(sums_ref.shape, F32)
        for row, line in enumerate(norm_sums(grad, xhat, gains[2:3], mod[5:6])):
            sums_ref[row : row + 1, :] = line
        grad_ref[...] = cot + norm_back(grad, xhat, rstd, slope)

    save((pack_send_ref, pack_send_hbm), (pack_keep_ref, pack_keep_hbm), (out_ref, out_hbm), (grad_ref, grad_hbm))

    @step
    def _():
        branch = grad_ref[...].astype(BF)
        grad = nt(branch, wo_ref[...]).astype(BF).astype(F32)
        grad_t = nt(wo_ref[...], branch).astype(BF).astype(F32)
        gq_ref[...] = attend_back(
            query_ref[...], grad, grad_t, out_t_ref[...], keys_ref, values_t_ref, probs_ref, slopes_ref, gk_ref,
            gv_ref,
        ).astype(BF)
        for ref, half in halves:
            narrow = pl.ds(pl.multiple_of(half * 256, 256), 256)
            ref[y] = tn(attended_ref[:, narrow], branch).astype(BF)
            ref[1 ^ y] = tn(all_ref[:ROWS, narrow], gq_ref[...]).astype(BF)
            ref[2 ^ y] = tn(all_ref[:, narrow], gk_ref[...]).astype(BF)
            ref[3 ^ y] = tn(all_ref[:, narrow], gv_ref[...]).astype(BF)

    save((mid_send_ref, mid_send_hbm), (mid_keep_ref, mid_keep_hbm))

    @step
    def _():
        part = nt(gk_ref[512:, :], wqkv_ref[:, wk]) + nt(gv_ref[512:, :], wqkv_ref[:, wv])
        send_ref[...] = part.astype(BF).reshape(4, ROWS, D)

    save((send_ref, send_hbm))

    @step
    def _():
        part = nt(gk_ref[:512, :], wqkv_ref[:, wk]) + nt(gv_ref[:512, :], wqkv_ref[:, wv])
        keep_ref[0] = (part[:ROWS] + nt(gq_ref[...], wqkv_ref[:, wq])).astype(BF)
        keep_ref[1:] = part[ROWS:].astype(BF).reshape(3, ROWS, D)

    save((keep_ref, keep_hbm))
    for copy in saved:
        copy.wait()


def wide_kernel(own_hbm, got_hbm, out_hbm, rows_ref, out_ref, sems):
    for copy in fetch([(own_hbm, rows_ref.at[:ROWS]), (got_hbm, rows_ref.at[ROWS:])], sems):
        copy.wait()
    out_ref[:1024, :] = tn(rows_ref[:, 1024:2048], rows_ref[:, D : 2 * D]).astype(BF)
    saved = fetch([(out_ref.at[:1024], out_hbm.at[:1024])], sems, 2)
    for j in range(2):
        part = tn(rows_ref[:, :D], rows_ref[:, 2048 + D * j : 2560 + D * j])
        rows = slice(1024 + D * j, 1536 + D * j)
        out_ref[rows, :] = part.astype(BF)
        saved += fetch([(out_ref.at[rows], out_hbm.at[rows])], sems, 3 + j)
    for copy in saved:
        copy.wait()


def cross_back_kernel(
    place_ref, mod_ref, gains_ref, sums_in_ref, act_ref, g0, g1, g2, g3,
    after_hbm, wo_hbm, grad_hbm, attended_hbm, values_t_hbm, probs_hbm, keys_hbm, query_hbm, tokens_hbm, wq_hbm,
    image_hbm, wkv_hbm,
    last_keep_hbm, last_send_hbm, keep_hbm, send_hbm, tokens_out_hbm,
    last_keep_ref, last_send_ref, keep_ref, send_ref, tokens_out_ref,
    g_ref, after_ref, wo_ref, grad_ref, attended_ref, values_t_ref, probs_ref, keys_ref, query_ref, tokens_ref,
    wq_ref, image_ref, wkv_ref, sums_ref, slopes_ref, kv_ref, normed_ref, sems,
):
    early = fetch(
        [(piece, g_ref.at[j]) for j, piece in enumerate((g0, g1, g2, g3))]
        + [
            (after_hbm, after_ref), (wo_hbm, wo_ref), (grad_hbm, grad_ref), (attended_hbm, attended_ref),
            (query_hbm, query_ref),
        ],
        sems,
    )
    copies = fetch(
        [
            (values_t_hbm, values_t_ref), (probs_hbm, probs_ref), (keys_hbm, keys_ref), (tokens_hbm, tokens_ref),
            (wq_hbm, wq_ref), (image_hbm, image_ref), (wkv_hbm, wkv_ref),
        ],
        sems, 9,
    )
    saved = []

    def save(*pairs):
        saved.extend(fetch(pairs, sems, 16 + len(saved)))

    y, core = place_ref[2], place_ref[3]
    halves = ((last_send_ref, 1 - core), (last_keep_ref, core))
    for copy in early:
        copy.wait()

    mod = mod_ref[...]
    gains = gains_ref[...].astype(F32)
    incoming = add_all([g_ref[j] for j in range(4)])
    xhat, rstd, slope = norm_parts(after_ref[...], gains[1:2], mod[3:4])
    sums_ref[...] = sums_in_ref[...]
    for row, line in enumerate(norm_sums(incoming, xhat, gains[1:2], mod[3:4])):
        sums_ref[3 + row : 4 + row, :] = line
    grad_ref[...] += norm_back(incoming, xhat, rstd, slope)
    branch = grad_ref[...].astype(BF)
    for ref, half in halves:
        narrow = pl.ds(pl.multiple_of(half * 256, 256), 256)
        ref[y, :256, :] = tn(attended_ref[:, narrow], branch).astype(BF)

    for copy in copies[:3]:
        copy.wait()
    grad = nt(branch, wo_ref[...]).astype(BF).astype(F32)
    grad_t = nt(wo_ref[...], branch).astype(BF).astype(F32)
    out_t = attended_ref[...].astype(F32).T
    query = query_ref[...].astype(F32) * SCALE
    gq = attend_back(
        query, grad, grad_t, out_t, keys_ref, values_t_ref, probs_ref, slopes_ref, kv_ref.at[0], kv_ref.at[1],
    ).astype(BF)
    for copy in copies[3:]:
        copy.wait()
    tokens = tokens_ref[...].astype(F32)
    xhat, rstd, slope = norm_parts(tokens, gains[0:1], mod[1:2])
    normed_ref[...] = (xhat * slope + mod[0:1]).astype(BF)
    incoming = nt(gq, wq_ref[...])
    for row, line in enumerate(norm_sums(incoming, xhat, gains[0:1], mod[1:2])):
        sums_ref[6 + row : 7 + row, :] = line
    tokens_out_ref[...] = grad_ref[...] + norm_back(incoming, xhat, rstd, slope)
    act = act_ref[...].astype(F32)
    sums_ref[9:10, :] = act[:, :D]
    sums_ref[10:11, :] = act[:, D:]
    sums = sums_ref[...].astype(BF)
    for ref, half in halves:
        narrow = pl.ds(pl.multiple_of(half * 256, 256), 256)
        ref[1 ^ y, :256, :] = tn(normed_ref[:, narrow], gq).astype(BF)
        part = tn(image_ref[...], kv_ref[half]).astype(BF)
        for side in range(2):
            ref[(2 + side) ^ y, :192, :] = part[192 * side : 192 * side + 192, :]
            ref[(2 + side) ^ y, 192:256, :] = jnp.zeros((64, D), BF)
        for j in range(4):
            ref[j, 256:, :] = sums

    save((last_send_ref, last_send_hbm), (last_keep_ref, last_keep_hbm), (tokens_out_ref, tokens_out_hbm))

    wk, wv = wkv_ref[:, :D], wkv_ref[:, D:]
    half_keys = IMG_KEYS // 2
    for ref, base in ((keep_ref, 0), (send_ref, half_keys)):
        span = slice(base, base + half_keys)
        part = nt(kv_ref[0, span, :], wk) + nt(kv_ref[1, span, :], wv)
        ref[...] = part.astype(BF).reshape(4, IMG_PAD, 384)

    save((keep_ref, keep_hbm), (send_ref, send_hbm))
    for copy in saved:
        copy.wait()


def fold_kernel(place_ref, m0, m1, m2, m3, l0, l1, l2, l3, t0, t1, t2, t3, total_ref):
    total_ref[:, :64, :] = add_all([m0[...], m1[...], m2[...], m3[...]]).astype(BF).reshape(4, 64, D)
    late = add_all([l0[...], l1[...], l2[...], l3[...]]).astype(BF)
    total_ref[:, 64:, :] = late[:256].reshape(4, 64, D)
    for j, ref in enumerate((t0, t1, t2, t3)):
        ref[:ROWS, :] = total_ref[place_ref[0] ^ j]
        ref[ROWS:, :] = late[256:]


def join_kernel(a_ref, b_ref, c_ref, d_ref, out_ref):
    refs = (a_ref, b_ref, c_ref, d_ref)
    out_ref[:ROWS, :] = add_all([ref[:ROWS, :] for ref in refs]).astype(BF)
    for j, ref in enumerate(refs):
        out_ref[ROWS + 16 * j : ROWS + 16 * j + 16, :] = ref[ROWS:, :]


def meet_kernel(a_ref, b_ref, c_ref, d_ref, out_ref, sums_ref):
    refs = (a_ref, b_ref, c_ref, d_ref)
    out_ref[...] = add_all([ref[:ROWS, :] for ref in refs]).astype(BF)
    for j, ref in enumerate(refs):
        sums_ref[64 * j : 64 * j + 64, :] = ref[ROWS:, :]


def wide_sum_kernel(parts_ref, copies_ref):
    total = jnp.sum(parts_ref[...].astype(F32), axis=0).astype(BF)
    for j in range(4):
        copies_ref[j] = total


def wide_copies_kernel(parts_ref, copies_ref):
    total = jnp.sum(parts_ref[...].astype(F32), axis=0).astype(BF)
    for j in range(16):
        copies_ref[j] = total


def modulation_kernel(sums_in_ref, a_ref, b_ref, c_ref, d_ref, gains_ref, image_ref, modw_hbm, modw_ref, sems):
    sums = sums_in_ref[...].astype(F32)
    acts = (jnp.concatenate([sums[:, 9, :], sums[:, 10, :]], axis=1) * 0.125).astype(BF)
    copies = []
    for norm in range(3):
        first = 3 * (2 - norm)
        gains_ref[norm : norm + 1, :] = jnp.sum(sums[:, first, :], axis=0, keepdims=True)
        for kind in range(2):
            part = 2 * norm + kind
            modw_ref[part] = tn(acts, sums[:, first + 1 + kind, :].astype(BF))
            target = modw_hbm.at[:, D * part : D * part + D]
            copies += fetch([(modw_ref.at[part], target)], sems, len(copies))
    image_ref[...] = add_all([a_ref[...], b_ref[...], c_ref[...], d_ref[...]])[:IMG_ROWS].reshape(IMG_ROWS, 1, 384)
    for copy in copies:
        copy.wait()


def out_kernel(side, place_ref, wide_hbm, p0, p1, p2, p3, *refs):
    targets, refs = (refs[:7], refs[7:]) if side == 0 else (refs[7:14], refs[14:])
    w_in_ref, w_out_ref, wo_self_ref, wqkv_ref, wo_ref, wq_ref, wkv_ref, wide_ref, late_ref, sems = refs
    w_in_hbm, w_out_hbm, wo_self_hbm, wqkv_hbm, wo_hbm, wq_hbm, wkv_hbm = targets
    x, y, core = place_ref[0], place_ref[2], place_ref[3]
    step = pl.when(core >= 0)
    half = core ^ side
    wide_in = fetch([(wide_hbm.at[8 * j : 8 * j + 8], wide_ref.at[8 * j : 8 * j + 8]) for j in range(2)], sems)
    late_in = fetch([(piece, late_ref.at[j]) for j, piece in enumerate((p0, p1, p2, p3))], sems, 2)
    saved = []

    def save(*pairs):
        saved.extend(fetch(pairs, sems, 6 + len(saved)))

    wide_rows = pl.ds(pl.multiple_of(half * 1024, 1024), 1024)
    rows = pl.ds(pl.multiple_of(half * 256, 256), 256)
    columns = pl.ds(pl.multiple_of(half * D, D), D)
    wide_in[0].wait()

    @step
    def _():
        w_out_ref[...] = wide_ref[:8].reshape(1024, D).astype(F32)

    save((w_out_ref, w_out_hbm.at[wide_rows]))
    wide_in[1].wait()

    @step
    def _():
        for j in range(2):
            w_in_ref[:, D * j : D * j + D] = wide_ref[8 + 4 * j : 12 + 4 * j].reshape(D, D).astype(F32)

    save((w_in_ref, w_in_hbm.at[:, wide_rows]))
    for copy in late_in:
        copy.wait()

    @step
    def _():
        for piece in range(4):
            block = y ^ piece
            for across in range(4):
                strip = x ^ across
                strip_rows = pl.ds(pl.multiple_of(strip * 64, 64), 64)
                early = late_ref[piece, across, :64, :].astype(F32)
                late = late_ref[piece, across, 64:, :].astype(F32)

                @pl.when(block == 0)
                def _():
                    wo_self_ref[strip_rows, :] = early
                    wo_ref[strip_rows, :] = late

                @pl.when(block > 0)
                def _():
                    wqkv_ref[strip_rows, pl.ds(pl.multiple_of((block - 1) * D, D), D)] = early

                @pl.when(block == 1)
                def _():
                    wq_ref[strip_rows, :] = late

                @pl.when((block > 1) & (strip < 3))
                def _():
                    start = pl.multiple_of((block - 2) * 192 + strip * 64, 64)
                    wkv_ref[pl.ds(start, 64), :] = late

    save(
        (wo_self_ref, wo_self_hbm.at[rows]), (wqkv_ref, wqkv_hbm.at[rows]), (wo_ref, wo_hbm.at[rows]),
        (wq_ref, wq_hbm.at[rows]), (wkv_ref, wkv_hbm.at[:, columns]),
    )
    for copy in saved:
        copy.wait()


def tie(*values):
    return lax.optimization_barrier(values)


def swap_core(value):
    return lax.ppermute(value, "core", CORE_SWAP)


def swap(value, axis, step):
    return lax.ppermute(value, axis, [(i, i ^ step) for i in range(4)])


def swap_y(value, step):
    return swap(value, "y", step)


def gather_eight(value):
    across = [value] + [swap_y(value, step) for step in (1, 2, 3)]
    return across + [swap_core(item) for item in across]


def scatter_eight(keep, send):
    return others(halve(keep, send), "y")


def add_all(items):
    total = items[0].astype(F32)
    for item in items[1:]:
        total = total + item.astype(F32)
    return total


def halve(keep, send):
    got = swap_core(send)
    return [(keep[j].astype(F32) + got[j].astype(F32)).astype(BF) for j in range(4)]


def spread(mixed):
    rows, width = mixed.shape
    return lax.all_to_all(mixed, ("x", "z"), 0, 0, tiled=True).reshape(16, rows // 16, width)


def collect(copies):
    return lax.all_to_all(copies, ("x", "z"), 0, 0, tiled=True)


def others(pieces, axis):
    return [pieces[0]] + [swap(pieces[step], axis, step) for step in (1, 2, 3)]


def gather_axis(value, axis):
    return jnp.stack(others([value] * 4, axis))


def local(
    tokens, camera, image, image_mask, point_rows, point_count, point_grads, mod_weight, norm_gains,
    wq_cross, wkv_cross, wo_cross, wqkv_self, wo_self, w_in, w_out,
):
    place = [lax.axis_index(axis).astype(jnp.int32) for axis in ("x", "z", "y", "core")]
    y, core = place[2:]
    owners = [2 * (y ^ (j % 4)) + (core ^ (j // 4)) for j in range(8)]
    place = jnp.stack(place + owners).astype(jnp.int32)
    toks = tokens[0]

    image_blocks = gather_eight(image[0])

    mask = (image_mask[0] > 0).astype(BF).reshape(2, 2, 2, IMG_ROWS)
    for axis, bit in ((0, y & 2), (1, y & 1), (2, core)):
        mask = jnp.where(bit != 0, jnp.flip(mask, axis), mask)
    mask = jnp.pad(mask.transpose(2, 0, 1, 3), ((0, 0),) * 3 + ((0, IMG_PAD - IMG_ROWS),)).reshape(1, IMG_KEYS)

    cot_keep, cot_send, mod, act = kernel_call(
        points_kernel,
        [((4, ROWS, D), BF), ((4, ROWS, D), BF), ((8, D), F32), ((1, 1024), BF)],
        [((1024, 6 * D), BF)], 6 * 10**9,
        place, point_count[0], point_rows, point_grads[0], camera, mod_weight, smem=2, hbm=1, copies=1,
    )
    cot_parts = scatter_eight(cot_keep, cot_send)

    after_cross, normed_two, attended_one, query_one = kernel_call(
        cross_kernel,
        [((ROWS, D), F32), ((ROWS, D), BF), ((ROWS, D), BF), ((ROWS, D), BF)],
        [
            ((IMG_KEYS, 384), BF), ((IMG_KEYS, D), BF), ((D, IMG_KEYS), BF), ((IMG_KEYS, 512), F32),
            ((2, IMG_KEYS, 512), BF), ((D, D), BF), ((384, 2 * D), BF), ((D, D), BF), ((IMG_KEYS, 128), F32),
        ],
        10 * 10**9,
        toks, mod, norm_gains, mask, *image_blocks, wq_cross, wkv_cross, wo_cross, hbm=3, copies=3, limit=60,
    )

    normed_two, *cot_parts = tie(normed_two, *cot_parts)
    across = others([normed_two] * 4, "y")
    keys_one, values_t_one, image_all, probs_one = kernel_call(
        cross_rest_kernel,
        [((IMG_KEYS, D), BF), ((D, IMG_KEYS), BF), ((IMG_KEYS, 384), BF), ((2, IMG_KEYS, 512), BF)],
        [
            ((384, 2 * D), BF), ((IMG_KEYS, D), BF), ((D, IMG_KEYS), BF), ((IMG_KEYS, 384), BF),
            ((2, IMG_KEYS, 512), BF), ((IMG_KEYS, 512), F32), ((IMG_KEYS, 128), F32),
        ],
        7 * 10**9, tie(query_one, normed_two)[0], mask, *image_blocks, wkv_cross, hbm=1, hbm_outs=4, copies=6,
    )
    keys_one, values_t_one, image_all, probs_one, *across = tie(keys_one, values_t_one, image_all, probs_one, *across)
    normed_blocks = across + [swap_core(item) for item in across]
    (
        sums, layer_out, grad_after_self, back_keep, back_send, mid_keep, mid_send, pack_keep, pack_send,
    ) = kernel_call(
        middle_kernel,
        [((16, D), F32)] + MIDDLE_OUTS,
        MIDDLE_OUTS
        + [
            ((ROWS, D), F32), ((D, 3 * D), BF), ((D, D), BF), ((D, 2048), BF), ((2048, D), BF), ((4, ROWS, D), BF),
            ((KEYS, D), BF), ((KEYS, D), BF), ((D, KEYS), BF),
            ((2, KEYS, 512), BF), ((KEYS, 512), F32), ((KEYS, 512), BF), ((KEYS, D), BF), ((KEYS, D), BF),
            ((ROWS, 2048), BF), ((ROWS, 2048), BF), ((ROWS, D), BF), ((ROWS, D), F32), ((D, ROWS), F32),
            ((ROWS, D), BF),
        ],
        20 * 10**9,
        place, mod, norm_gains, *normed_blocks, *cot_parts, after_cross, wqkv_self, wo_self, w_in, w_out,
        smem=1, hbm=17, hbm_outs=8, copies=25, limit=50,
    )

    back_parts = halve(back_keep, back_send)
    pack_send, mid_send, *back_parts = tie(pack_send, mid_send, *back_parts)
    pack_got = swap_core(pack_send)
    mid_got = swap_core(mid_send)
    back_parts = others(back_parts, "y")
    (wide_mixed,) = kernel_call(
        wide_kernel, [((2048, D), BF)], [((256, 3072), BF), ((2048, D), BF)], 3 * 10**9, pack_keep, pack_got,
        hbm=2, hbm_outs=1, copies=5, limit=20,
    )
    mid_pieces = [(mid_keep[j].astype(F32) + mid_got[j].astype(F32)).astype(BF) for j in range(4)]
    wide_mixed, *pieces = tie(wide_mixed, *back_parts, *mid_pieces)
    back_parts, mid_pieces = pieces[:4], pieces[4:]
    wide_parts = spread(wide_mixed)
    mid_pieces = others(mid_pieces, "y")

    last_keep, last_send, img_keep, img_send, grad_tokens = kernel_call(
        cross_back_kernel,
        CROSS_OUTS,
        CROSS_OUTS
        + [
            ((4, ROWS, D), BF), ((ROWS, D), F32), ((D, D), BF), ((ROWS, D), F32), ((ROWS, D), BF), ((D, IMG_KEYS), BF),
            ((2, IMG_KEYS, 512), BF), ((IMG_KEYS, D), BF), ((ROWS, D), BF), ((ROWS, D), BF), ((D, D), BF),
            ((IMG_KEYS, 384), BF), ((384, 2 * D), BF), ((16, D), F32), ((IMG_KEYS, 512), BF), ((2, IMG_KEYS, D), BF),
            ((ROWS, D), BF),
        ],
        11 * 10**9,
        place, mod, norm_gains, sums, act, *back_parts, after_cross, wo_cross, grad_after_self, attended_one,
        values_t_one, probs_one, keys_one, query_one, toks, wq_cross, image_all, wkv_cross,
        smem=1, hbm=16, hbm_outs=5, copies=22, limit=54,
    )
    last_send, img_send, *mid_pieces = tie(last_send, img_send, *mid_pieces)
    last_pieces = others(halve(last_keep, last_send), "y")
    img_mixed = halve(img_keep, img_send)
    (wide,) = kernel_call(wide_sum_kernel, [((4, ROWS, D), BF)], [], 2 * 10**9, wide_parts, limit=16)
    *last_pieces, wide, img_mixed = tie(*last_pieces, wide, img_mixed)
    late_pieces = kernel_call(
        fold_kernel, [((144, D), BF)] * 4, [((4, ROWS, D), BF)], 2 * 10**9, place, *mid_pieces, *last_pieces, smem=1, limit=16,
    )
    late_pieces = others(late_pieces, "x")
    late_pieces[1], wide = tie(late_pieces[1], wide)
    wide = lax.all_to_all(wide, "y", 0, 0, tiled=True)
    (late,) = kernel_call(join_kernel, [((192, D), BF)], [], 10**9, *late_pieces, limit=16)
    late, *img_mixed = tie(late, *img_mixed)
    late_pieces = others([late] * 4, "z")
    img_pieces = [img_mixed[0], swap_y(img_mixed[1], 1), swap_y(img_mixed[2], 2)]
    *late_pieces, wide = tie(*late_pieces, wide)
    late, all_sums = kernel_call(meet_kernel, [((ROWS, D), BF), ((256, D), BF)], [], 10**9, *late_pieces, limit=16)
    late, img_mixed[3] = tie(late, img_mixed[3])
    img_pieces.append(swap_y(img_mixed[3], 3))
    late_pieces = others([late] * 4, "x")
    (wide,) = kernel_call(wide_copies_kernel, [((16, ROWS, D), BF)], [], 2 * 10**9, wide)
    *late_pieces, wide, img_pieces[1], img_pieces[2] = tie(*late_pieces, wide, img_pieces[1], img_pieces[2])
    late = jnp.stack(late_pieces)
    wide = collect(wide)
    late_own = others([late] * 4, "y")
    g_gains, grad_image, g_mod = kernel_call(
        modulation_kernel, [((3, D), F32), ((IMG_ROWS, 1, 384), F32), ((1024, 6 * D), F32)], [((6, 1024, D), F32)],
        7 * 10**9, tie(all_sums, late)[0].reshape(16, 16, D), *img_pieces, hbm_outs=1, copies=6,
    )
    late_other = [swap_core(late_own[0])]
    late_own, late_other, g_gains, g_mod, wide = tie(late_own, late_other, g_gains, g_mod, wide)
    late_other = late_other + [swap_core(item) for item in late_own[1:]]
    halves = [
        ((D, 1024), F32), ((1024, D), F32), ((256, D), F32), ((256, 3 * D), F32), ((256, D), F32), ((256, D), F32),
        ((384, D), F32), ((16, ROWS, D), BF), ((4, 4, ROWS, D), BF),
    ]
    wide_other = swap_core(wide)
    grads = kernel_call(
        functools.partial(out_kernel, 0), GRAD_OUTS, halves, 4 * 10**9, place, wide, *late_own,
        smem=1, hbm=5, hbm_outs=7, copies=13, limit=40,
    )
    g_in, g_out, g_wo_self, g_wqkv, g_wo_cross, g_wq, g_wkv = kernel_call(
        functools.partial(out_kernel, 1), GRAD_OUTS, halves, 4 * 10**9, place, wide_other, *late_other, *grads,
        smem=1, hbm=12, hbm_outs=7, copies=13, limit=40, aliases={6 + j: j for j in range(7)},
    )
    return (
        layer_out[None], grad_tokens[None], grad_image.reshape(1, IMG_ROWS, 384), g_mod, g_gains, g_wq, g_wkv, g_wo_cross, g_wqkv,
        g_wo_self, g_in, g_out,
    )


def solution(mesh):
    split = Mesh(mesh.devices.reshape(4, 4, 4, 2), ("x", "z", "y", "core"))
    obj, tok = ("x", "z"), ("y", "core")
    return jax.shard_map(
        local,
        mesh=split,
        in_specs=(
            P(obj, tok, None), P(obj, None), P(obj, tok, None), P(obj, None), P(obj, tok), P(obj, tok),
            P(obj, tok, None),
        )
        + (P(),) * 9,
        out_specs=(P(obj, tok, None),) * 3 + (P(),) * 9,
        check_vma=False,
    )
```

```python
import functools

import jax
import jax.numpy as jnp
from jax import lax
from jax.experimental import pallas as pl
from jax.experimental.pallas import tpu as pltpu
from jax.sharding import Mesh
from jax.sharding import PartitionSpec as P

BF = jnp.bfloat16
F32 = jnp.float32
D = 512
ROWS = 128
IMG_ROWS = 130
IMG_PAD = 144
IMG_KEYS = 8 * IMG_PAD
KEYS = 8 * ROWS
SCALE = 0.125
MIDDLE_OUTS = [
    ((ROWS, D), BF), ((ROWS, D), F32), ((4, ROWS, D), BF), ((4, ROWS, D), BF),
    ((4, 256, D), BF), ((4, 256, D), BF), ((ROWS, 3072), BF), ((ROWS, 3072), BF),
]
CROSS_OUTS = [
    ((4, 272, D), BF), ((4, 272, D), BF), ((4, IMG_PAD, 384), BF), ((4, IMG_PAD, 384), BF), ((ROWS, D), F32),
]
GRAD_OUTS = [
    ((D, 2048), F32), ((2048, D), F32), ((D, D), F32), ((D, 3 * D), F32), ((D, D), F32), ((D, D), F32),
    ((384, 2 * D), F32),
]
CORE_SWAP = [(0, 1), (1, 0)]
VMEM = pl.BlockSpec(memory_space=pltpu.VMEM)
SMEM = pl.BlockSpec(memory_space=pltpu.SMEM)
HBM = pl.BlockSpec(memory_space=pl.ANY)


def nn(left, right):
    return jnp.dot(left, right, preferred_element_type=F32)


def nt(left, right):
    return lax.dot_general(left, right, (((1,), (1,)), ((), ())), preferred_element_type=F32)


def tn(left, right):
    return lax.dot_general(left, right, (((0,), (0,)), ((), ())), preferred_element_type=F32)


def kernel_call(body, outs, scratch, flops, *args, smem=0, hbm=0, hbm_outs=0, copies=0, limit=60, aliases=None):
    in_specs = [SMEM] * smem + [VMEM] * (len(args) - smem - hbm) + [HBM] * hbm
    moved = sum(item.size * item.dtype.itemsize for item in args)
    return pl.pallas_call(
        body,
        out_shape=[jax.ShapeDtypeStruct(shape, dtype) for shape, dtype in outs],
        in_specs=in_specs,
        out_specs=[VMEM] * (len(outs) - hbm_outs) + [HBM] * hbm_outs,
        scratch_shapes=[pltpu.VMEM(shape, dtype) for shape, dtype in scratch]
        + ([pltpu.SemaphoreType.DMA((copies,))] if copies else []),
        input_output_aliases=aliases or {},
        compiler_params=pltpu.CompilerParams(vmem_limit_bytes=limit << 20),
        cost_estimate=pl.CostEstimate(flops=flops, bytes_accessed=moved, transcendentals=0),
    )(*args)


def fetch(pairs, semaphores, first=0):
    copies = [
        pltpu.make_async_copy(source, target, semaphores.at[first + i]) for i, (source, target) in enumerate(pairs)
    ]
    for copy in copies:
        copy.start()
    return copies


def norm_parts(values, gain, scale):
    center = values - jnp.mean(values, axis=-1, keepdims=True)
    rstd = lax.rsqrt(jnp.mean(center * center, axis=-1, keepdims=True) + 1e-05)
    return center * rstd, rstd, gain * (1.0 + scale)


def norm_back(grad, xhat, rstd, slope):
    scaled = grad * slope
    return rstd * (
        scaled
        - jnp.mean(scaled, axis=-1, keepdims=True)
        - xhat * jnp.mean(scaled * xhat, axis=-1, keepdims=True)
    )


def norm_sums(grad, xhat, gain, scale):
    total = jnp.sum(grad * xhat, axis=0, keepdims=True)
    return total * (1.0 + scale), jnp.sum(grad, axis=0, keepdims=True), total * gain


def spread_columns(block):
    head = lax.broadcasted_iota(jnp.int32, block.shape, 0) >> 6
    return jnp.concatenate([jnp.where(head == j, block, 0.0) for j in range(4)], axis=1)


def spread_rows(block):
    head = lax.broadcasted_iota(jnp.int32, block.shape, 1) >> 6
    return jnp.concatenate([jnp.where(head == j, block, 0.0) for j in range(4)], axis=0)


def gather_heads(wide):
    return jnp.concatenate(
        [wide[64 * j : 64 * j + 64, 128 * j : 128 * j + 128] for j in range(4)], axis=0
    )


def fold8(values, reduce):
    rows, width = values.shape
    return reduce(values.reshape(rows // 8, 8, width), axis=0)


def chunked(total):
    return [(start, min(256, total - start)) for start in range(0, total, 256)]


def soften_quad(quad, q_t, keys_ref, probs_ref, score_ref, bias_ref):
    chunks = chunked(keys_ref.shape[0])
    lanes = slice(256 * quad, 256 * quad + 256)
    spread = spread_columns(q_t[lanes, :]).astype(BF)
    top = None
    for start, size in chunks:
        scores = nn(keys_ref[start : start + size, lanes], spread)
        if bias_ref is not None:
            scores = scores + jnp.concatenate([bias_ref[start : start + size, :]] * 4, axis=1)
        score_ref[start : start + size, :] = scores
        here = fold8(scores, jnp.max)
        top = here if top is None else jnp.maximum(top, here)
    top = jnp.max(top, axis=0, keepdims=True)
    total = None
    for start, size in chunks:
        weights = jnp.exp(score_ref[start : start + size, :] - top)
        score_ref[start : start + size, :] = weights
        here = fold8(weights, jnp.sum)
        total = here if total is None else total + here
    inverse = 1.0 / jnp.sum(total, axis=0, keepdims=True)
    for start, size in chunks:
        probs_ref[quad, start : start + size, :] = (score_ref[start : start + size, :] * inverse).astype(BF)


def attend(q_t, keys_ref, values_t_ref, probs_ref, score_ref, bias_ref):
    parts = []
    for quad in range(2):
        soften_quad(quad, q_t, keys_ref, probs_ref, score_ref, bias_ref)
        parts.append(gather_heads(nn(values_t_ref[256 * quad : 256 * quad + 256, :], probs_ref[quad])))
    return jnp.concatenate(parts, axis=0)


def attend_back(q_s, grad, grad_t, out_t, keys_ref, values_t_ref, probs_ref, slopes_ref, gk_ref, gv_ref):
    inner = grad_t * out_t
    parts = []
    for quad in range(2):
        lanes = slice(256 * quad, 256 * quad + 256)
        spread = spread_columns(grad_t[lanes, :]).astype(BF)
        delta = jnp.concatenate(
            [
                jnp.sum(inner[256 * quad + 64 * j : 256 * quad + 64 * j + 64, :], axis=0, keepdims=True)
                for j in range(4)
            ],
            axis=1,
        )
        grad_rows = spread_rows(grad[:, lanes]).astype(BF)
        query_rows = spread_rows(q_s[:, lanes]).astype(BF)
        for start, size in chunked(keys_ref.shape[0]):
            span = slice(start, start + size)
            grad_probs = tn(values_t_ref[lanes, span], spread)
            probs = probs_ref[quad, span, :]
            slopes = (probs.astype(F32) * (grad_probs - delta)).astype(BF)
            slopes_ref[span, :] = slopes
            gv_ref[span, lanes] = nn(probs, grad_rows).astype(BF)
            gk_ref[span, lanes] = nn(slopes, query_rows).astype(BF)
        parts.append(gather_heads(tn(keys_ref[:, lanes], slopes_ref[...])))
    return jnp.concatenate(parts, axis=0).T * SCALE


def points_kernel(place_ref, count_ref, rows_ref, grads_ref, camera_ref, modw_hbm, keep_ref, send_ref, mod_ref, act_ref, modw_ref, sems):
    copies = fetch([(modw_hbm, modw_ref)], sems)
    row_ids = rows_ref[...]
    slot = lax.broadcasted_iota(jnp.int32, row_ids.shape, 1)
    row_ids = jnp.where(slot < count_ref[0], row_ids, -1)
    for block in range(8):
        target = lax.broadcasted_iota(jnp.int32, (ROWS, row_ids.shape[1]), 0) + place_ref[4 + block] * ROWS
        onehot = jnp.where(target == row_ids, 1.0, 0.0).astype(BF)
        part = nn(onehot, grads_ref[...]).astype(BF)
        out = keep_ref if block < 4 else send_ref
        out[block % 4] = part
    camera = camera_ref[...].astype(F32)
    act = (camera / (1.0 + jnp.exp(-camera))).astype(BF)
    act_ref[...] = act
    copies[0].wait()
    modulation = nn(jnp.broadcast_to(act, (16, act.shape[1])), modw_ref[...])
    for row in range(6):
        mod_ref[row : row + 1, :] = modulation[0:1, D * row : D * row + D]
    mod_ref[6:8, :] = jnp.zeros((2, D), F32)


def stack_image(image_ref, blocks):
    for j, block in enumerate(blocks):
        base = IMG_PAD * j
        image_ref[base + 128 : base + IMG_PAD, :] = jnp.zeros((16, image_ref.shape[1]), BF)
        image_ref[base : base + IMG_ROWS, :] = block[...]


def mask_columns(mask_ref, bias_ref):
    row = lax.broadcasted_iota(jnp.int32, (16, IMG_KEYS), 0)
    padded = jnp.where(row == 0, mask_ref[...].astype(F32), 0.0).astype(BF)
    kept = tn(padded, jnp.ones((16, 128), BF))
    bias_ref[...] = jnp.where(kept > 0.5, 0.0, -1e30)


def cross_kernel(
    tokens_ref, mod_ref, gains_ref, mask_ref, i0, i1, i2, i3, i4, i5, i6, i7, wq_hbm, wkv_hbm, wo_hbm,
    after_ref, normed_ref, attended_ref, query_ref,
    image_ref, keys_ref, values_t_ref, score_ref, probs_ref, wq_ref, wkv_ref, wo_ref, bias_ref, sems,
):
    copies = fetch([(wkv_hbm, wkv_ref)], sems)
    mask_columns(mask_ref, bias_ref)
    stack_image(image_ref, (i0, i1, i2, i3, i4, i5, i6, i7))
    copies[0].wait()
    copies += fetch([(wq_hbm, wq_ref), (wo_hbm, wo_ref)], sems, 1)
    keys_ref[...] = nn(image_ref[...], wkv_ref[:, :D]).astype(BF)
    values_t_ref[...] = nt(wkv_ref[:, D:].T, image_ref[...]).astype(BF)
    mod = mod_ref[...]
    gains = gains_ref[...].astype(F32)
    tokens = tokens_ref[...].astype(F32)
    xhat, _, slope = norm_parts(tokens, gains[0:1], mod[1:2])
    normed = (xhat * slope + mod[0:1]).astype(BF)
    copies[1].wait()
    query = nn(normed, wq_ref[...]).astype(BF)
    query_ref[...] = query
    q_t = query.astype(F32).T * SCALE
    out_t = attend(q_t, keys_ref, values_t_ref, probs_ref, score_ref, bias_ref)
    attended = out_t.T.astype(BF)
    attended_ref[...] = attended
    copies[2].wait()
    after = tokens + nn(attended, wo_ref[...])
    after_ref[...] = after
    xhat, _, slope = norm_parts(after, gains[1:2], mod[3:4])
    normed_ref[...] = (xhat * slope + mod[2:3]).astype(BF)


def cross_rest_kernel(
    query_ref, mask_ref, i0, i1, i2, i3, i4, i5, i6, i7, wkv_hbm,
    keys_hbm, values_t_hbm, image_hbm, probs_hbm,
    wkv_ref, keys_ref, values_t_ref, image_ref, probs_ref, score_ref, bias_ref, sems,
):
    copies = fetch([(wkv_hbm, wkv_ref)], sems)
    mask_columns(mask_ref, bias_ref)
    stack_image(image_ref, (i0, i1, i2, i3, i4, i5, i6, i7))
    saved = fetch([(image_ref, image_hbm)], sems, 1)
    copies[0].wait()
    keys_ref[...] = nn(image_ref[...], wkv_ref[:, :D]).astype(BF)
    values_t_ref[...] = nt(wkv_ref[:, D:].T, image_ref[...]).astype(BF)
    saved += fetch([(keys_ref, keys_hbm), (values_t_ref, values_t_hbm)], sems, 2)
    q_t = query_ref[...].astype(F32).T * SCALE
    for quad in range(2):
        soften_quad(quad, q_t, keys_ref, probs_ref, score_ref, bias_ref)
        saved += fetch([(probs_ref.at[quad], probs_hbm.at[quad])], sems, 4 + quad)
    for copy in saved:
        copy.wait()


def gelu_parts(value):
    c = 0.7978845608028654
    square = value * value
    bent = jnp.tanh(c * value * (1.0 + 0.044715 * square))
    half = 0.5 * (1.0 + bent)
    slope = half + 0.5 * value * (1.0 - bent * bent) * (c * (1.0 + 3.0 * 0.044715 * square))
    return value * half, slope


def middle_kernel(
    place_ref, mod_ref, gains_ref, n0, n1, n2, n3, n4, n5, n6, n7, c0, c1, c2, c3,
    after_hbm, wqkv_hbm, wo_hbm, w_in_hbm, w_out_hbm,
    sums_ref, out_hbm, grad_hbm, keep_hbm, send_hbm, mid_keep_hbm, mid_send_hbm, pack_keep_hbm, pack_send_hbm,
    out_ref, grad_ref, keep_ref, send_ref, mid_keep_ref, mid_send_ref, pack_keep_ref, pack_send_ref,
    after_ref, wqkv_ref, wo_ref, w_in_ref, w_out_ref, cot_ref,
    all_ref, keys_ref, values_t_ref, probs_ref, score_ref, slopes_ref, gk_ref, gv_ref,
    hidden_ref, inner_ref, attended_ref, query_ref, out_t_ref, gq_ref, sems,
):
    blocks = (n0, n1, n2, n3, n4, n5, n6, n7)
    copies = fetch(
        [(wqkv_hbm, wqkv_ref)]
        + [(block, all_ref.at[ROWS * j : ROWS * j + ROWS]) for j, block in enumerate(blocks)],
        sems,
    )
    saved = []

    def save(*pairs):
        saved.extend(fetch(pairs, sems, 17 + len(saved)))

    y, core = place_ref[2], place_ref[3]
    step = pl.when(core >= 0)
    halves = ((mid_send_ref, 1 - core), (mid_keep_ref, core))
    wq, wk, wv = (pl.ds(D * j, D) for j in range(3))
    for copy in copies:
        copy.wait()
    copies = fetch(
        [(after_hbm, after_ref), (wo_hbm, wo_ref), (w_in_hbm, w_in_ref), (w_out_hbm, w_out_ref)]
        + [(piece, cot_ref.at[j]) for j, piece in enumerate((c0, c1, c2, c3))],
        sems, 9,
    )

    @step
    def _():
        query = nn(all_ref[:ROWS, :], wqkv_ref[:, wq]).astype(BF).astype(F32) * SCALE
        query_ref[...] = query
        keys_ref[...] = nn(all_ref[...], wqkv_ref[:, wk]).astype(BF)
        values_t_ref[...] = nt(wqkv_ref[:, wv].T, all_ref[...]).astype(BF)
        out_t = attend(query.T, keys_ref, values_t_ref, probs_ref, score_ref, None)
        out_t_ref[...] = out_t
        attended_ref[...] = out_t.T.astype(BF)

    for copy in copies:
        copy.wait()

    @step
    def _():
        mod = mod_ref[...]
        gains = gains_ref[...].astype(F32)
        after = after_ref[...] + nn(attended_ref[...], wo_ref[...])
        xhat, rstd, slope = norm_parts(after, gains[2:3], mod[5:6])
        normed = (xhat * slope + mod[4:5]).astype(BF)
        inner = nn(normed, w_in_ref[...])
        value, bend = gelu_parts(inner)
        hidden_ref[...] = value.astype(BF)
        result = after + nn(hidden_ref[...], w_out_ref[...])
        out_ref[...] = result.astype(BF)
        cot = add_all([cot_ref[j] for j in range(4)])
        branch = cot.astype(BF)
        grad_inner = (nt(branch, w_out_ref[...]) * bend).astype(BF)
        inner_ref[...] = grad_inner
        for ref, half in ((pack_send_ref, 1 - core), (pack_keep_ref, core)):
            wide = pl.ds(pl.multiple_of(half * 1024, 1024), 1024)
            ref[:, :D] = normed
            ref[:, D : 2 * D] = branch
            ref[:, 1024:2048] = hidden_ref[:, wide]
            ref[:, 2048:] = inner_ref[:, wide]
        grad = nt(grad_inner, w_in_ref[...])
        sums_ref[...] = jnp.zeros(sums_ref.shape, F32)
        for row, line in enumerate(norm_sums(grad, xhat, gains[2:3], mod[5:6])):
            sums_ref[row : row + 1, :] = line
        grad_ref[...] = cot + norm_back(grad, xhat, rstd, slope)

    save((pack_send_ref, pack_send_hbm), (pack_keep_ref, pack_keep_hbm), (out_ref, out_hbm), (grad_ref, grad_hbm))

    @step
    def _():
        branch = grad_ref[...].astype(BF)
        grad = nt(branch, wo_ref[...]).astype(BF).astype(F32)
        grad_t = nt(wo_ref[...], branch).astype(BF).astype(F32)
        gq_ref[...] = attend_back(
            query_ref[...], grad, grad_t, out_t_ref[...], keys_ref, values_t_ref, probs_ref, slopes_ref, gk_ref,
            gv_ref,
        ).astype(BF)
        for ref, half in halves:
            narrow = pl.ds(pl.multiple_of(half * 256, 256), 256)
            ref[y] = tn(attended_ref[:, narrow], branch).astype(BF)
            ref[1 ^ y] = tn(all_ref[:ROWS, narrow], gq_ref[...]).astype(BF)
            ref[2 ^ y] = tn(all_ref[:, narrow], gk_ref[...]).astype(BF)
            ref[3 ^ y] = tn(all_ref[:, narrow], gv_ref[...]).astype(BF)

    save((mid_send_ref, mid_send_hbm), (mid_keep_ref, mid_keep_hbm))

    @step
    def _():
        part = nt(gk_ref[512:, :], wqkv_ref[:, wk]) + nt(gv_ref[512:, :], wqkv_ref[:, wv])
        send_ref[...] = part.astype(BF).reshape(4, ROWS, D)

    save((send_ref, send_hbm))

    @step
    def _():
        part = nt(gk_ref[:512, :], wqkv_ref[:, wk]) + nt(gv_ref[:512, :], wqkv_ref[:, wv])
        keep_ref[0] = (part[:ROWS] + nt(gq_ref[...], wqkv_ref[:, wq])).astype(BF)
        keep_ref[1:] = part[ROWS:].astype(BF).reshape(3, ROWS, D)

    save((keep_ref, keep_hbm))
    for copy in saved:
        copy.wait()


def wide_kernel(own_hbm, got_hbm, out_hbm, rows_ref, out_ref, sems):
    for copy in fetch([(own_hbm, rows_ref.at[:ROWS]), (got_hbm, rows_ref.at[ROWS:])], sems):
        copy.wait()
    out_ref[:1024, :] = tn(rows_ref[:, 1024:2048], rows_ref[:, D : 2 * D]).astype(BF)
    saved = fetch([(out_ref.at[:1024], out_hbm.at[:1024])], sems, 2)
    for j in range(2):
        part = tn(rows_ref[:, :D], rows_ref[:, 2048 + D * j : 2560 + D * j])
        rows = slice(1024 + D * j, 1536 + D * j)
        out_ref[rows, :] = part.astype(BF)
        saved += fetch([(out_ref.at[rows], out_hbm.at[rows])], sems, 3 + j)
    for copy in saved:
        copy.wait()


def cross_back_kernel(
    place_ref, mod_ref, gains_ref, sums_in_ref, act_ref, g0, g1, g2, g3,
    after_hbm, wo_hbm, grad_hbm, attended_hbm, values_t_hbm, probs_hbm, keys_hbm, query_hbm, tokens_hbm, wq_hbm,
    image_hbm, wkv_hbm,
    last_keep_hbm, last_send_hbm, keep_hbm, send_hbm, tokens_out_hbm,
    last_keep_ref, last_send_ref, keep_ref, send_ref, tokens_out_ref,
    g_ref, after_ref, wo_ref, grad_ref, attended_ref, values_t_ref, probs_ref, keys_ref, query_ref, tokens_ref,
    wq_ref, image_ref, wkv_ref, sums_ref, slopes_ref, kv_ref, normed_ref, sems,
):
    early = fetch(
        [(piece, g_ref.at[j]) for j, piece in enumerate((g0, g1, g2, g3))]
        + [
            (after_hbm, after_ref), (wo_hbm, wo_ref), (grad_hbm, grad_ref), (attended_hbm, attended_ref),
            (query_hbm, query_ref),
        ],
        sems,
    )
    copies = fetch(
        [
            (values_t_hbm, values_t_ref), (probs_hbm, probs_ref), (keys_hbm, keys_ref), (tokens_hbm, tokens_ref),
            (wq_hbm, wq_ref), (image_hbm, image_ref), (wkv_hbm, wkv_ref),
        ],
        sems, 9,
    )
    saved = []

    def save(*pairs):
        saved.extend(fetch(pairs, sems, 16 + len(saved)))

    y, core = place_ref[2], place_ref[3]
    halves = ((last_send_ref, 1 - core), (last_keep_ref, core))
    for copy in early:
        copy.wait()

    mod = mod_ref[...]
    gains = gains_ref[...].astype(F32)
    incoming = add_all([g_ref[j] for j in range(4)])
    xhat, rstd, slope = norm_parts(after_ref[...], gains[1:2], mod[3:4])
    sums_ref[...] = sums_in_ref[...]
    for row, line in enumerate(norm_sums(incoming, xhat, gains[1:2], mod[3:4])):
        sums_ref[3 + row : 4 + row, :] = line
    grad_ref[...] += norm_back(incoming, xhat, rstd, slope)
    branch = grad_ref[...].astype(BF)
    for ref, half in halves:
        narrow = pl.ds(pl.multiple_of(half * 256, 256), 256)
        ref[y, :256, :] = tn(attended_ref[:, narrow], branch).astype(BF)

    for copy in copies[:3]:
        copy.wait()
    grad = nt(branch, wo_ref[...]).astype(BF).astype(F32)
    grad_t = nt(wo_ref[...], branch).astype(BF).astype(F32)
    out_t = attended_ref[...].astype(F32).T
    query = query_ref[...].astype(F32) * SCALE
    gq = attend_back(
        query, grad, grad_t, out_t, keys_ref, values_t_ref, probs_ref, slopes_ref, kv_ref.at[0], kv_ref.at[1],
    ).astype(BF)
    for copy in copies[3:]:
        copy.wait()
    tokens = tokens_ref[...].astype(F32)
    xhat, rstd, slope = norm_parts(tokens, gains[0:1], mod[1:2])
    normed_ref[...] = (xhat * slope + mod[0:1]).astype(BF)
    incoming = nt(gq, wq_ref[...])
    for row, line in enumerate(norm_sums(incoming, xhat, gains[0:1], mod[1:2])):
        sums_ref[6 + row : 7 + row, :] = line
    tokens_out_ref[...] = grad_ref[...] + norm_back(incoming, xhat, rstd, slope)
    act = act_ref[...].astype(F32)
    sums_ref[9:10, :] = act[:, :D]
    sums_ref[10:11, :] = act[:, D:]
    sums = sums_ref[...].astype(BF)
    for ref, half in halves:
        narrow = pl.ds(pl.multiple_of(half * 256, 256), 256)
        ref[1 ^ y, :256, :] = tn(normed_ref[:, narrow], gq).astype(BF)
        part = tn(image_ref[...], kv_ref[half]).astype(BF)
        for side in range(2):
            ref[(2 + side) ^ y, :192, :] = part[192 * side : 192 * side + 192, :]
            ref[(2 + side) ^ y, 192:256, :] = jnp.zeros((64, D), BF)
        for j in range(4):
            ref[j, 256:, :] = sums

    save((last_send_ref, last_send_hbm), (last_keep_ref, last_keep_hbm), (tokens_out_ref, tokens_out_hbm))

    wk, wv = wkv_ref[:, :D], wkv_ref[:, D:]
    half_keys = IMG_KEYS // 2
    for ref, base in ((keep_ref, 0), (send_ref, half_keys)):
        span = slice(base, base + half_keys)
        part = nt(kv_ref[0, span, :], wk) + nt(kv_ref[1, span, :], wv)
        ref[...] = part.astype(BF).reshape(4, IMG_PAD, 384)

    save((keep_ref, keep_hbm), (send_ref, send_hbm))
    for copy in saved:
        copy.wait()


def fold_kernel(place_ref, m0, m1, m2, m3, l0, l1, l2, l3, t0, t1, t2, t3, total_ref):
    total_ref[:, :64, :] = add_all([m0[...], m1[...], m2[...], m3[...]]).astype(BF).reshape(4, 64, D)
    late = add_all([l0[...], l1[...], l2[...], l3[...]]).astype(BF)
    total_ref[:, 64:, :] = late[:256].reshape(4, 64, D)
    for j, ref in enumerate((t0, t1, t2, t3)):
        ref[:ROWS, :] = total_ref[place_ref[0] ^ j]
        ref[ROWS:, :] = late[256:]


def join_kernel(a_ref, b_ref, c_ref, d_ref, out_ref):
    refs = (a_ref, b_ref, c_ref, d_ref)
    out_ref[:ROWS, :] = add_all([ref[:ROWS, :] for ref in refs]).astype(BF)
    for j, ref in enumerate(refs):
        out_ref[ROWS + 16 * j : ROWS + 16 * j + 16, :] = ref[ROWS:, :]


def meet_kernel(a_ref, b_ref, c_ref, d_ref, out_ref, sums_ref):
    refs = (a_ref, b_ref, c_ref, d_ref)
    out_ref[...] = add_all([ref[:ROWS, :] for ref in refs]).astype(BF)
    for j, ref in enumerate(refs):
        sums_ref[64 * j : 64 * j + 64, :] = ref[ROWS:, :]


def wide_sum_kernel(parts_ref, copies_ref):
    total = jnp.sum(parts_ref[...].astype(F32), axis=0).astype(BF)
    for j in range(4):
        copies_ref[j] = total


def wide_copies_kernel(parts_ref, copies_ref):
    total = jnp.sum(parts_ref[...].astype(F32), axis=0).astype(BF)
    for j in range(16):
        copies_ref[j] = total


def image_kernel(a_ref, b_ref, c_ref, d_ref, image_ref):
    total = add_all([a_ref[...], b_ref[...], c_ref[...], d_ref[...]])
    image_ref[...] = total[:IMG_ROWS].reshape(IMG_ROWS, 1, 384)


def modulation_kernel(sums_in_ref, gains_ref, modw_hbm, modw_ref, sems):
    sums = sums_in_ref[...].astype(F32)
    acts = (jnp.concatenate([sums[:, 9, :], sums[:, 10, :]], axis=1) * 0.125).astype(BF)
    copies = []
    for norm in range(3):
        first = 3 * (2 - norm)
        gains_ref[norm : norm + 1, :] = jnp.sum(sums[:, first, :], axis=0, keepdims=True)
        for kind in range(2):
            part = 2 * norm + kind
            modw_ref[part] = tn(acts, sums[:, first + 1 + kind, :].astype(BF))
            target = modw_hbm.at[:, D * part : D * part + D]
            copies += fetch([(modw_ref.at[part], target)], sems, len(copies))
    for copy in copies:
        copy.wait()


def out_kernel(side, place_ref, wide_hbm, p0, p1, p2, p3, *refs):
    targets, refs = (refs[:7], refs[7:]) if side == 0 else (refs[7:14], refs[14:])
    w_in_ref, w_out_ref, wo_self_ref, wqkv_ref, wo_ref, wq_ref, wkv_ref, wide_ref, late_ref, sems = refs
    w_in_hbm, w_out_hbm, wo_self_hbm, wqkv_hbm, wo_hbm, wq_hbm, wkv_hbm = targets
    x, y, core = place_ref[0], place_ref[2], place_ref[3]
    step = pl.when(core >= 0)
    half = core ^ side
    wide_in = fetch([(wide_hbm.at[8 * j : 8 * j + 8], wide_ref.at[8 * j : 8 * j + 8]) for j in range(2)], sems)
    late_in = fetch([(piece, late_ref.at[j]) for j, piece in enumerate((p0, p1, p2, p3))], sems, 2)
    saved = []

    def save(*pairs):
        saved.extend(fetch(pairs, sems, 6 + len(saved)))

    wide_rows = pl.ds(pl.multiple_of(half * 1024, 1024), 1024)
    rows = pl.ds(pl.multiple_of(half * 256, 256), 256)
    columns = pl.ds(pl.multiple_of(half * D, D), D)
    wide_in[0].wait()

    @step
    def _():
        w_out_ref[...] = wide_ref[:8].reshape(1024, D).astype(F32)

    save((w_out_ref, w_out_hbm.at[wide_rows]))
    wide_in[1].wait()

    @step
    def _():
        for j in range(2):
            w_in_ref[:, D * j : D * j + D] = wide_ref[8 + 4 * j : 12 + 4 * j].reshape(D, D).astype(F32)

    save((w_in_ref, w_in_hbm.at[:, wide_rows]))
    for copy in late_in:
        copy.wait()

    @step
    def _():
        for piece in range(4):
            block = y ^ piece
            for across in range(4):
                strip = x ^ across
                strip_rows = pl.ds(pl.multiple_of(strip * 64, 64), 64)
                early = late_ref[piece, across, :64, :].astype(F32)
                late = late_ref[piece, across, 64:, :].astype(F32)

                @pl.when(block == 0)
                def _():
                    wo_self_ref[strip_rows, :] = early
                    wo_ref[strip_rows, :] = late

                @pl.when(block > 0)
                def _():
                    wqkv_ref[strip_rows, pl.ds(pl.multiple_of((block - 1) * D, D), D)] = early

                @pl.when(block == 1)
                def _():
                    wq_ref[strip_rows, :] = late

                @pl.when((block > 1) & (strip < 3))
                def _():
                    start = pl.multiple_of((block - 2) * 192 + strip * 64, 64)
                    wkv_ref[pl.ds(start, 64), :] = late

    save(
        (wo_self_ref, wo_self_hbm.at[rows]), (wqkv_ref, wqkv_hbm.at[rows]), (wo_ref, wo_hbm.at[rows]),
        (wq_ref, wq_hbm.at[rows]), (wkv_ref, wkv_hbm.at[:, columns]),
    )
    for copy in saved:
        copy.wait()


def tie(*values):
    return lax.optimization_barrier(values)


def swap_core(value):
    return lax.ppermute(value, "core", CORE_SWAP)


def swap(value, axis, step):
    return lax.ppermute(value, axis, [(i, i ^ step) for i in range(4)])


def swap_y(value, step):
    return swap(value, "y", step)


def gather_eight(value):
    across = [value] + [swap_y(value, step) for step in (1, 2, 3)]
    return across + [swap_core(item) for item in across]


def scatter_eight(keep, send):
    return others(halve(keep, send), "y")


def add_all(items):
    total = items[0].astype(F32)
    for item in items[1:]:
        total = total + item.astype(F32)
    return total


def halve(keep, send):
    got = swap_core(send)
    return [(keep[j].astype(F32) + got[j].astype(F32)).astype(BF) for j in range(4)]


def spread(mixed):
    rows, width = mixed.shape
    return lax.all_to_all(mixed, ("x", "z"), 0, 0, tiled=True).reshape(16, rows // 16, width)


def collect(copies):
    return lax.all_to_all(copies, ("x", "z"), 0, 0, tiled=True)


def others(pieces, axis):
    return [pieces[0]] + [swap(pieces[step], axis, step) for step in (1, 2, 3)]


def gather_axis(value, axis):
    return jnp.stack(others([value] * 4, axis))


def local(
    tokens, camera, image, image_mask, point_rows, point_count, point_grads, mod_weight, norm_gains,
    wq_cross, wkv_cross, wo_cross, wqkv_self, wo_self, w_in, w_out,
):
    place = [lax.axis_index(axis).astype(jnp.int32) for axis in ("x", "z", "y", "core")]
    y, core = place[2:]
    owners = [2 * (y ^ (j % 4)) + (core ^ (j // 4)) for j in range(8)]
    place = jnp.stack(place + owners).astype(jnp.int32)
    toks = tokens[0]

    image_blocks = gather_eight(image[0])

    mask = (image_mask[0] > 0).astype(BF).reshape(2, 2, 2, IMG_ROWS)
    for axis, bit in ((0, y & 2), (1, y & 1), (2, core)):
        mask = jnp.where(bit != 0, jnp.flip(mask, axis), mask)
    mask = jnp.pad(mask.transpose(2, 0, 1, 3), ((0, 0),) * 3 + ((0, IMG_PAD - IMG_ROWS),)).reshape(1, IMG_KEYS)

    cot_keep, cot_send, mod, act = kernel_call(
        points_kernel,
        [((4, ROWS, D), BF), ((4, ROWS, D), BF), ((8, D), F32), ((1, 1024), BF)],
        [((1024, 6 * D), BF)], 6 * 10**9,
        place, point_count[0], point_rows, point_grads[0], camera, mod_weight, smem=2, hbm=1, copies=1,
    )
    cot_parts = scatter_eight(cot_keep, cot_send)

    after_cross, normed_two, attended_one, query_one = kernel_call(
        cross_kernel,
        [((ROWS, D), F32), ((ROWS, D), BF), ((ROWS, D), BF), ((ROWS, D), BF)],
        [
            ((IMG_KEYS, 384), BF), ((IMG_KEYS, D), BF), ((D, IMG_KEYS), BF), ((IMG_KEYS, 512), F32),
            ((2, IMG_KEYS, 512), BF), ((D, D), BF), ((384, 2 * D), BF), ((D, D), BF), ((IMG_KEYS, 128), F32),
        ],
        10 * 10**9,
        toks, mod, norm_gains, mask, *image_blocks, wq_cross, wkv_cross, wo_cross, hbm=3, copies=3, limit=60,
    )

    normed_two, *cot_parts = tie(normed_two, *cot_parts)
    across = others([normed_two] * 4, "y")
    keys_one, values_t_one, image_all, probs_one = kernel_call(
        cross_rest_kernel,
        [((IMG_KEYS, D), BF), ((D, IMG_KEYS), BF), ((IMG_KEYS, 384), BF), ((2, IMG_KEYS, 512), BF)],
        [
            ((384, 2 * D), BF), ((IMG_KEYS, D), BF), ((D, IMG_KEYS), BF), ((IMG_KEYS, 384), BF),
            ((2, IMG_KEYS, 512), BF), ((IMG_KEYS, 512), F32), ((IMG_KEYS, 128), F32),
        ],
        7 * 10**9, tie(query_one, normed_two)[0], mask, *image_blocks, wkv_cross, hbm=1, hbm_outs=4, copies=6,
    )
    keys_one, values_t_one, image_all, probs_one, *across = tie(keys_one, values_t_one, image_all, probs_one, *across)
    normed_blocks = across + [swap_core(item) for item in across]
    (
        sums, layer_out, grad_after_self, back_keep, back_send, mid_keep, mid_send, pack_keep, pack_send,
    ) = kernel_call(
        middle_kernel,
        [((16, D), F32)] + MIDDLE_OUTS,
        MIDDLE_OUTS
        + [
            ((ROWS, D), F32), ((D, 3 * D), BF), ((D, D), BF), ((D, 2048), BF), ((2048, D), BF), ((4, ROWS, D), BF),
            ((KEYS, D), BF), ((KEYS, D), BF), ((D, KEYS), BF),
            ((2, KEYS, 512), BF), ((KEYS, 512), F32), ((KEYS, 512), BF), ((KEYS, D), BF), ((KEYS, D), BF),
            ((ROWS, 2048), BF), ((ROWS, 2048), BF), ((ROWS, D), BF), ((ROWS, D), F32), ((D, ROWS), F32),
            ((ROWS, D), BF),
        ],
        20 * 10**9,
        place, mod, norm_gains, *normed_blocks, *cot_parts, after_cross, wqkv_self, wo_self, w_in, w_out,
        smem=1, hbm=17, hbm_outs=8, copies=25, limit=50,
    )

    back_parts = halve(back_keep, back_send)
    pack_send, mid_send, *back_parts = tie(pack_send, mid_send, *back_parts)
    pack_got = swap_core(pack_send)
    mid_got = swap_core(mid_send)
    back_parts = others(back_parts, "y")
    (wide_mixed,) = kernel_call(
        wide_kernel, [((2048, D), BF)], [((256, 3072), BF), ((2048, D), BF)], 3 * 10**9, pack_keep, pack_got,
        hbm=2, hbm_outs=1, copies=5, limit=20,
    )
    mid_pieces = [(mid_keep[j].astype(F32) + mid_got[j].astype(F32)).astype(BF) for j in range(4)]
    wide_mixed, *pieces = tie(wide_mixed, *back_parts, *mid_pieces)
    back_parts, mid_pieces = pieces[:4], pieces[4:]
    wide_parts = spread(wide_mixed)
    mid_pieces = others(mid_pieces, "y")

    last_keep, last_send, img_keep, img_send, grad_tokens = kernel_call(
        cross_back_kernel,
        CROSS_OUTS,
        CROSS_OUTS
        + [
            ((4, ROWS, D), BF), ((ROWS, D), F32), ((D, D), BF), ((ROWS, D), F32), ((ROWS, D), BF), ((D, IMG_KEYS), BF),
            ((2, IMG_KEYS, 512), BF), ((IMG_KEYS, D), BF), ((ROWS, D), BF), ((ROWS, D), BF), ((D, D), BF),
            ((IMG_KEYS, 384), BF), ((384, 2 * D), BF), ((16, D), F32), ((IMG_KEYS, 512), BF), ((2, IMG_KEYS, D), BF),
            ((ROWS, D), BF),
        ],
        11 * 10**9,
        place, mod, norm_gains, sums, act, *back_parts, after_cross, wo_cross, grad_after_self, attended_one,
        values_t_one, probs_one, keys_one, query_one, toks, wq_cross, image_all, wkv_cross,
        smem=1, hbm=16, hbm_outs=5, copies=22, limit=54,
    )
    last_send, img_send, *mid_pieces = tie(last_send, img_send, *mid_pieces)
    last_pieces = others(halve(last_keep, last_send), "y")
    img_mixed = halve(img_keep, img_send)
    (wide,) = kernel_call(wide_sum_kernel, [((4, ROWS, D), BF)], [], 2 * 10**9, wide_parts, limit=16)
    *last_pieces, wide, img_mixed = tie(*last_pieces, wide, img_mixed)
    late_pieces = kernel_call(
        fold_kernel, [((144, D), BF)] * 4, [((4, ROWS, D), BF)], 2 * 10**9, place, *mid_pieces, *last_pieces, smem=1, limit=16,
    )
    late_pieces = others(late_pieces, "x")
    late_pieces[1], wide = tie(late_pieces[1], wide)
    wide = lax.all_to_all(wide, "y", 0, 0, tiled=True)
    (late,) = kernel_call(join_kernel, [((192, D), BF)], [], 10**9, *late_pieces, limit=16)
    late, *img_mixed = tie(late, *img_mixed)
    late_pieces = others([late] * 4, "z")
    img_pieces = [img_mixed[0], swap_y(img_mixed[1], 1), swap_y(img_mixed[2], 2)]
    *late_pieces, wide = tie(*late_pieces, wide)
    late, all_sums = kernel_call(meet_kernel, [((ROWS, D), BF), ((256, D), BF)], [], 10**9, *late_pieces, limit=16)
    late, img_mixed[3] = tie(late, img_mixed[3])
    img_pieces.append(swap_y(img_mixed[3], 3))
    late_pieces = others([late] * 4, "x")
    (wide,) = kernel_call(wide_copies_kernel, [((16, ROWS, D), BF)], [], 2 * 10**9, wide)
    *late_pieces, wide, img_pieces[1], img_pieces[2] = tie(*late_pieces, wide, img_pieces[1], img_pieces[2])
    late = jnp.stack(late_pieces)
    wide = collect(wide)
    late_own = others([late] * 4, "y")
    g_gains, g_mod = kernel_call(
        modulation_kernel, [((3, D), F32), ((1024, 6 * D), F32)], [((6, 1024, D), F32)],
        7 * 10**9, tie(all_sums, late)[0].reshape(16, 16, D), hbm_outs=1, copies=6,
    )
    (grad_image,) = kernel_call(image_kernel, [((IMG_ROWS, 1, 384), F32)], [], 10**9, *img_pieces)
    late_other = [swap_core(late_own[0])]
    late_own, late_other, g_gains, g_mod, grad_image, wide = tie(
        late_own, late_other, g_gains, g_mod, grad_image, wide
    )
    late_other = late_other + [swap_core(item) for item in late_own[1:]]
    halves = [
        ((D, 1024), F32), ((1024, D), F32), ((256, D), F32), ((256, 3 * D), F32), ((256, D), F32), ((256, D), F32),
        ((384, D), F32), ((16, ROWS, D), BF), ((4, 4, ROWS, D), BF),
    ]
    wide_other = swap_core(wide)
    grads = kernel_call(
        functools.partial(out_kernel, 0), GRAD_OUTS, halves, 4 * 10**9, place, wide, *late_own,
        smem=1, hbm=5, hbm_outs=7, copies=13, limit=40,
    )
    g_in, g_out, g_wo_self, g_wqkv, g_wo_cross, g_wq, g_wkv = kernel_call(
        functools.partial(out_kernel, 1), GRAD_OUTS, halves, 4 * 10**9, place, wide_other, *late_other, *grads,
        smem=1, hbm=12, hbm_outs=7, copies=13, limit=40, aliases={6 + j: j for j in range(7)},
    )
    return (
        layer_out[None], grad_tokens[None], grad_image.reshape(1, IMG_ROWS, 384), g_mod, g_gains, g_wq, g_wkv, g_wo_cross, g_wqkv,
        g_wo_self, g_in, g_out,
    )


def solution(mesh):
    split = Mesh(mesh.devices.reshape(4, 4, 4, 2), ("x", "z", "y", "core"))
    obj, tok = ("x", "z"), ("y", "core")
    return jax.shard_map(
        local,
        mesh=split,
        in_specs=(
            P(obj, tok, None), P(obj, None), P(obj, tok, None), P(obj, None), P(obj, tok), P(obj, tok),
            P(obj, tok, None),
        )
        + (P(),) * 9,
        out_specs=(P(obj, tok, None),) * 3 + (P(),) * 9,
        check_vma=False,
    )
```
